512 devices in a mesh: dp: 8 (over y_hi, x), cls: 64 (over z, y_lo, core).
Axes of the slice: x: 4, y: 4 (y_hi: 2, y_lo: 2; y = y_hi * 2 + y_lo), z: 16, core: 2. Of those that a mesh axis runs over, the one named last changes fastest.
Arguments:
- embeddings: bfloat16 [8192, 512], P(('dp', 'cls')), may hold values from -60 to 60
- labels: int32 [8192], P('dp'), may hold values from 0 to 131071, as said below
- row_weight: float32 [8192], P('dp'), may hold values from 0.5 to 5
- prototypes: bfloat16 [131072, 512], P('cls'), may hold values from -18 to 18
Outputs:
- emb_grad: bfloat16 [8192, 512], P(('dp', 'cls'))
- proto_grad: bfloat16 [131072, 512], P('cls')
The draws below stay inside these ranges and needn't reach their ends.
Inputs may be any that keep to these rules, and one draw needn't show every extreme that they name: `labels`: a class label of the bank for each row.
All inputs are finite; a program needn't handle non-finite values.
Results may differ from the reference program's by a relative error of at most 0.015.
Values may be sent and summed in bfloat16 or wider, within the bound.
A program may use at most 64 MiB of HBM per device.

```python
import math
import jax
import jax.numpy as jnp
from jax import lax

D = 512
C_DEV = 2048
B_DEV = 16
CLASSES = 131072
BATCH = 8192
N_DP = 8
N_CLS = 64


def shared_parts(key):
    label_draw = jax.random.randint(jax.random.fold_in(key, 11), (N_DP * N_CLS * B_DEV,), 0, C_DEV * N_CLS)
    scale_draw = jax.random.uniform(jax.random.fold_in(key, 12), (C_DEV * N_CLS, 1), jnp.float32, jnp.log(0.3), jnp.log(3.0))
    base_draw = jax.random.truncated_normal(jax.random.fold_in(key, 13), -3.0, 3.0, (C_DEV * N_CLS, D), jnp.float32)
    return (label_draw.astype(jnp.int32), jnp.exp(scale_draw), base_draw)


def draw_labels(key, part):
    label_draw, scale_draw, base_draw = shared_parts(key)
    return label_draw


def draw_prototypes(key, part):
    label_draw, scale_draw, base_draw = shared_parts(key)
    values = base_draw * scale_draw
    return values.astype(jnp.bfloat16)


def draw_embeddings(key, part):
    label_draw, scale_draw, base_draw = shared_parts(key)
    key = jax.random.fold_in(key, 31)
    rows = N_DP * N_CLS * B_DEV
    aligned = base_draw[label_draw]
    share = jax.random.uniform(jax.random.fold_in(key, 1), (rows, 1), jnp.float32, 0.0, 1.0)
    noise = jax.random.truncated_normal(jax.random.fold_in(key, 2), -3.0, 3.0, (rows, D), jnp.float32)
    lengths = jnp.exp(jax.random.uniform(jax.random.fold_in(key, 3), (rows, 1), jnp.float32, jnp.log(0.5), jnp.log(5.0)))
    values = lengths * (share * aligned + jnp.sqrt(1.0 - share * share) * noise)
    return values.astype(jnp.bfloat16)


def levels(key, shape, cuts, smallest, largest):
    def one(axis_at, shards_of):
        steps = jax.random.uniform(jax.random.fold_in(jax.random.fold_in(key, 6), axis_at), (shards_of,), jnp.float32, smallest / len(cuts), largest / len(cuts))
        return jnp.repeat(jnp.exp(steps), shape[axis_at] // shards_of).reshape((-1,) + (1,) * (len(shape) - axis_at - 1))

    level = one(*cuts[0])
    for cut in cuts[1:]:
        level = level * one(*cut)
    return level


def setup_inputs(seed: int = 0) -> dict:
    splits = jax.random.split(jax.random.key(seed), 5)
    return {
        "embeddings": draw_embeddings(jax.random.fold_in(splits[4], 71), 0),
        "labels": draw_labels(jax.random.fold_in(splits[4], 71), 0),
        "row_weight": jnp.clip(jnp.exp(math.log(5.0) - 2.3025851 * jax.random.uniform(splits[2], (BATCH,), jnp.float32) ** levels(splits[2], (BATCH,), ((0, 8),), -0.2, 0.2)), 0.5, 5.0),
        "prototypes": draw_prototypes(jax.random.fold_in(splits[4], 71), 0),
    }


scale_factor = 64.0
margin = 0.5
sine_floor = 0.04
norm_eps = 1e-06

def unit_rows(values):
    wide = values.astype(jnp.float32)
    inverse = lax.rsqrt(lax.optimization_barrier(jnp.sum(wide * wide, axis=1, keepdims=True)) + norm_eps)
    return (inverse, wide * inverse)

def reference(embeddings, labels, row_weight, prototypes):
    emb_inv, emb_unit = unit_rows(embeddings)
    proto_inv, proto_unit = unit_rows(prototypes)
    unit_emb = emb_unit.astype(jnp.bfloat16)
    unit_proto = proto_unit.astype(jnp.bfloat16)
    group_rows = B_DEV * N_CLS
    emb_blocks = unit_emb.reshape(N_DP, group_rows, D)
    label_blocks = labels.reshape(N_DP, group_rows)
    weight_blocks = row_weight.reshape(N_DP, group_rows)
    class_ids = lax.broadcasted_iota(jnp.int32, (group_rows, CLASSES), 1)

    def group_step(carry, pieces):
        rows_bf, block_labels, block_weights = pieces
        cosine = jnp.dot(rows_bf, unit_proto.T, preferred_element_type=jnp.float32)
        is_target = class_ids == block_labels[:, None]
        target_cos = lax.optimization_barrier(jnp.sum(jnp.where(is_target, cosine, 0.0), axis=1))
        sine = jnp.sqrt(jnp.maximum(1.0 - target_cos * target_cos, sine_floor))
        target_logit = scale_factor * (target_cos * math.cos(margin) - sine * math.sin(margin))
        logits = jnp.where(is_target, target_logit[:, None], scale_factor * cosine)
        exponent = jnp.exp(logits)
        totals = lax.optimization_barrier(jnp.sum(exponent, axis=1))
        probability = exponent / totals[:, None]
        logit_grad = block_weights[:, None] * (probability - is_target.astype(jnp.float32))
        bound_free = 1.0 - target_cos * target_cos > sine_floor
        target_slope = scale_factor * (math.cos(margin) + jnp.where(bound_free, math.sin(margin) * target_cos / sine, 0.0))
        slope_factor = jnp.where(is_target, target_slope[:, None], scale_factor)
        grad_cos = (logit_grad * slope_factor).astype(jnp.bfloat16)
        emb_dir = jnp.dot(grad_cos, unit_proto, preferred_element_type=jnp.float32)
        group_proto = jnp.dot(grad_cos.T, rows_bf, preferred_element_type=jnp.float32)
        carry = carry + group_proto.astype(jnp.bfloat16).astype(jnp.float32)
        return (carry, emb_dir)
    start_sum = jnp.zeros((CLASSES, D), jnp.float32)
    proto_dir, emb_dirs = lax.scan(group_step, start_sum, (emb_blocks, label_blocks, weight_blocks))
    emb_dir = emb_dirs.reshape(N_DP * group_rows, D)
    emb_grad = emb_inv * (emb_dir - emb_unit * lax.optimization_barrier(jnp.sum(emb_unit * emb_dir, axis=1, keepdims=True)))
    proto_grad = proto_inv * (proto_dir - proto_unit * lax.optimization_barrier(jnp.sum(proto_unit * proto_dir, axis=1, keepdims=True)))
    return (emb_grad.astype(jnp.bfloat16), proto_grad.astype(jnp.bfloat16))
```

```python
import math

import jax
import jax.numpy as jnp
from jax import lax
from jax.experimental import pallas as pl
from jax.experimental.pallas import tpu as pltpu
from jax.sharding import PartitionSpec as P

scale_factor = 64.0
margin = 0.5
sine_floor = 0.04
norm_eps = 1e-06
log2e = 1.4426950408889634
MESH = pl.DeviceIdType.MESH
F32 = jnp.float32
BF = jnp.bfloat16

D = 512
C = 2048
R = 1024
Q = 256
CH = 256


def unit_rows(values):
    wide = values.astype(F32)
    inverse = lax.rsqrt(jnp.sum(wide * wide, axis=1, keepdims=True) + norm_eps)
    return (inverse, wide * inverse)


def finish_rows(direction, unit_part, inverse):
    return (
        inverse * (direction - unit_part * jnp.sum(unit_part * direction, axis=1, keepdims=True))
    ).astype(BF)


def kernel(
    emb_ref, lab_ref, wgt_ref, proto_hbm,
    emb_out, out,
    proto, unit, u, e, g, part,
    tot, tot_loc, tot_z,
    ra, rb, ra2, rb2, sa, sb, ta, tb,
    ed, r1, f1, r2, f2, r3, f3, r4,
    proto_sem,
    ag_s, ag_r, tl_s, tl_r, tz_s, tz_r, rs_s, rs_r, em_s, em_r,
):
    dp = lax.axis_index("dp")
    cls = lax.axis_index("cls")
    yh, x = dp // 4, dp % 4
    z, y, c = cls // 4, (cls // 2) % 2, cls % 2
    zh, zl = z // 4, z % 4

    def at_z(k):
        return (dp, ((z + k) % 16) * 4 + y * 2 + c)

    def at_local(dy, dc):
        yy = (y + dy) % 2
        cc = (c + dc) % 2
        return (dp, z * 4 + yy * 2 + cc)

    def at_x(k):
        return (yh * 4 + (x + k) % 4, cls)

    y_peer = ((1 - yh) * 4 + x, cls)
    core_peer = at_local(0, 1)
    ylo_peer = at_local(1, 0)

    def send(src, dst, ssem, rsem, where):
        cp = pltpu.make_async_remote_copy(
            src_ref=src, dst_ref=dst, send_sem=ssem, recv_sem=rsem,
            device_id=where, device_id_type=MESH,
        )
        cp.start()
        return cp

    barrier = pltpu.get_barrier_semaphore()
    friends = [at_z(k) for k in range(1, 16)]
    friends += [core_peer, ylo_peer, at_local(1, 1)]
    friends += [at_x(1), at_x(2), at_x(3), y_peer]
    for friend in friends:
        pl.semaphore_signal(barrier, inc=1, device_id=friend, device_id_type=MESH)
    load = pltpu.make_async_copy(proto_hbm, proto, proto_sem)
    load.start()
    emb_inv, emb_unit = unit_rows(emb_ref[...])
    u[c, y, zl, pl.ds(pl.multiple_of(zh * 16, 16), 16), :] = emb_unit.astype(BF)
    pl.semaphore_wait(barrier, len(friends))

    sends = []
    own_block = u.at[c, y, zl, pl.ds(pl.multiple_of(zh * 16, 16), 16)]
    p1 = [send(own_block, own_block, ag_s.at[i], ag_r.at[i], at_z(k)) for i, k in enumerate((8, 4, 12))]

    load.wait()

    def normalize(i, carry):
        rows = pl.ds(pl.multiple_of(i * CH, CH), CH)
        unit[rows, :] = unit_rows(proto[rows, :])[1].astype(BF)
        return carry

    lax.fori_loop(0, C // CH, normalize, 0)

    for cp in p1:
        cp.wait()
    own_set = u.at[c, y, zl]
    p2 = [send(own_set, own_set, ag_s.at[3 + i], ag_r.at[3 + i], at_z(k)) for i, k in enumerate((2, 1, 15))]
    toy = [send(own_set, own_set, ag_s.at[6], ag_r.at[6], ylo_peer)]
    toc = [send(own_set, own_set, ag_s.at[10], ag_r.at[10], core_peer)]
    for i, k in enumerate((2, 1, 15)):
        p2[i].wait()
        got = u.at[c, y, (zl + 16 - k) % 4]
        toy.append(send(got, got, ag_s.at[7 + i], ag_r.at[7 + i], ylo_peer))
        toc.append(send(got, got, ag_s.at[11 + i], ag_r.at[11 + i], core_peer))

    class_iota = lax.broadcasted_iota(jnp.int32, (CH, Q), 0)
    first_class = cls * C

    def first_pass(cc, yy):
        q = cc * 2 + yy
        lanes = pl.ds(pl.multiple_of(q * Q, Q), Q)
        labels = lab_ref[:, lanes] - first_class
        rows_u = u[cc, yy].reshape(Q, D)

        def step(i, carry):
            total, target = carry
            base = pl.multiple_of(i * CH, CH)
            cosine = lax.dot_general(
                unit[pl.ds(base, CH), :], rows_u, (((1,), (1,)), ((), ())),
                preferred_element_type=F32,
            )
            is_target = class_iota == labels - base
            ex = jnp.where(is_target, 0.0, jnp.exp2(cosine * (scale_factor * log2e)))
            tc = jnp.where(is_target, cosine, 0.0)
            e[q, pl.ds(base, CH), :] = ex
            total = total + jnp.sum(ex.reshape(CH // 8, 8, Q), axis=0)
            target = target + jnp.sum(tc.reshape(CH // 8, 8, Q), axis=0)
            return (total, target)

        zero = jnp.zeros((8, Q), F32)
        total, target = lax.fori_loop(0, C // CH, step, (zero, zero))
        total = jnp.sum(total, axis=0, keepdims=True)
        target_cos = jnp.sum(target, axis=0, keepdims=True)
        here = (labels >= 0) & (labels < C)
        sine = jnp.sqrt(jnp.maximum(1.0 - target_cos * target_cos, sine_floor))
        target_logit = scale_factor * (target_cos * math.cos(margin) - sine * math.sin(margin))
        target_exp = jnp.exp(target_logit)
        tot[0, :, lanes] = total + jnp.where(here, target_exp, 0.0)
        bound_free = 1.0 - target_cos * target_cos > sine_floor
        slope = scale_factor * (
            math.cos(margin) + jnp.where(bound_free, math.sin(margin) * target_cos / sine, 0.0)
        )
        tot[1, :, lanes] = target_exp
        tot[2, :, lanes] = slope

    first_pass(c, y)
    tod = []
    for i, k in enumerate((0, 2, 1, 15)):
        toy[i].wait()
        got = u.at[c, 1 - y, (zl + 16 - k) % 4]
        tod.append(send(got, got, ag_s.at[14 + i], ag_r.at[14 + i], core_peer))
    first_pass(c, 1 - y)
    for cp in toc:
        cp.wait()
    first_pass(1 - c, y)
    for cp in tod:
        cp.wait()
    first_pass(1 - c, 1 - y)

    loc = []
    for i, (dy, dc) in enumerate(((1, 0), (0, 1), (1, 1))):
        loc.append(send(tot.at[0], tot_loc.at[i], tl_s.at[i], tl_r.at[i], at_local(dy, dc)))
    for cp in loc:
        cp.wait()
    slab = tot[0] + tot_loc[0] + tot_loc[1] + tot_loc[2]
    tot[3] = slab
    along = []
    order = (8, 7, 9, 6, 10, 5, 11, 4, 12, 3, 13, 2, 14, 1, 15)
    for k in order:
        along.append(send(tot.at[3], tot_z.at[k - 1], tz_s.at[k - 1], tz_r.at[k - 1], at_z(k)))
    for cp in along:
        cp.wait()
    totals = slab
    for k in range(15):
        totals = totals + tot_z[k]

    weight = wgt_ref[...]
    row_scale = scale_factor * weight / totals
    label_grad = weight * (tot[1] / totals - 1.0) * tot[2]
    tot[4] = row_scale
    tot[5] = label_grad

    def second_pass(base):
        base = pl.multiple_of(base, CH)
        rows = pl.ds(base, CH)
        for q in range(4):
            lanes = slice(q * Q, (q + 1) * Q)
            is_target = class_iota == lab_ref[:, lanes] - (first_class + base)
            grad = jnp.where(is_target, tot[5, :, lanes], e[q, rows, :] * tot[4, :, lanes])
            g[rows, lanes] = grad.astype(BF)
        part[rows, :] = jnp.dot(
            g[rows, :], u[...].reshape(R, D), preferred_element_type=F32
        ).astype(BF)

    H = C // 2
    other = H + (1 - yh) * 512
    mine = H + yh * 512

    def rows_of(ref, start, n):
        return ref.at[pl.ds(pl.multiple_of(start, 128), n)]

    rs = []
    plan = (("x", 2), ("y", 0), ("x", 1), ("y", 1), ("x", 3))
    for kind, k in plan:
        if kind == "x":
            base = ((x + k) % 4) * 256
            second_pass(base)
            rs.append(send(rows_of(part, base, 256), ra.at[k - 1], rs_s.at[k - 1], rs_r.at[k - 1], at_x(k)))
        else:
            base = other + k * 256
            second_pass(base)
            rs.append(send(rows_of(part, base, 256), rb.at[k], rs_s.at[3 + k], rs_r.at[3 + k], y_peer))
    second_pass(x * 256)
    second_pass(mine)
    second_pass(mine + 256)

    def emb_product(cc, yy):
        q = cc * 2 + yy
        lanes = pl.ds(pl.multiple_of(q * Q, Q), Q)
        ed[cc, yy] = lax.dot_general(
            g[:, lanes], unit[...], (((0,), (0,)), ((), ())), preferred_element_type=F32
        ).astype(BF)

    emb_product(1 - c, 0)
    emb_product(1 - c, 1)
    em1 = send(ed.at[1 - c], r1, em_s.at[0], em_r.at[0], core_peer)
    emb_product(c, 0)
    emb_product(c, 1)
    em1.wait()
    f1[...] = (ed[c].astype(F32) + r1[...].astype(F32)).astype(BF).reshape(2, 4, 64, D)
    em2 = []
    for i, k in enumerate((2, 1, 15)):
        for yy in range(2):
            at = 1 + i * 2 + yy
            em2.append(send(f1.at[yy, (zl + k) % 4], r2.at[i, yy], em_s.at[at], em_r.at[at], at_z(k)))

    for cp in rs:
        cp.wait()
    n = 128
    own_a = part[pl.ds(pl.multiple_of(x * 256, 256), 256), :].astype(F32)
    sum_a = own_a + ra[0].astype(F32) + ra[1].astype(F32) + ra[2].astype(F32)
    sa[...] = sum_a.astype(BF).reshape(2, n, D)
    rs2 = [send(sa.at[1 - yh], ra2, rs_s.at[5], rs_r.at[5], y_peer)]
    own_b = part[pl.ds(pl.multiple_of(mine, 256), 512), :].astype(F32)
    sum_b = own_b + rb[...].reshape(512, D).astype(F32)
    sb[...] = sum_b.astype(BF).reshape(4, n, D)
    for k in (2, 1, 3):
        rs2.append(send(sb.at[(x + k) % 4], rb2.at[k - 1], rs_s.at[5 + k], rs_r.at[5 + k], at_x(k)))

    for cp in em2:
        cp.wait()
    f2[...] = (
        f1[:, zl].astype(F32) + r2[0].astype(F32) + r2[1].astype(F32) + r2[2].astype(F32)
    ).astype(BF)
    em3 = []
    for i, k in enumerate((8, 4, 12)):
        to = pl.ds(pl.multiple_of(((zh + k // 4) % 4) * 16, 16), 16)
        for yy in range(2):
            at = 7 + i * 2 + yy
            em3.append(send(f2.at[yy, to], r3.at[i, yy], em_s.at[at], em_r.at[at], at_z(k)))

    for cp in rs2:
        cp.wait()
    at_a = pl.multiple_of(x * 256 + yh * n, n)
    at_b = pl.multiple_of(mine + x * n, n)
    inv_a, unit_a = unit_rows(proto[pl.ds(at_a, n), :])
    dir_a = sa[yh].astype(F32) + ra2[...].astype(F32)
    out[pl.ds(at_a, n), :] = finish_rows(dir_a, unit_a, inv_a)
    ag2 = []
    mine_a = out.at[pl.ds(at_a, n)]
    ag_y = send(mine_a, mine_a, rs_s.at[9], rs_r.at[9], y_peer)
    inv_b, unit_b = unit_rows(proto[pl.ds(at_b, n), :])
    dir_b = sb[x].astype(F32) + rb2[0].astype(F32) + rb2[1].astype(F32) + rb2[2].astype(F32)
    out[pl.ds(at_b, n), :] = finish_rows(dir_b, unit_b, inv_b)
    mine_b = out.at[pl.ds(at_b, n)]
    ag_x = []
    for k in (2, 1, 3):
        ag_x.append(send(mine_b, mine_b, rs_s.at[9 + k], rs_r.at[9 + k], at_x(k)))
    ag2.append(send(mine_b, mine_b, rs_s.at[13], rs_r.at[13], y_peer))
    for k in (2, 1, 3):
        ag2.append(send(mine_a, mine_a, rs_s.at[13 + k], rs_r.at[13 + k], at_x(k)))

    for cp in em3:
        cp.wait()
    own3 = pl.ds(pl.multiple_of(zh * 16, 16), 16)
    f3[...] = (
        f2[:, own3].astype(F32) + r3[0].astype(F32) + r3[1].astype(F32) + r3[2].astype(F32)
    ).astype(BF)
    em4 = send(f3.at[1 - y], r4, em_s.at[13], em_r.at[13], ylo_peer)

    ag_y.wait()
    got = out.at[pl.ds(pl.multiple_of(x * 256 + (1 - yh) * n, n), n)]
    for k in (2, 1, 3):
        ag2.append(send(got, got, rs_s.at[16 + k], rs_r.at[16 + k], at_x(k)))
    for i, k in enumerate((2, 1, 3)):
        ag_x[i].wait()
        got = out.at[pl.ds(pl.multiple_of(mine + ((x + 4 - k) % 4) * n, n), n)]
        ag2.append(send(got, got, rs_s.at[20 + i], rs_r.at[20 + i], y_peer))

    em4.wait()
    emb_dir = f3[y].astype(F32) + r4[...].astype(F32)
    emb_inv, emb_unit = unit_rows(emb_ref[...])
    emb_out[...] = finish_rows(emb_dir, emb_unit, emb_inv)

    for cp in ag2:
        cp.wait()


def on_device(embeddings, labels, row_weight, prototypes):
    def order(values):
        return values.reshape(4, 4, 2, 2, 16).transpose(3, 2, 1, 0, 4).reshape(1, R)

    vmem = pl.BlockSpec(memory_space=pltpu.VMEM)
    dma = pltpu.SemaphoreType.DMA
    return pl.pallas_call(
        kernel,
        out_shape=(
            jax.ShapeDtypeStruct((16, D), BF),
            jax.ShapeDtypeStruct((C, D), BF),
        ),
        in_specs=[vmem, vmem, vmem, pl.BlockSpec(memory_space=pl.ANY)],
        out_specs=(vmem, vmem),
        scratch_shapes=[
            pltpu.VMEM((C, D), BF),
            pltpu.VMEM((C, D), BF),
            pltpu.VMEM((2, 2, 4, 64, D), BF),
            pltpu.VMEM((4, C, Q), F32),
            pltpu.VMEM((C, R), BF),
            pltpu.VMEM((C, D), BF),
            pltpu.VMEM((6, 1, R), F32),
            pltpu.VMEM((3, 1, R), F32),
            pltpu.VMEM((15, 1, R), F32),
            pltpu.VMEM((3, 256, D), BF),
            pltpu.VMEM((2, 256, D), BF),
            pltpu.VMEM((128, D), BF),
            pltpu.VMEM((3, 128, D), BF),
            pltpu.VMEM((2, 128, D), BF),
            pltpu.VMEM((4, 128, D), BF),
            pltpu.VMEM((128, D), BF),
            pltpu.VMEM((128, D), BF),
            pltpu.VMEM((2, 2, Q, D), BF),
            pltpu.VMEM((2, Q, D), BF),
            pltpu.VMEM((2, 4, 64, D), BF),
            pltpu.VMEM((3, 2, 64, D), BF),
            pltpu.VMEM((2, 64, D), BF),
            pltpu.VMEM((3, 2, 16, D), BF),
            pltpu.VMEM((2, 16, D), BF),
            pltpu.VMEM((16, D), BF),
            dma,
            dma((18,)), dma((18,)),
            dma((3,)), dma((3,)),
            dma((15,)), dma((15,)),
            dma((23,)), dma((23,)),
            dma((14,)), dma((14,)),
        ],
        compiler_params=pltpu.CompilerParams(
            collective_id=0, has_side_effects=True, vmem_limit_bytes=56 * 2**20
        ),
        name="margin_softmax_backward",
    )(embeddings, order(labels), order(row_weight), prototypes)


def solution(mesh):
    return jax.shard_map(
        on_device,
        mesh=mesh,
        in_specs=(P(("dp", "cls"), None), P("dp"), P("dp"), P("cls", None)),
        out_specs=(P(("dp", "cls"), None), P("cls", None)),
        check_vma=False,
    )
```

```python
import math

import jax
import jax.numpy as jnp
from jax import lax
from jax.experimental import pallas as pl
from jax.experimental.pallas import tpu as pltpu
from jax.sharding import PartitionSpec as P

scale_factor = 64.0
margin = 0.5
sine_floor = 0.04
norm_eps = 1e-06
log2e = 1.4426950408889634
MESH = pl.DeviceIdType.MESH
F32 = jnp.float32
BF = jnp.bfloat16

D = 512
C = 2048
R = 1024
Q = 256
CH = 256
FH = 512


def unit_rows(values):
    wide = values.astype(F32)
    inverse = lax.rsqrt(jnp.sum(wide * wide, axis=1, keepdims=True) + norm_eps)
    return (inverse, wide * inverse)


def finish_rows(direction, unit_part, inverse):
    return (
        inverse * (direction - unit_part * jnp.sum(unit_part * direction, axis=1, keepdims=True))
    ).astype(BF)


def order_rows(labels, weights, lab_ref, tot):
    pieces = [(labels >> 12), (labels >> 6) & 63, labels & 63]
    pieces = [piece.astype(F32) for piece in pieces]
    rest = weights
    for _ in range(3):
        top = rest.astype(BF).astype(F32)
        pieces.append(top)
        rest = rest - top
    stacked = jnp.concatenate(pieces, axis=0).astype(BF)
    lane = lax.broadcasted_iota(jnp.int32, (128, 512), 0)
    to = lax.broadcasted_iota(jnp.int32, (128, 512), 1)
    from_lane = ((to >> 6) & 1) * 64 + ((to >> 7) & 1) * 32 + (to >> 8) * 16 + (to & 15)
    move = jnp.where(lane == from_lane, 1.0, 0.0).astype(BF)
    moved = jnp.dot(stacked, move, preferred_element_type=F32)
    row = lax.broadcasted_iota(jnp.int32, (8, 128), 0)
    z_high = (lax.broadcasted_iota(jnp.int32, (8, 128), 1) >> 4) & 3
    for tile in range(8):
        keep = row == z_high * 2 + tile % 2
        cut = moved[:, tile // 2 * 128 : (tile // 2 + 1) * 128]
        got = [
            jnp.sum(jnp.where(keep, cut[8 * i : 8 * i + 8], 0.0), axis=0, keepdims=True)
            for i in range(6)
        ]
        lanes = slice(tile * 128, (tile + 1) * 128)
        lab_ref[:, lanes] = (got[0] * 4096.0 + got[1] * 64.0 + got[2]).astype(jnp.int32)
        tot[6, :, lanes] = got[3] + got[4] + got[5]


def kernel(
    emb_ref, lab_in, wgt_in, proto_hbm,
    emb_out, out,
    proto, unit, u, e, g, part,
    lab_ref, tot, tot_loc, tot_z,
    ra, rb, ra2, rb2, sa, sb, ta, tb,
    ed, r1, f1, r2, f2, r3, f3, r4,
    proto_sem,
    ag_s, ag_r, tl_s, tl_r, tz_s, tz_r, rs_s, rs_r, em_s, em_r,
):
    dp = lax.axis_index("dp")
    cls = lax.axis_index("cls")
    yh, x = dp // 4, dp % 4
    z, y, c = cls // 4, (cls // 2) % 2, cls % 2
    zh, zl = z // 4, z % 4

    def at_z(k):
        return (dp, ((z + k) % 16) * 4 + y * 2 + c)

    def at_local(dy, dc):
        yy = (y + dy) % 2
        cc = (c + dc) % 2
        return (dp, z * 4 + yy * 2 + cc)

    def at_x(k):
        return (yh * 4 + (x + k) % 4, cls)

    y_peer = ((1 - yh) * 4 + x, cls)
    core_peer = at_local(0, 1)
    ylo_peer = at_local(1, 0)

    def send(src, dst, ssem, rsem, where):
        cp = pltpu.make_async_remote_copy(
            src_ref=src, dst_ref=dst, send_sem=ssem, recv_sem=rsem,
            device_id=where, device_id_type=MESH,
        )
        cp.start()
        return cp

    barrier = pltpu.get_barrier_semaphore()
    friends = [at_z(k) for k in range(1, 16)]
    friends += [core_peer, ylo_peer, at_local(1, 1)]
    friends += [at_x(1), at_x(2), at_x(3), y_peer]
    for friend in friends:
        pl.semaphore_signal(barrier, inc=1, device_id=friend, device_id_type=MESH)
    load = pltpu.make_async_copy(proto_hbm, proto, proto_sem)
    load.start()
    emb_inv, emb_unit = unit_rows(emb_ref[...])
    u[c, y, zl, pl.ds(pl.multiple_of(zh * 16, 16), 16), :] = emb_unit.astype(BF)
    pl.semaphore_wait(barrier, len(friends))

    sends = []
    own_block = u.at[c, y, zl, pl.ds(pl.multiple_of(zh * 16, 16), 16)]
    p1 = [send(own_block, own_block, ag_s.at[i], ag_r.at[i], at_z(k)) for i, k in enumerate((8, 4, 12))]

    load.wait()

    def normalize(i, carry):
        rows = pl.ds(pl.multiple_of(i * CH, CH), CH)
        unit[rows, :] = unit_rows(proto[rows, :])[1].astype(BF)
        return carry

    lax.fori_loop(0, C // CH // 2, normalize, 0)
    for cp in p1:
        cp.wait()
    own_set = u.at[c, y, zl]
    p2 = [send(own_set, own_set, ag_s.at[3 + i], ag_r.at[3 + i], at_z(k)) for i, k in enumerate((2, 1, 15))]
    lax.fori_loop(C // CH // 2, C // CH, normalize, 0)
    order_rows(lab_in[...], wgt_in[...], lab_ref, tot)
    toy = [send(own_set, own_set, ag_s.at[6], ag_r.at[6], ylo_peer)]
    toc = [send(own_set, own_set, ag_s.at[10], ag_r.at[10], core_peer)]
    for i, k in enumerate((2, 1, 15)):
        p2[i].wait()
        got = u.at[c, y, (zl + 16 - k) % 4]
        toy.append(send(got, got, ag_s.at[7 + i], ag_r.at[7 + i], ylo_peer))
        toc.append(send(got, got, ag_s.at[11 + i], ag_r.at[11 + i], core_peer))

    class_iota = lax.broadcasted_iota(jnp.int32, (CH, Q), 0)
    wide_iota = lax.broadcasted_iota(jnp.int32, (FH, Q), 0)
    first_class = cls * C

    def first_pass(cc, yy):
        q = cc * 2 + yy
        lanes = pl.ds(pl.multiple_of(q * Q, Q), Q)
        labels = lab_ref[:, lanes] - first_class
        rows_u = u[cc, yy].reshape(Q, D)

        def step(i, carry):
            total, target = carry
            base = pl.multiple_of(i * FH, FH)
            cosine = lax.dot_general(
                unit[pl.ds(base, FH), :], rows_u, (((1,), (1,)), ((), ())),
                preferred_element_type=F32,
            )
            is_target = wide_iota == labels - base
            ex = jnp.where(is_target, 0.0, jnp.exp2(cosine * (scale_factor * log2e)))
            tc = jnp.where(is_target, cosine, 0.0)
            e[q, pl.ds(base, FH), :] = ex
            total = total + jnp.sum(ex.reshape(FH // 8, 8, Q), axis=0)
            target = target + jnp.sum(tc.reshape(FH // 8, 8, Q), axis=0)
            return (total, target)

        zero = jnp.zeros((8, Q), F32)
        total, target = lax.fori_loop(0, C // FH, step, (zero, zero))
        total = jnp.sum(total, axis=0, keepdims=True)
        target_cos = jnp.sum(target, axis=0, keepdims=True)
        here = (labels >= 0) & (labels < C)
        sine = jnp.sqrt(jnp.maximum(1.0 - target_cos * target_cos, sine_floor))
        target_logit = scale_factor * (target_cos * math.cos(margin) - sine * math.sin(margin))
        target_exp = jnp.exp(target_logit)
        tot[0, :, lanes] = total + jnp.where(here, target_exp, 0.0)
        bound_free = 1.0 - target_cos * target_cos > sine_floor
        slope = scale_factor * (
            math.cos(margin) + jnp.where(bound_free, math.sin(margin) * target_cos / sine, 0.0)
        )
        tot[1, :, lanes] = target_exp
        tot[2, :, lanes] = slope

    first_pass(c, y)
    for cp in toc:
        cp.wait()
    first_pass(1 - c, y)
    tod = []
    for i, k in enumerate((0, 2, 1, 15)):
        toy[i].wait()
        got = u.at[c, 1 - y, (zl + 16 - k) % 4]
        tod.append(send(got, got, ag_s.at[14 + i], ag_r.at[14 + i], core_peer))
    first_pass(c, 1 - y)
    for cp in tod:
        cp.wait()
    first_pass(1 - c, 1 - y)

    loc = []
    for i, (dy, dc) in enumerate(((1, 0), (0, 1), (1, 1))):
        loc.append(send(tot.at[0], tot_loc.at[i], tl_s.at[i], tl_r.at[i], at_local(dy, dc)))
    for cp in loc:
        cp.wait()
    slab = tot[0] + tot_loc[0] + tot_loc[1] + tot_loc[2]
    tot[3] = slab
    along = []
    order = (8, 7, 9, 6, 10, 5, 11, 4, 12, 3, 13, 2, 14, 1, 15)
    for k in order:
        along.append(send(tot.at[3], tot_z.at[k - 1], tz_s.at[k - 1], tz_r.at[k - 1], at_z(k)))
    for cp in along:
        cp.wait()
    totals = slab
    for k in range(15):
        totals = totals + tot_z[k]

    weight = tot[6]
    row_scale = scale_factor * weight / totals
    label_grad = weight * (tot[1] / totals - 1.0) * tot[2]
    tot[4] = row_scale
    tot[5] = label_grad

    def second_pass(base):
        base = pl.multiple_of(base, CH)
        rows = pl.ds(base, CH)
        for q in range(4):
            lanes = slice(q * Q, (q + 1) * Q)
            is_target = class_iota == lab_ref[:, lanes] - (first_class + base)
            grad = jnp.where(is_target, tot[5, :, lanes], e[q, rows, :] * tot[4, :, lanes])
            g[rows, lanes] = grad.astype(BF)
        part[rows, :] = jnp.dot(
            g[rows, :], u[...].reshape(R, D), preferred_element_type=F32
        ).astype(BF)

    H = C // 2
    other = H + (1 - yh) * 512
    mine = H + yh * 512

    def rows_of(ref, start, n):
        return ref.at[pl.ds(pl.multiple_of(start, 128), n)]

    rs = []
    plan = (("x", 2), ("y", 0), ("x", 1), ("y", 1), ("x", 3))
    for kind, k in plan:
        if kind == "x":
            base = ((x + k) % 4) * 256
            second_pass(base)
            rs.append(send(rows_of(part, base, 256), ra.at[k - 1], rs_s.at[k - 1], rs_r.at[k - 1], at_x(k)))
        else:
            base = other + k * 256
            second_pass(base)
            rs.append(send(rows_of(part, base, 256), rb.at[k], rs_s.at[3 + k], rs_r.at[3 + k], y_peer))
    second_pass(x * 256)
    second_pass(mine)
    second_pass(mine + 256)

    def emb_product(cc, yy):
        q = cc * 2 + yy
        lanes = pl.ds(pl.multiple_of(q * Q, Q), Q)
        ed[cc, yy] = lax.dot_general(
            g[:, lanes], unit[...], (((0,), (0,)), ((), ())), preferred_element_type=F32
        ).astype(BF)

    emb_product(1 - c, 0)
    emb_product(1 - c, 1)
    em1 = send(ed.at[1 - c], r1, em_s.at[0], em_r.at[0], core_peer)
    emb_product(c, 0)
    emb_product(c, 1)
    em1.wait()
    f1[...] = (ed[c].astype(F32) + r1[...].astype(F32)).astype(BF).reshape(2, 4, 64, D)
    em2 = []
    for i, k in enumerate((2, 1, 15)):
        for yy in range(2):
            at = 1 + i * 2 + yy
            em2.append(send(f1.at[yy, (zl + k) % 4], r2.at[i, yy], em_s.at[at], em_r.at[at], at_z(k)))

    for cp in rs:
        cp.wait()
    n = 128
    own_a = part[pl.ds(pl.multiple_of(x * 256, 256), 256), :].astype(F32)
    sum_a = own_a + ra[0].astype(F32) + ra[1].astype(F32) + ra[2].astype(F32)
    sa[...] = sum_a.astype(BF).reshape(2, n, D)
    rs2 = [send(sa.at[1 - yh], ra2, rs_s.at[5], rs_r.at[5], y_peer)]
    own_b = part[pl.ds(pl.multiple_of(mine, 256), 512), :].astype(F32)
    sum_b = own_b + rb[...].reshape(512, D).astype(F32)
    sb[...] = sum_b.astype(BF).reshape(4, n, D)
    for k in (2, 1, 3):
        rs2.append(send(sb.at[(x + k) % 4], rb2.at[k - 1], rs_s.at[5 + k], rs_r.at[5 + k], at_x(k)))

    for cp in em2:
        cp.wait()
    f2[...] = (
        f1[:, zl].astype(F32) + r2[0].astype(F32) + r2[1].astype(F32) + r2[2].astype(F32)
    ).astype(BF)
    em3 = []
    for i, k in enumerate((8, 4, 12)):
        to = pl.ds(pl.multiple_of(((zh + k // 4) % 4) * 16, 16), 16)
        for yy in range(2):
            at = 7 + i * 2 + yy
            em3.append(send(f2.at[yy, to], r3.at[i, yy], em_s.at[at], em_r.at[at], at_z(k)))

    for cp in rs2:
        cp.wait()
    at_a = pl.multiple_of(x * 256 + yh * n, n)
    at_b = pl.multiple_of(mine + x * n, n)
    inv_a, unit_a = unit_rows(proto[pl.ds(at_a, n), :])
    dir_a = sa[yh].astype(F32) + ra2[...].astype(F32)
    out[pl.ds(at_a, n), :] = finish_rows(dir_a, unit_a, inv_a)
    ag2 = []
    mine_a = out.at[pl.ds(at_a, n)]
    ag_y = send(mine_a, mine_a, rs_s.at[9], rs_r.at[9], y_peer)
    inv_b, unit_b = unit_rows(proto[pl.ds(at_b, n), :])
    dir_b = sb[x].astype(F32) + rb2[0].astype(F32) + rb2[1].astype(F32) + rb2[2].astype(F32)
    out[pl.ds(at_b, n), :] = finish_rows(dir_b, unit_b, inv_b)
    mine_b = out.at[pl.ds(at_b, n)]
    ag_x = []
    for k in (2, 1, 3):
        ag_x.append(send(mine_b, mine_b, rs_s.at[9 + k], rs_r.at[9 + k], at_x(k)))
    ag2.append(send(mine_b, mine_b, rs_s.at[13], rs_r.at[13], y_peer))
    for k in (2, 1, 3):
        ag2.append(send(mine_a, mine_a, rs_s.at[13 + k], rs_r.at[13 + k], at_x(k)))

    for cp in em3:
        cp.wait()
    own3 = pl.ds(pl.multiple_of(zh * 16, 16), 16)
    f3[...] = (
        f2[:, own3].astype(F32) + r3[0].astype(F32) + r3[1].astype(F32) + r3[2].astype(F32)
    ).astype(BF)
    em4 = send(f3.at[1 - y], r4, em_s.at[13], em_r.at[13], ylo_peer)

    ag_y.wait()
    got = out.at[pl.ds(pl.multiple_of(x * 256 + (1 - yh) * n, n), n)]
    for k in (2, 1, 3):
        ag2.append(send(got, got, rs_s.at[16 + k], rs_r.at[16 + k], at_x(k)))
    for i, k in enumerate((2, 1, 3)):
        ag_x[i].wait()
        got = out.at[pl.ds(pl.multiple_of(mine + ((x + 4 - k) % 4) * n, n), n)]
        ag2.append(send(got, got, rs_s.at[20 + i], rs_r.at[20 + i], y_peer))

    em4.wait()
    emb_dir = f3[y].astype(F32) + r4[...].astype(F32)
    emb_inv, emb_unit = unit_rows(emb_ref[...])
    emb_out[...] = finish_rows(emb_dir, emb_unit, emb_inv)

    for cp in ag2:
        cp.wait()


def write_out(emb_grad, proto_grad, emb_out, proto_out, emb_sem, proto_sem):
    copies = [
        pltpu.make_async_copy(proto_grad, proto_out, proto_sem),
        pltpu.make_async_copy(emb_grad, emb_out, emb_sem),
    ]
    for cp in copies:
        cp.start()
    for cp in copies:
        cp.wait()


def on_device(embeddings, labels, row_weight, prototypes):
    vmem = pl.BlockSpec(memory_space=pltpu.VMEM)
    dma = pltpu.SemaphoreType.DMA
    grads = pl.pallas_call(
        kernel,
        out_shape=(
            pltpu.VMEM((16, D), BF),
            pltpu.VMEM((C, D), BF),
        ),
        in_specs=[vmem, vmem, vmem, pl.BlockSpec(memory_space=pl.ANY)],
        out_specs=(vmem, vmem),
        scratch_shapes=[
            pltpu.VMEM((C, D), BF),
            pltpu.VMEM((C, D), BF),
            pltpu.VMEM((2, 2, 4, 64, D), BF),
            pltpu.VMEM((4, C, Q), F32),
            pltpu.VMEM((C, R), BF),
            pltpu.VMEM((C, D), BF),
            pltpu.VMEM((1, R), jnp.int32),
            pltpu.VMEM((7, 1, R), F32),
            pltpu.VMEM((3, 1, R), F32),
            pltpu.VMEM((15, 1, R), F32),
            pltpu.VMEM((3, 256, D), BF),
            pltpu.VMEM((2, 256, D), BF),
            pltpu.VMEM((128, D), BF),
            pltpu.VMEM((3, 128, D), BF),
            pltpu.VMEM((2, 128, D), BF),
            pltpu.VMEM((4, 128, D), BF),
            pltpu.VMEM((128, D), BF),
            pltpu.VMEM((128, D), BF),
            pltpu.VMEM((2, 2, Q, D), BF),
            pltpu.VMEM((2, Q, D), BF),
            pltpu.VMEM((2, 4, 64, D), BF),
            pltpu.VMEM((3, 2, 64, D), BF),
            pltpu.VMEM((2, 64, D), BF),
            pltpu.VMEM((3, 2, 16, D), BF),
            pltpu.VMEM((2, 16, D), BF),
            pltpu.VMEM((16, D), BF),
            dma,
            dma((18,)), dma((18,)),
            dma((3,)), dma((3,)),
            dma((15,)), dma((15,)),
            dma((23,)), dma((23,)),
            dma((14,)), dma((14,)),
        ],
        compiler_params=pltpu.CompilerParams(
            collective_id=0, has_side_effects=True, vmem_limit_bytes=56 * 2**20
        ),
        name="margin_softmax_backward",
    )(embeddings, labels.reshape(8, 128), row_weight.reshape(8, 128), prototypes)
    anywhere = pl.BlockSpec(memory_space=pl.ANY)
    return pl.pallas_call(
        write_out,
        out_shape=(
            jax.ShapeDtypeStruct((16, D), BF),
            jax.ShapeDtypeStruct((C, D), BF),
        ),
        in_specs=[vmem, vmem],
        out_specs=(anywhere, anywhere),
        scratch_shapes=[dma, dma],
        name="write_out",
    )(*grads)


def solution(mesh):
    return jax.shard_map(
        on_device,
        mesh=mesh,
        in_specs=(P(("dp", "cls"), None), P("dp"), P("dp"), P("cls", None)),
        out_specs=(P(("dp", "cls"), None), P("cls", None)),
        check_vma=False,
    )
```

```python
import math

import jax
import jax.numpy as jnp
from jax import lax
from jax.experimental import pallas as pl
from jax.experimental.pallas import tpu as pltpu
from jax.sharding import PartitionSpec as P

scale_factor = 64.0
margin = 0.5
sine_floor = 0.04
norm_eps = 1e-06
log2e = 1.4426950408889634
MESH = pl.DeviceIdType.MESH
F32 = jnp.float32
BF = jnp.bfloat16

D = 512
C = 2048
R = 1024
Q = 256
NA = 144
NB = 112
FIRST_B = 8 * NA
CH = 256
FH = 512


def unit_rows(values):
    wide = values.astype(F32)
    inverse = lax.rsqrt(jnp.sum(wide * wide, axis=1, keepdims=True) + norm_eps)
    return (inverse, wide * inverse)


def finish_rows(direction, unit_part, inverse):
    return (
        inverse * (direction - unit_part * jnp.sum(unit_part * direction, axis=1, keepdims=True))
    ).astype(BF)


def order_rows(labels, weights, lab_ref, tot):
    pieces = [(labels >> 12), (labels >> 6) & 63, labels & 63]
    pieces = [piece.astype(F32) for piece in pieces]
    rest = weights
    for _ in range(3):
        top = rest.astype(BF).astype(F32)
        pieces.append(top)
        rest = rest - top
    stacked = jnp.concatenate(pieces, axis=0).astype(BF)
    lane = lax.broadcasted_iota(jnp.int32, (128, 512), 0)
    to = lax.broadcasted_iota(jnp.int32, (128, 512), 1)
    from_lane = ((to >> 6) & 1) * 64 + ((to >> 7) & 1) * 32 + (to >> 8) * 16 + (to & 15)
    move = jnp.where(lane == from_lane, 1.0, 0.0).astype(BF)
    moved = jnp.dot(stacked, move, preferred_element_type=F32)
    row = lax.broadcasted_iota(jnp.int32, (8, 128), 0)
    z_high = (lax.broadcasted_iota(jnp.int32, (8, 128), 1) >> 4) & 3
    for tile in range(8):
        keep = row == z_high * 2 + tile % 2
        cut = moved[:, tile // 2 * 128 : (tile // 2 + 1) * 128]
        got = [
            jnp.sum(jnp.where(keep, cut[8 * i : 8 * i + 8], 0.0), axis=0, keepdims=True)
            for i in range(6)
        ]
        lanes = slice(tile * 128, (tile + 1) * 128)
        lab_ref[:, lanes] = (got[0] * 4096.0 + got[1] * 64.0 + got[2]).astype(jnp.int32)
        tot[6, :, lanes] = got[3] + got[4] + got[5]


def kernel(
    emb_ref, lab_in, wgt_in, proto_hbm,
    emb_out, out,
    proto, unit, u, e, g, part,
    lab_ref, tot, tot_loc, tot_z,
    fw, both, ra, rb, ra2, rb2, sa, sb,
    ed, r1, f1, r2, f2, r3, f3, r4,
    proto_sem,
    ag_s, ag_r, tl_s, tl_r, tz_s, tz_r, rs_s, rs_r, em_s, em_r,
):
    dp = lax.axis_index("dp")
    cls = lax.axis_index("cls")
    yh, x = dp // 4, dp % 4
    z, y, c = cls // 4, (cls // 2) % 2, cls % 2
    zh, zl = z // 4, z % 4

    def at_z(k):
        return (dp, ((z + k) % 16) * 4 + y * 2 + c)

    def at_local(dy, dc):
        yy = (y + dy) % 2
        cc = (c + dc) % 2
        return (dp, z * 4 + yy * 2 + cc)

    def at_x(k):
        return (yh * 4 + (x + k) % 4, cls)

    y_peer = ((1 - yh) * 4 + x, cls)
    core_peer = at_local(0, 1)
    ylo_peer = at_local(1, 0)

    def send(src, dst, ssem, rsem, where):
        cp = pltpu.make_async_remote_copy(
            src_ref=src, dst_ref=dst, send_sem=ssem, recv_sem=rsem,
            device_id=where, device_id_type=MESH,
        )
        cp.start()
        return cp

    barrier = pltpu.get_barrier_semaphore()
    friends = [at_z(k) for k in range(1, 16)]
    friends += [core_peer, ylo_peer, at_local(1, 1)]
    friends += [at_x(1), at_x(2), at_x(3), y_peer]
    for friend in friends:
        pl.semaphore_signal(barrier, inc=1, device_id=friend, device_id_type=MESH)
    load = pltpu.make_async_copy(proto_hbm, proto, proto_sem)
    load.start()
    emb_inv, emb_unit = unit_rows(emb_ref[...])
    u[c, y, zl, pl.ds(pl.multiple_of(zh * 16, 16), 16), :] = emb_unit.astype(BF)
    pl.semaphore_wait(barrier, len(friends))

    sends = []
    own_block = u.at[c, y, zl, pl.ds(pl.multiple_of(zh * 16, 16), 16)]
    p1 = [send(own_block, own_block, ag_s.at[i], ag_r.at[i], at_z(k)) for i, k in enumerate((8, 4, 12))]

    load.wait()

    def normalize(i, carry):
        rows = pl.ds(pl.multiple_of(i * CH, CH), CH)
        unit[rows, :] = unit_rows(proto[rows, :])[1].astype(BF)
        return carry

    lax.fori_loop(0, C // CH // 2, normalize, 0)
    for cp in p1:
        cp.wait()
    own_set = u.at[c, y, zl]
    p2 = [send(own_set, own_set, ag_s.at[3 + i], ag_r.at[3 + i], at_z(k)) for i, k in enumerate((2, 1, 15))]
    lax.fori_loop(C // CH // 2, C // CH, normalize, 0)
    order_rows(lab_in[...], wgt_in[...], lab_ref, tot)
    toy = [send(own_set, own_set, ag_s.at[6], ag_r.at[6], ylo_peer)]
    toc = [send(own_set, own_set, ag_s.at[10], ag_r.at[10], core_peer)]
    for i, k in enumerate((2, 1, 15)):
        p2[i].wait()
        got = u.at[c, y, (zl + 16 - k) % 4]
        toy.append(send(got, got, ag_s.at[7 + i], ag_r.at[7 + i], ylo_peer))
        toc.append(send(got, got, ag_s.at[11 + i], ag_r.at[11 + i], core_peer))

    class_iota = lax.broadcasted_iota(jnp.int32, (2 * NA, Q), 0)
    wide_iota = lax.broadcasted_iota(jnp.int32, (FH, Q), 0)
    first_class = cls * C

    def first_pass(cc, yy):
        q = cc * 2 + yy
        lanes = pl.ds(pl.multiple_of(q * Q, Q), Q)
        labels = lab_ref[:, lanes] - first_class
        rows_u = u[cc, yy].reshape(Q, D)

        def step(i, carry):
            total, target = carry
            base = pl.multiple_of(i * FH, FH)
            cosine = lax.dot_general(
                unit[pl.ds(base, FH), :], rows_u, (((1,), (1,)), ((), ())),
                preferred_element_type=F32,
            )
            is_target = wide_iota == labels - base
            ex = jnp.where(is_target, 0.0, jnp.exp2(cosine * (scale_factor * log2e)))
            tc = jnp.where(is_target, cosine, 0.0)
            e[q, pl.ds(base, FH), :] = ex
            total = total + jnp.sum(ex.reshape(FH // 8, 8, Q), axis=0)
            target = target + jnp.sum(tc.reshape(FH // 8, 8, Q), axis=0)
            return (total, target)

        zero = jnp.zeros((8, Q), F32)
        total, target = lax.fori_loop(0, C // FH, step, (zero, zero))
        total = jnp.sum(total, axis=0, keepdims=True)
        target_cos = jnp.sum(target, axis=0, keepdims=True)
        here = (labels >= 0) & (labels < C)
        sine = jnp.sqrt(jnp.maximum(1.0 - target_cos * target_cos, sine_floor))
        target_logit = scale_factor * (target_cos * math.cos(margin) - sine * math.sin(margin))
        target_exp = jnp.exp(target_logit)
        tot[0, :, lanes] = total + jnp.where(here, target_exp, 0.0)
        bound_free = 1.0 - target_cos * target_cos > sine_floor
        slope = scale_factor * (
            math.cos(margin) + jnp.where(bound_free, math.sin(margin) * target_cos / sine, 0.0)
        )
        tot[1, :, lanes] = target_exp
        tot[2, :, lanes] = slope

    first_pass(c, y)
    for cp in toc:
        cp.wait()
    first_pass(1 - c, y)
    tod = []
    for i, k in enumerate((0, 2, 1, 15)):
        toy[i].wait()
        got = u.at[c, 1 - y, (zl + 16 - k) % 4]
        tod.append(send(got, got, ag_s.at[14 + i], ag_r.at[14 + i], core_peer))
    first_pass(c, 1 - y)
    for cp in tod:
        cp.wait()
    first_pass(1 - c, 1 - y)

    loc = []
    for i, (dy, dc) in enumerate(((1, 0), (0, 1), (1, 1))):
        loc.append(send(tot.at[0], tot_loc.at[i], tl_s.at[i], tl_r.at[i], at_local(dy, dc)))
    for cp in loc:
        cp.wait()
    slab = tot[0] + tot_loc[0] + tot_loc[1] + tot_loc[2]
    tot[3] = slab
    along = []
    order = (8, 7, 9, 6, 10, 5, 11, 4, 12, 3, 13, 2, 14, 1, 15)
    for k in order:
        along.append(send(tot.at[3], tot_z.at[k - 1], tz_s.at[k - 1], tz_r.at[k - 1], at_z(k)))
    for cp in along:
        cp.wait()
    totals = slab
    for k in range(15):
        totals = totals + tot_z[k]

    weight = tot[6]
    row_scale = scale_factor * weight / totals
    label_grad = weight * (tot[1] / totals - 1.0) * tot[2]
    tot[4] = row_scale
    tot[5] = label_grad

    def second_pass(base, n):
        base = pl.multiple_of(base, 16)
        rows = pl.ds(base, n)
        for q in range(4):
            lanes = slice(q * Q, (q + 1) * Q)
            is_target = class_iota[:n] == lab_ref[:, lanes] - (first_class + base)
            grad = jnp.where(is_target, tot[5, :, lanes], e[q, rows, :] * tot[4, :, lanes])
            g[rows, lanes] = grad.astype(BF)
        part[rows, :] = jnp.dot(
            g[rows, :], u[...].reshape(R, D), preferred_element_type=F32
        ).astype(BF)

    def rows_of(ref, start, n):
        return ref.at[pl.ds(pl.multiple_of(start, 16), n)]

    def value(ref, start, n):
        return ref[pl.ds(pl.multiple_of(start, 16), n), :].astype(F32)

    def a_rows(k):
        return ((x + k) % 4) * (2 * NA)

    other = FIRST_B + (1 - yh) * (4 * NB)
    mine = FIRST_B + yh * (4 * NB)
    to_left, to_right = at_x(3), at_x(1)

    second_pass(a_rows(2), 2 * NA)
    far_r = send(rows_of(part, a_rows(2), NA), fw.at[0], rs_s.at[0], rs_r.at[0], to_right)
    far_l = send(rows_of(part, a_rows(2) + NA, NA), fw.at[1], rs_s.at[1], rs_r.at[1], to_left)
    second_pass(other, 2 * NB)
    rs_b = [send(rows_of(part, other, 2 * NB), rb.at[0], rs_s.at[2], rs_r.at[2], y_peer)]
    second_pass(a_rows(1), 2 * NA)
    rs_a = [send(rows_of(part, a_rows(1) + NA, NA), ra.at[0, 1], rs_s.at[3], rs_r.at[3], to_right)]
    second_pass(a_rows(3), 2 * NA)
    rs_a.append(send(rows_of(part, a_rows(3), NA), ra.at[1, 0], rs_s.at[4], rs_r.at[4], to_left))
    second_pass(other + 2 * NB, 2 * NB)
    rs_b.append(send(rows_of(part, other + 2 * NB, 2 * NB), rb.at[1], rs_s.at[5], rs_r.at[5], y_peer))
    far_r.wait()
    both[0] = (value(part, a_rows(1), NA) + fw[0].astype(F32)).astype(BF)
    rs_a.append(send(both.at[0], ra.at[0, 0], rs_s.at[6], rs_r.at[6], to_right))
    far_l.wait()
    both[1] = (value(part, a_rows(3) + NA, NA) + fw[1].astype(F32)).astype(BF)
    rs_a.append(send(both.at[1], ra.at[1, 1], rs_s.at[7], rs_r.at[7], to_left))
    second_pass(a_rows(0), 2 * NA)
    second_pass(mine, 2 * NB)
    second_pass(mine + 2 * NB, 2 * NB)

    def emb_product(cc, yy):
        q = cc * 2 + yy
        lanes = pl.ds(pl.multiple_of(q * Q, Q), Q)
        ed[cc, yy] = lax.dot_general(
            g[:, lanes], unit[...], (((0,), (0,)), ((), ())), preferred_element_type=F32
        ).astype(BF)

    emb_product(1 - c, 0)
    emb_product(1 - c, 1)
    em1 = send(ed.at[1 - c], r1, em_s.at[0], em_r.at[0], core_peer)
    emb_product(c, 0)
    emb_product(c, 1)
    em1.wait()
    f1[...] = (ed[c].astype(F32) + r1[...].astype(F32)).astype(BF).reshape(2, 4, 64, D)
    em2 = []
    for i, k in enumerate((2, 1, 15)):
        for yy in range(2):
            at = 1 + i * 2 + yy
            em2.append(send(f1.at[yy, (zl + k) % 4], r2.at[i, yy], em_s.at[at], em_r.at[at], at_z(k)))

    for cp in rs_b:
        cp.wait()
    sum_b = value(part, mine, 4 * NB) + rb[...].reshape(4 * NB, D).astype(F32)
    sb[...] = sum_b.astype(BF).reshape(4, NB, D)
    rs2 = []
    for k in (2, 1, 3):
        rs2.append(send(sb.at[(x + k) % 4], rb2.at[k - 1], rs_s.at[8 + k], rs_r.at[8 + k], at_x(k)))
    for cp in rs_a:
        cp.wait()
    sum_a = value(part, a_rows(0), 2 * NA)
    for side in range(2):
        sum_a = sum_a + ra[side].reshape(2 * NA, D).astype(F32)
    sa[...] = sum_a.astype(BF).reshape(2, NA, D)
    rs2.append(send(sa.at[1 - yh], ra2, rs_s.at[8], rs_r.at[8], y_peer))

    for cp in em2:
        cp.wait()
    f2[...] = (
        f1[:, zl].astype(F32) + r2[0].astype(F32) + r2[1].astype(F32) + r2[2].astype(F32)
    ).astype(BF)
    em3 = []
    for i, k in enumerate((8, 4, 12)):
        to = pl.ds(pl.multiple_of(((zh + k // 4) % 4) * 16, 16), 16)
        for yy in range(2):
            at = 7 + i * 2 + yy
            em3.append(send(f2.at[yy, to], r3.at[i, yy], em_s.at[at], em_r.at[at], at_z(k)))

    for cp in rs2:
        cp.wait()
    serial = [12]

    def pass_on(start, n, where):
        at = serial[0]
        serial[0] += 1
        rows = rows_of(out, start, n)
        return send(rows, rows, rs_s.at[at], rs_r.at[at], where)

    def a_start(k, half):
        return a_rows(k) + half * NA

    def b_start(k, half):
        return FIRST_B + half * (4 * NB) + ((x + k) % 4) * NB

    mine_a, mine_b = a_start(0, yh), b_start(0, yh)
    dir_b = value(sb.at[x], 0, NB)
    for k in range(3):
        dir_b = dir_b + rb2[k].astype(F32)
    inv_b, unit_b = unit_rows(value(proto, mine_b, NB))
    out[pl.ds(pl.multiple_of(mine_b, 16), NB), :] = finish_rows(dir_b, unit_b, inv_b)
    b_near = [pass_on(mine_b, NB, to_right), pass_on(mine_b, NB, to_left)]
    rest = [pass_on(mine_b, NB, y_peer)]
    dir_a = sa[yh].astype(F32) + ra2[...].astype(F32)
    inv_a, unit_a = unit_rows(value(proto, mine_a, NA))
    out[pl.ds(pl.multiple_of(mine_a, 16), NA), :] = finish_rows(dir_a, unit_a, inv_a)
    a_cross = pass_on(mine_a, NA, y_peer)
    a_near = [pass_on(mine_a, NA, to_right), pass_on(mine_a, NA, to_left)]

    for cp in em3:
        cp.wait()
    own3 = pl.ds(pl.multiple_of(zh * 16, 16), 16)
    f3[...] = (
        f2[:, own3].astype(F32) + r3[0].astype(F32) + r3[1].astype(F32) + r3[2].astype(F32)
    ).astype(BF)
    em4 = send(f3.at[1 - y], r4, em_s.at[13], em_r.at[13], ylo_peer)

    b_cut, a_cut = 64, 80
    b_near[0].wait()
    b_far = [pass_on(b_start(3, yh), b_cut, to_right)]
    rest.append(pass_on(b_start(3, yh), NB, y_peer))
    b_near[1].wait()
    b_far.append(pass_on(b_start(1, yh) + b_cut, NB - b_cut, to_left))
    rest.append(pass_on(b_start(1, yh), NB, y_peer))
    a_cross.wait()
    c_near = [pass_on(a_start(0, 1 - yh), NA, to_right), pass_on(a_start(0, 1 - yh), NA, to_left)]
    a_near[0].wait()
    rest.append(pass_on(a_start(3, yh), a_cut, to_right))
    a_near[1].wait()
    rest.append(pass_on(a_start(1, yh) + a_cut, NA - a_cut, to_left))
    b_far[0].wait()
    rest.append(pass_on(b_start(2, yh), b_cut, y_peer))
    b_far[1].wait()
    rest.append(pass_on(b_start(2, yh) + b_cut, NB - b_cut, y_peer))
    c_near[0].wait()
    rest.append(pass_on(a_start(3, 1 - yh), a_cut, to_right))
    c_near[1].wait()
    rest.append(pass_on(a_start(1, 1 - yh) + a_cut, NA - a_cut, to_left))

    em4.wait()
    emb_dir = f3[y].astype(F32) + r4[...].astype(F32)
    emb_inv, emb_unit = unit_rows(emb_ref[...])
    emb_out[...] = finish_rows(emb_dir, emb_unit, emb_inv)

    for cp in rest:
        cp.wait()


def write_out(emb_grad, proto_grad, emb_out, proto_out, emb_sem, proto_sem):
    copies = [
        pltpu.make_async_copy(proto_grad, proto_out, proto_sem),
        pltpu.make_async_copy(emb_grad, emb_out, emb_sem),
    ]
    for cp in copies:
        cp.start()
    for cp in copies:
        cp.wait()


def on_device(embeddings, labels, row_weight, prototypes):
    vmem = pl.BlockSpec(memory_space=pltpu.VMEM)
    dma = pltpu.SemaphoreType.DMA
    grads = pl.pallas_call(
        kernel,
        out_shape=(
            pltpu.VMEM((16, D), BF),
            pltpu.VMEM((C, D), BF),
        ),
        in_specs=[vmem, vmem, vmem, pl.BlockSpec(memory_space=pl.ANY)],
        out_specs=(vmem, vmem),
        scratch_shapes=[
            pltpu.VMEM((C, D), BF),
            pltpu.VMEM((C, D), BF),
            pltpu.VMEM((2, 2, 4, 64, D), BF),
            pltpu.VMEM((4, C, Q), F32),
            pltpu.VMEM((C, R), BF),
            pltpu.VMEM((C, D), BF),
            pltpu.VMEM((1, R), jnp.int32),
            pltpu.VMEM((7, 1, R), F32),
            pltpu.VMEM((3, 1, R), F32),
            pltpu.VMEM((15, 1, R), F32),
            pltpu.VMEM((2, NA, D), BF),
            pltpu.VMEM((2, NA, D), BF),
            pltpu.VMEM((2, 2, NA, D), BF),
            pltpu.VMEM((2, 2 * NB, D), BF),
            pltpu.VMEM((NA, D), BF),
            pltpu.VMEM((3, NB, D), BF),
            pltpu.VMEM((2, NA, D), BF),
            pltpu.VMEM((4, NB, D), BF),
            pltpu.VMEM((2, 2, Q, D), BF),
            pltpu.VMEM((2, Q, D), BF),
            pltpu.VMEM((2, 4, 64, D), BF),
            pltpu.VMEM((3, 2, 64, D), BF),
            pltpu.VMEM((2, 64, D), BF),
            pltpu.VMEM((3, 2, 16, D), BF),
            pltpu.VMEM((2, 16, D), BF),
            pltpu.VMEM((16, D), BF),
            dma,
            dma((18,)), dma((18,)),
            dma((3,)), dma((3,)),
            dma((15,)), dma((15,)),
            dma((30,)), dma((30,)),
            dma((14,)), dma((14,)),
        ],
        compiler_params=pltpu.CompilerParams(
            collective_id=0, has_side_effects=True, vmem_limit_bytes=56 * 2**20
        ),
        name="margin_softmax_backward",
    )(embeddings, labels.reshape(8, 128), row_weight.reshape(8, 128), prototypes)
    anywhere = pl.BlockSpec(memory_space=pl.ANY)
    return pl.pallas_call(
        write_out,
        out_shape=(
            jax.ShapeDtypeStruct((16, D), BF),
            jax.ShapeDtypeStruct((C, D), BF),
        ),
        in_specs=[vmem, vmem],
        out_specs=(anywhere, anywhere),
        scratch_shapes=[dma, dma],
        name="write_out",
    )(*[pltpu.with_memory_space_constraint(grad, pltpu.VMEM) for grad in grads])


def solution(mesh):
    return jax.shard_map(
        on_device,
        mesh=mesh,
        in_specs=(P(("dp", "cls"), None), P("dp"), P("dp"), P("cls", None)),
        out_specs=(P(("dp", "cls"), None), P("cls", None)),
        check_vma=False,
    )
```

```python
import math

import jax
import jax.numpy as jnp
from jax import lax
from jax.experimental import pallas as pl
from jax.experimental.pallas import tpu as pltpu
from jax.sharding import PartitionSpec as P

scale_factor = 64.0
margin = 0.5
sine_floor = 0.04
norm_eps = 1e-06
log2e = 1.4426950408889634
MESH = pl.DeviceIdType.MESH
F32 = jnp.float32
BF = jnp.bfloat16

D = 512
C = 2048
R = 1024
Q = 256
NA = 144
NB = 112
FIRST_B = 8 * NA
CH = 256


def unit_rows(values):
    wide = values.astype(F32)
    inverse = lax.rsqrt(jnp.sum(wide * wide, axis=1, keepdims=True) + norm_eps)
    return (inverse, wide * inverse)


def finish_rows(direction, unit_part, inverse):
    return (
        inverse * (direction - unit_part * jnp.sum(unit_part * direction, axis=1, keepdims=True))
    ).astype(BF)


def order_rows(labels, weights, lab_ref, tot):
    pieces = [(labels >> 12), (labels >> 6) & 63, labels & 63]
    pieces = [piece.astype(F32) for piece in pieces]
    rest = weights
    for _ in range(3):
        top = rest.astype(BF).astype(F32)
        pieces.append(top)
        rest = rest - top
    stacked = jnp.concatenate(pieces, axis=0).astype(BF)
    lane = lax.broadcasted_iota(jnp.int32, (128, 512), 0)
    to = lax.broadcasted_iota(jnp.int32, (128, 512), 1)
    from_lane = ((to >> 6) & 1) * 64 + ((to >> 7) & 1) * 32 + (to >> 8) * 16 + (to & 15)
    move = jnp.where(lane == from_lane, 1.0, 0.0).astype(BF)
    moved = jnp.dot(stacked, move, preferred_element_type=F32)
    row = lax.broadcasted_iota(jnp.int32, (8, 128), 0)
    z_high = (lax.broadcasted_iota(jnp.int32, (8, 128), 1) >> 4) & 3
    for tile in range(8):
        keep = row == z_high * 2 + tile % 2
        cut = moved[:, tile // 2 * 128 : (tile // 2 + 1) * 128]
        got = [
            jnp.sum(jnp.where(keep, cut[8 * i : 8 * i + 8], 0.0), axis=0, keepdims=True)
            for i in range(6)
        ]
        lanes = slice(tile * 128, (tile + 1) * 128)
        lab_ref[:, lanes] = (got[0] * 4096.0 + got[1] * 64.0 + got[2]).astype(jnp.int32)
        tot[6, :, lanes] = got[3] + got[4] + got[5]


def kernel(
    emb_hbm, lab_hbm, wgt_hbm, proto_hbm,
    emb_out, out,
    emb_ref, lab_in, wgt_in, proto, unit, u, e, g, part,
    lab_ref, tot, tot_loc, tot_z,
    fw, both, ra, rb, ra2, rb2, sa, sb,
    ed, r1, f1, r2, f2, r3, f3, r4,
    in_sems,
    ag_s, ag_r, tl_s, tl_r, tz_s, tz_r, rs_s, rs_r, em_s, em_r,
):
    dp = lax.axis_index("dp")
    cls = lax.axis_index("cls")
    yh, x = dp // 4, dp % 4
    z, y, c = cls // 4, (cls // 2) % 2, cls % 2
    zh, zl = z // 4, z % 4

    def at_z(k):
        return (dp, ((z + k) % 16) * 4 + y * 2 + c)

    def at_local(dy, dc):
        yy = (y + dy) % 2
        cc = (c + dc) % 2
        return (dp, z * 4 + yy * 2 + cc)

    def at_x(k):
        return (yh * 4 + (x + k) % 4, cls)

    y_peer = ((1 - yh) * 4 + x, cls)
    core_peer = at_local(0, 1)
    ylo_peer = at_local(1, 0)

    def send(src, dst, ssem, rsem, where):
        cp = pltpu.make_async_remote_copy(
            src_ref=src, dst_ref=dst, send_sem=ssem, recv_sem=rsem,
            device_id=where, device_id_type=MESH,
        )
        cp.start()
        return cp

    barrier = pltpu.get_barrier_semaphore()
    friends = [at_z(k) for k in (8, 4, 12, 7, 9, 6, 10, 5, 11, 3, 13, 2, 14, 1, 15)]
    friends += [core_peer, ylo_peer, at_local(1, 1)]
    friends += [at_x(1), at_x(2), at_x(3), y_peer]
    for friend in friends:
        pl.semaphore_signal(barrier, inc=1, device_id=friend, device_id_type=MESH)
    sources = ((emb_hbm, emb_ref), (lab_hbm, lab_in), (wgt_hbm, wgt_in), (proto_hbm, proto))
    loads = [pltpu.make_async_copy(src, dst, in_sems.at[i]) for i, (src, dst) in enumerate(sources)]
    for load in loads:
        load.start()
    loads[0].wait()
    emb_inv, emb_unit = unit_rows(emb_ref[...])
    u[c, y, zl, pl.ds(pl.multiple_of(zh * 16, 16), 16), :] = emb_unit.astype(BF)
    pl.semaphore_wait(barrier, len(friends))

    sends = []
    own_block = u.at[c, y, zl, pl.ds(pl.multiple_of(zh * 16, 16), 16)]
    p1 = [send(own_block, own_block, ag_s.at[i], ag_r.at[i], at_z(k)) for i, k in enumerate((8, 4, 12))]

    for load in loads[1:]:
        load.wait()

    def normalize(i, carry):
        rows = pl.ds(pl.multiple_of(i * CH, CH), CH)
        unit[rows, :] = unit_rows(proto[rows, :])[1].astype(BF)
        return carry

    lax.fori_loop(0, C // CH // 2, normalize, 0)
    for cp in p1:
        cp.wait()
    own_set = u.at[c, y, zl]
    p2 = [send(own_set, own_set, ag_s.at[3 + i], ag_r.at[3 + i], at_z(k)) for i, k in enumerate((1, 15, 2))]
    lax.fori_loop(C // CH // 2, C // CH, normalize, 0)
    order_rows(lab_in[...], wgt_in[...], lab_ref, tot)
    toy = [send(own_set, own_set, ag_s.at[6], ag_r.at[6], ylo_peer)]
    toc = [send(own_set, own_set, ag_s.at[10], ag_r.at[10], core_peer)]
    for i, k in enumerate((1, 15, 2)):
        p2[i].wait()
        got = u.at[c, y, (zl + 16 - k) % 4]
        toy.append(send(got, got, ag_s.at[7 + i], ag_r.at[7 + i], ylo_peer))
        toc.append(send(got, got, ag_s.at[11 + i], ag_r.at[11 + i], core_peer))

    class_iota = lax.broadcasted_iota(jnp.int32, (C, Q), 0)
    first_class = cls * C

    def first_pass(cc, yy):
        q = cc * 2 + yy
        lanes = pl.ds(pl.multiple_of(q * Q, Q), Q)
        labels = lab_ref[:, lanes] - first_class
        rows_u = u[cc, yy].reshape(Q, D)

        cosine = lax.dot_general(
            unit[...], rows_u, (((1,), (1,)), ((), ())), preferred_element_type=F32
        )
        is_target = class_iota == labels
        ex = jnp.where(is_target, 0.0, jnp.exp2(cosine * (scale_factor * log2e)))
        e[q] = ex
        total = jnp.sum(ex, axis=0, keepdims=True)
        target_cos = jnp.sum(jnp.where(is_target, cosine, 0.0), axis=0, keepdims=True)
        here = (labels >= 0) & (labels < C)
        sine = jnp.sqrt(jnp.maximum(1.0 - target_cos * target_cos, sine_floor))
        target_logit = scale_factor * (target_cos * math.cos(margin) - sine * math.sin(margin))
        target_exp = jnp.exp(target_logit)
        tot[0, :, lanes] = total + jnp.where(here, target_exp, 0.0)
        bound_free = 1.0 - target_cos * target_cos > sine_floor
        slope = scale_factor * (
            math.cos(margin) + jnp.where(bound_free, math.sin(margin) * target_cos / sine, 0.0)
        )
        tot[1, :, lanes] = target_exp
        tot[2, :, lanes] = slope

    first_pass(c, y)
    for cp in toc:
        cp.wait()
    first_pass(1 - c, y)
    tod = []
    for i, k in enumerate((0, 1, 15, 2)):
        toy[i].wait()
        got = u.at[c, 1 - y, (zl + 16 - k) % 4]
        tod.append(send(got, got, ag_s.at[14 + i], ag_r.at[14 + i], core_peer))
    first_pass(c, 1 - y)
    for cp in tod:
        cp.wait()
    first_pass(1 - c, 1 - y)

    loc = []
    for i, (dy, dc) in enumerate(((1, 0), (0, 1), (1, 1))):
        loc.append(send(tot.at[0], tot_loc.at[i], tl_s.at[i], tl_r.at[i], at_local(dy, dc)))
    for cp in loc:
        cp.wait()
    slab = tot[0] + tot_loc[0] + tot_loc[1] + tot_loc[2]
    tot[3] = slab
    along = []
    order = (8, 7, 9, 6, 10, 5, 11, 4, 12, 3, 13, 2, 14, 1, 15)
    for k in order:
        along.append(send(tot.at[3], tot_z.at[k - 1], tz_s.at[k - 1], tz_r.at[k - 1], at_z(k)))
    for cp in along:
        cp.wait()
    totals = slab
    for k in range(15):
        totals = totals + tot_z[k]

    weight = tot[6]
    row_scale = scale_factor * weight / totals
    label_grad = weight * (tot[1] / totals - 1.0) * tot[2]
    tot[4] = row_scale
    tot[5] = label_grad

    def second_pass(base, n):
        base = pl.multiple_of(base, 16)
        rows = pl.ds(base, n)
        for q in range(4):
            lanes = slice(q * Q, (q + 1) * Q)
            is_target = class_iota[:n] == lab_ref[:, lanes] - (first_class + base)
            grad = jnp.where(is_target, tot[5, :, lanes], e[q, rows, :] * tot[4, :, lanes])
            g[rows, lanes] = grad.astype(BF)
        part[rows, :] = jnp.dot(
            g[rows, :], u[...].reshape(R, D), preferred_element_type=F32
        ).astype(BF)

    def rows_of(ref, start, n):
        return ref.at[pl.ds(pl.multiple_of(start, 16), n)]

    def value(ref, start, n):
        return ref[pl.ds(pl.multiple_of(start, 16), n), :].astype(F32)

    def a_rows(k):
        return ((x + k) % 4) * (2 * NA)

    other = FIRST_B + (1 - yh) * (4 * NB)
    mine = FIRST_B + yh * (4 * NB)
    to_left, to_right = at_x(3), at_x(1)

    second_pass(a_rows(2), 2 * NA)
    far_r = send(rows_of(part, a_rows(2), NA), fw.at[0], rs_s.at[0], rs_r.at[0], to_right)
    far_l = send(rows_of(part, a_rows(2) + NA, NA), fw.at[1], rs_s.at[1], rs_r.at[1], to_left)
    second_pass(other, 2 * NB)
    rs_b = [send(rows_of(part, other, 2 * NB), rb.at[0], rs_s.at[2], rs_r.at[2], y_peer)]
    second_pass(a_rows(1), 2 * NA)
    rs_a = [send(rows_of(part, a_rows(1) + NA, NA), ra.at[0, 1], rs_s.at[3], rs_r.at[3], to_right)]
    second_pass(a_rows(3), 2 * NA)
    rs_a.append(send(rows_of(part, a_rows(3), NA), ra.at[1, 0], rs_s.at[4], rs_r.at[4], to_left))
    second_pass(other + 2 * NB, 2 * NB)
    rs_b.append(send(rows_of(part, other + 2 * NB, 2 * NB), rb.at[1], rs_s.at[5], rs_r.at[5], y_peer))
    second_pass(a_rows(0), 2 * NA)
    second_pass(mine, 2 * NB)
    second_pass(mine + 2 * NB, 2 * NB)

    def emb_product(cc, yy):
        q = cc * 2 + yy
        lanes = pl.ds(pl.multiple_of(q * Q, Q), Q)
        ed[cc, yy] = lax.dot_general(
            g[:, lanes], unit[...], (((0,), (0,)), ((), ())), preferred_element_type=F32
        ).astype(BF)

    emb_product(1 - c, 0)
    emb_product(1 - c, 1)
    em1 = send(ed.at[1 - c], r1, em_s.at[0], em_r.at[0], core_peer)

    far_r.wait()
    both[0] = (value(part, a_rows(1), NA) + fw[0].astype(F32)).astype(BF)
    rs_a.append(send(both.at[0], ra.at[0, 0], rs_s.at[6], rs_r.at[6], to_right))
    far_l.wait()
    both[1] = (value(part, a_rows(3) + NA, NA) + fw[1].astype(F32)).astype(BF)
    rs_a.append(send(both.at[1], ra.at[1, 1], rs_s.at[7], rs_r.at[7], to_left))
    emb_product(c, 0)
    emb_product(c, 1)

    def to_x_owner(k):
        slot = jnp.where(k == 0, 1, k) - 1
        return pltpu.make_async_remote_copy(
            src_ref=sb.at[(x + k) % 4], dst_ref=rb2.at[slot],
            send_sem=rs_s.at[9 + slot], recv_sem=rs_r.at[9 + slot],
            device_id=at_x(k), device_id_type=MESH,
        )

    def half_b(half):
        rs_b[half].wait()
        sum_b = value(part, mine + half * (2 * NB), 2 * NB) + rb[half].astype(F32)
        sb[2 * half : 2 * half + 2] = sum_b.astype(BF).reshape(2, NB, D)
        for place in (2 * half, 2 * half + 1):

            @pl.when(x != place)
            def _():
                to_x_owner((place + 4 - x) % 4).start()

    half_b(0)
    em1.wait()
    f1[...] = (ed[c].astype(F32) + r1[...].astype(F32)).astype(BF).reshape(2, 4, 64, D)
    em2 = []
    for i, k in enumerate((2, 1, 15)):
        for yy in range(2):
            at = 1 + i * 2 + yy
            em2.append(send(f1.at[yy, (zl + k) % 4], r2.at[i, yy], em_s.at[at], em_r.at[at], at_z(k)))
    for cp in rs_a:
        cp.wait()
    sum_a = value(part, a_rows(0), 2 * NA)
    for side in range(2):
        sum_a = sum_a + ra[side].reshape(2 * NA, D).astype(F32)
    sa[...] = sum_a.astype(BF).reshape(2, NA, D)
    rs2 = [send(sa.at[1 - yh], ra2, rs_s.at[8], rs_r.at[8], y_peer)]
    half_b(1)
    rs2 += [to_x_owner(k) for k in (2, 1, 3)]

    serial = [12]

    def pass_on(start, n, where):
        at = serial[0]
        serial[0] += 1
        rows = rows_of(out, start, n)
        return send(rows, rows, rs_s.at[at], rs_r.at[at], where)

    def a_start(k, half):
        return a_rows(k) + half * NA

    def b_start(k, half):
        return FIRST_B + half * (4 * NB) + ((x + k) % 4) * NB

    mine_a, mine_b = a_start(0, yh), b_start(0, yh)
    inv_b, unit_b = unit_rows(value(proto, mine_b, NB))
    inv_a, unit_a = unit_rows(value(proto, mine_a, NA))
    for cp in rs2:
        cp.wait()
    dir_b = value(sb.at[x], 0, NB)
    for k in range(3):
        dir_b = dir_b + rb2[k].astype(F32)
    out[pl.ds(pl.multiple_of(mine_b, 16), NB), :] = finish_rows(dir_b, unit_b, inv_b)
    b_near = [pass_on(mine_b, NB, to_right), pass_on(mine_b, NB, to_left)]
    rest = [pass_on(mine_b, NB, y_peer)]
    dir_a = sa[yh].astype(F32) + ra2[...].astype(F32)
    out[pl.ds(pl.multiple_of(mine_a, 16), NA), :] = finish_rows(dir_a, unit_a, inv_a)
    a_cross = pass_on(mine_a, NA, y_peer)
    a_near = [pass_on(mine_a, NA, to_right), pass_on(mine_a, NA, to_left)]

    for cp in em2:
        cp.wait()
    f2[...] = (
        f1[:, zl].astype(F32) + r2[0].astype(F32) + r2[1].astype(F32) + r2[2].astype(F32)
    ).astype(BF)
    em3 = []
    for i, k in enumerate((8, 4, 12)):
        to = pl.ds(pl.multiple_of(((zh + k // 4) % 4) * 16, 16), 16)
        for yy in range(2):
            at = 7 + i * 2 + yy
            em3.append(send(f2.at[yy, to], r3.at[i, yy], em_s.at[at], em_r.at[at], at_z(k)))

    b_cut, a_cut = 64, 80
    b_near[0].wait()
    b_far = [pass_on(b_start(3, yh), b_cut, to_right)]
    rest.append(pass_on(b_start(3, yh), NB, y_peer))
    b_near[1].wait()
    b_far.append(pass_on(b_start(1, yh) + b_cut, NB - b_cut, to_left))
    rest.append(pass_on(b_start(1, yh), NB, y_peer))
    a_cross.wait()
    c_near = [pass_on(a_start(0, 1 - yh), NA, to_right), pass_on(a_start(0, 1 - yh), NA, to_left)]
    a_near[0].wait()
    rest.append(pass_on(a_start(3, yh), a_cut, to_right))
    a_near[1].wait()
    rest.append(pass_on(a_start(1, yh) + a_cut, NA - a_cut, to_left))
    b_far[0].wait()
    rest.append(pass_on(b_start(2, yh), b_cut, y_peer))
    b_far[1].wait()
    rest.append(pass_on(b_start(2, yh) + b_cut, NB - b_cut, y_peer))
    for cp in em3:
        cp.wait()
    own3 = pl.ds(pl.multiple_of(zh * 16, 16), 16)
    f3[...] = (
        f2[:, own3].astype(F32) + r3[0].astype(F32) + r3[1].astype(F32) + r3[2].astype(F32)
    ).astype(BF)
    em4 = send(f3.at[1 - y], r4, em_s.at[13], em_r.at[13], ylo_peer)
    c_near[0].wait()
    rest.append(pass_on(a_start(3, 1 - yh), a_cut, to_right))
    c_near[1].wait()
    rest.append(pass_on(a_start(1, 1 - yh) + a_cut, NA - a_cut, to_left))

    em4.wait()
    emb_dir = f3[y].astype(F32) + r4[...].astype(F32)
    emb_inv, emb_unit = unit_rows(emb_ref[...])
    emb_out[...] = finish_rows(emb_dir, emb_unit, emb_inv)

    for cp in rest:
        cp.wait()


def write_out(emb_grad, proto_grad, emb_out, proto_out, emb_sem, proto_sem):
    copies = [
        pltpu.make_async_copy(proto_grad, proto_out, proto_sem),
        pltpu.make_async_copy(emb_grad, emb_out, emb_sem),
    ]
    for cp in copies:
        cp.start()
    for cp in copies:
        cp.wait()


def on_device(embeddings, labels, row_weight, prototypes):
    vmem = pl.BlockSpec(memory_space=pltpu.VMEM)
    anywhere = pl.BlockSpec(memory_space=pl.ANY)
    dma = pltpu.SemaphoreType.DMA
    grads = pl.pallas_call(
        kernel,
        out_shape=(
            pltpu.VMEM((16, D), BF),
            pltpu.VMEM((C, D), BF),
        ),
        in_specs=[anywhere] * 4,
        out_specs=(vmem, vmem),
        scratch_shapes=[
            pltpu.VMEM((16, D), BF),
            pltpu.VMEM((8, 128), jnp.int32),
            pltpu.VMEM((8, 128), F32),
            pltpu.VMEM((C, D), BF),
            pltpu.VMEM((C, D), BF),
            pltpu.VMEM((2, 2, 4, 64, D), BF),
            pltpu.VMEM((4, C, Q), F32),
            pltpu.VMEM((C, R), BF),
            pltpu.VMEM((C, D), BF),
            pltpu.VMEM((1, R), jnp.int32),
            pltpu.VMEM((7, 1, R), F32),
            pltpu.VMEM((3, 1, R), F32),
            pltpu.VMEM((15, 1, R), F32),
            pltpu.VMEM((2, NA, D), BF),
            pltpu.VMEM((2, NA, D), BF),
            pltpu.VMEM((2, 2, NA, D), BF),
            pltpu.VMEM((2, 2 * NB, D), BF),
            pltpu.VMEM((NA, D), BF),
            pltpu.VMEM((3, NB, D), BF),
            pltpu.VMEM((2, NA, D), BF),
            pltpu.VMEM((4, NB, D), BF),
            pltpu.VMEM((2, 2, Q, D), BF),
            pltpu.VMEM((2, Q, D), BF),
            pltpu.VMEM((2, 4, 64, D), BF),
            pltpu.VMEM((3, 2, 64, D), BF),
            pltpu.VMEM((2, 64, D), BF),
            pltpu.VMEM((3, 2, 16, D), BF),
            pltpu.VMEM((2, 16, D), BF),
            pltpu.VMEM((16, D), BF),
            dma((4,)),
            dma((18,)), dma((18,)),
            dma((3,)), dma((3,)),
            dma((15,)), dma((15,)),
            dma((30,)), dma((30,)),
            dma((14,)), dma((14,)),
        ],
        compiler_params=pltpu.CompilerParams(
            collective_id=0, has_side_effects=True, vmem_limit_bytes=56 * 2**20
        ),
        name="margin_softmax_backward",
    )(embeddings, labels.reshape(8, 128), row_weight.reshape(8, 128), prototypes)
    return pl.pallas_call(
        write_out,
        out_shape=(
            jax.ShapeDtypeStruct((16, D), BF),
            jax.ShapeDtypeStruct((C, D), BF),
        ),
        in_specs=[vmem, vmem],
        out_specs=(anywhere, anywhere),
        scratch_shapes=[dma, dma],
        name="write_out",
    )(*[pltpu.with_memory_space_constraint(grad, pltpu.VMEM) for grad in grads])


def solution(mesh):
    return jax.shard_map(
        on_device,
        mesh=mesh,
        in_specs=(P(("dp", "cls"), None), P("dp"), P("dp"), P("cls", None)),
        out_specs=(P(("dp", "cls"), None), P("cls", None)),
        check_vma=False,
    )
```

```python
import math

import jax
import jax.numpy as jnp
from jax import lax
from jax.experimental import pallas as pl
from jax.experimental.pallas import tpu as pltpu
from jax.sharding import PartitionSpec as P

scale_factor = 64.0
margin = 0.5
sine_floor = 0.04
norm_eps = 1e-06
log2e = 1.4426950408889634
MESH = pl.DeviceIdType.MESH
F32 = jnp.float32
BF = jnp.bfloat16

D = 512
C = 2048
R = 1024
Q = 256
NA = 144
NB = 112
FIRST_B = 8 * NA
CH = 256


def unit_rows(values):
    wide = values.astype(F32)
    inverse = lax.rsqrt(jnp.sum(wide * wide, axis=1, keepdims=True) + norm_eps)
    return (inverse, wide * inverse)


def finish_rows(direction, unit_part, inverse):
    return (
        inverse * (direction - unit_part * jnp.sum(unit_part * direction, axis=1, keepdims=True))
    ).astype(BF)


def order_rows(labels, weights, lab_ref, tot):
    pieces = [(labels >> 12), (labels >> 6) & 63, labels & 63]
    pieces = [piece.astype(F32) for piece in pieces]
    rest = weights
    for _ in range(3):
        top = rest.astype(BF).astype(F32)
        pieces.append(top)
        rest = rest - top
    stacked = jnp.concatenate(pieces, axis=0).astype(BF)
    lane = lax.broadcasted_iota(jnp.int32, (128, 512), 0)
    to = lax.broadcasted_iota(jnp.int32, (128, 512), 1)
    from_lane = ((to >> 6) & 1) * 64 + ((to >> 7) & 1) * 32 + (to >> 8) * 16 + (to & 15)
    move = jnp.where(lane == from_lane, 1.0, 0.0).astype(BF)
    moved = jnp.dot(stacked, move, preferred_element_type=F32)
    row = lax.broadcasted_iota(jnp.int32, (8, 128), 0)
    z_high = (lax.broadcasted_iota(jnp.int32, (8, 128), 1) >> 4) & 3
    for tile in range(8):
        keep = row == z_high * 2 + tile % 2
        cut = moved[:, tile // 2 * 128 : (tile // 2 + 1) * 128]
        got = [
            jnp.sum(jnp.where(keep, cut[8 * i : 8 * i + 8], 0.0), axis=0, keepdims=True)
            for i in range(6)
        ]
        lanes = slice(tile * 128, (tile + 1) * 128)
        lab_ref[:, lanes] = (got[0] * 4096.0 + got[1] * 64.0 + got[2]).astype(jnp.int32)
        tot[6, :, lanes] = got[3] + got[4] + got[5]


def kernel(
    emb_hbm, lab_hbm, wgt_hbm, proto_hbm,
    emb_out, out,
    emb_ref, lab_in, wgt_in, proto, unit, u, e, g, part,
    lab_ref, tot, tot_loc, tot_z,
    fw, both, ra, rb, ra2, rb2, sa, sb,
    ed, r1, f1, r2, f2, r3, f3, r4,
    in_sems, core_sem,
    ag_s, ag_r, tl_s, tl_r, tz_s, tz_r, rs_s, rs_r, em_s, em_r,
):
    dp = lax.axis_index("dp")
    cls = lax.axis_index("cls")
    yh, x = dp // 4, dp % 4
    z, y, c = cls // 4, (cls // 2) % 2, cls % 2
    zh, zl = z // 4, z % 4

    def at_z(k):
        return (dp, ((z + k) % 16) * 4 + y * 2 + c)

    def at_local(dy, dc):
        yy = (y + dy) % 2
        cc = (c + dc) % 2
        return (dp, z * 4 + yy * 2 + cc)

    def at_x(k):
        return (yh * 4 + (x + k) % 4, cls)

    y_peer = ((1 - yh) * 4 + x, cls)
    core_peer = at_local(0, 1)
    ylo_peer = at_local(1, 0)

    def copy_to(src, dst, ssem, rsem, where):
        return pltpu.make_async_remote_copy(
            src_ref=src, dst_ref=dst, send_sem=ssem, recv_sem=rsem,
            device_id=where, device_id_type=MESH,
        )

    def send(*args):
        cp = copy_to(*args)
        cp.start()
        return cp

    barrier = pltpu.get_barrier_semaphore()
    friends = [at_z(k) for k in (8, 4, 12, 7, 9, 6, 10, 5, 11, 3, 13, 2, 14, 1, 15)]
    friends += [ylo_peer, at_x(1), at_x(2), at_x(3), y_peer]
    partners = [core_peer, at_local(1, 1)]
    for friend in friends:
        pl.semaphore_signal(barrier, inc=1, device_id=friend, device_id_type=MESH)

    @pl.when(c == 0)
    def _():
        for partner in partners:
            pl.semaphore_signal(barrier, inc=1, device_id=partner, device_id_type=MESH)

    sources = ((emb_hbm, emb_ref), (lab_hbm, lab_in), (wgt_hbm, wgt_in), (proto_hbm, proto))
    loads = [pltpu.make_async_copy(src, dst, in_sems.at[i]) for i, (src, dst) in enumerate(sources)]
    for load in loads:
        load.start()
    loads[0].wait()
    emb_inv, emb_unit = unit_rows(emb_ref[...])
    u[c, y, zl, pl.ds(pl.multiple_of(zh * 16, 16), 16), :] = emb_unit.astype(BF)

    @pl.when(c == 0)
    def _():
        pl.semaphore_wait(barrier, len(friends))

    @pl.when(c == 1)
    def _():
        pl.semaphore_wait(barrier, len(friends) + len(partners))
        for partner in partners:
            pl.semaphore_signal(core_sem, inc=1, device_id=partner, device_id_type=MESH)


    sends = []
    own_block = u.at[c, y, zl, pl.ds(pl.multiple_of(zh * 16, 16), 16)]
    p1 = [send(own_block, own_block, ag_s.at[i], ag_r.at[i], at_z(k)) for i, k in enumerate((8, 4, 12))]

    for load in loads[1:]:
        load.wait()

    def normalize(i, carry):
        rows = pl.ds(pl.multiple_of(i * CH, CH), CH)
        unit[rows, :] = unit_rows(proto[rows, :])[1].astype(BF)
        return carry

    lax.fori_loop(0, C // CH // 2, normalize, 0)
    for cp in p1:
        cp.wait()
    own_set = u.at[c, y, zl]
    p2 = [send(own_set, own_set, ag_s.at[3 + i], ag_r.at[3 + i], at_z(k)) for i, k in enumerate((1, 15, 2))]
    lax.fori_loop(C // CH // 2, C // CH, normalize, 0)
    order_rows(lab_in[...], wgt_in[...], lab_ref, tot)
    toy = [send(own_set, own_set, ag_s.at[6], ag_r.at[6], ylo_peer)]
    for i, k in enumerate((1, 15, 2)):
        p2[i].wait()
        got = u.at[c, y, (zl + 16 - k) % 4]
        toy.append(send(got, got, ag_s.at[7 + i], ag_r.at[7 + i], ylo_peer))

    class_iota = lax.broadcasted_iota(jnp.int32, (C, Q), 0)
    first_class = cls * C

    def first_pass(cc, yy):
        q = cc * 2 + yy
        lanes = pl.ds(pl.multiple_of(q * Q, Q), Q)
        labels = lab_ref[:, lanes] - first_class
        rows_u = u[cc, yy].reshape(Q, D)

        cosine = lax.dot_general(
            unit[...], rows_u, (((1,), (1,)), ((), ())), preferred_element_type=F32
        )
        is_target = class_iota == labels
        ex = jnp.where(is_target, 0.0, jnp.exp2(cosine * (scale_factor * log2e)))
        e[q] = ex
        total = jnp.sum(ex, axis=0, keepdims=True)
        target_cos = jnp.sum(jnp.where(is_target, cosine, 0.0), axis=0, keepdims=True)
        here = (labels >= 0) & (labels < C)
        sine = jnp.sqrt(jnp.maximum(1.0 - target_cos * target_cos, sine_floor))
        target_logit = scale_factor * (target_cos * math.cos(margin) - sine * math.sin(margin))
        target_exp = jnp.exp(target_logit)
        tot[0, :, lanes] = total + jnp.where(here, target_exp, 0.0)
        bound_free = 1.0 - target_cos * target_cos > sine_floor
        slope = scale_factor * (
            math.cos(margin) + jnp.where(bound_free, math.sin(margin) * target_cos / sine, 0.0)
        )
        tot[1, :, lanes] = target_exp
        tot[2, :, lanes] = slope

    @pl.when(c == 0)
    def _():
        pl.semaphore_wait(core_sem, len(partners))

    toc = send(u.at[c, y], u.at[c, y], ag_s.at[10], ag_r.at[10], core_peer)
    tod = []
    for i, k in enumerate((0, 1, 15, 2)):
        got = u.at[c, 1 - y, (zl + 16 - k) % 4]
        tod.append(copy_to(got, got, ag_s.at[14 + i], ag_r.at[14 + i], core_peer))

    def other_core_here():
        toc.wait_recv()
        for cp in tod:
            cp.wait_recv()

    def core_0_rows(i, carry):
        first_pass(0, i)
        return carry

    @pl.when(c == 1)
    def _():
        other_core_here()
        lax.fori_loop(0, 2, core_0_rows, 0)

    for i in range(4):
        toy[i].wait()
        tod[i].start()

    @pl.when(c == 0)
    def _():
        lax.fori_loop(0, 2, core_0_rows, 0)
        toc.wait_recv()

    first_pass(1, y)

    @pl.when(c == 0)
    def _():
        for cp in tod:
            cp.wait_recv()

    first_pass(1, 1 - y)
    for cp in [toc] + tod:
        cp.wait_send()

    loc = []
    for i, (dy, dc) in enumerate(((1, 0), (0, 1), (1, 1))):
        loc.append(send(tot.at[0], tot_loc.at[i], tl_s.at[i], tl_r.at[i], at_local(dy, dc)))
    for cp in loc:
        cp.wait()
    slab = tot[0] + tot_loc[0] + tot_loc[1] + tot_loc[2]
    tot[3] = slab
    along = []
    order = (8, 7, 9, 6, 10, 5, 11, 4, 12, 3, 13, 2, 14, 1, 15)
    for k in order:
        along.append(send(tot.at[3], tot_z.at[k - 1], tz_s.at[k - 1], tz_r.at[k - 1], at_z(k)))
    for cp in along:
        cp.wait()
    totals = slab
    for k in range(15):
        totals = totals + tot_z[k]

    weight = tot[6]
    row_scale = scale_factor * weight / totals
    label_grad = weight * (tot[1] / totals - 1.0) * tot[2]
    tot[4] = row_scale
    tot[5] = label_grad

    def second_pass(base, n):
        base = pl.multiple_of(base, 16)
        rows = pl.ds(base, n)
        for q in range(4):
            lanes = slice(q * Q, (q + 1) * Q)
            is_target = class_iota[:n] == lab_ref[:, lanes] - (first_class + base)
            grad = jnp.where(is_target, tot[5, :, lanes], e[q, rows, :] * tot[4, :, lanes])
            g[rows, lanes] = grad.astype(BF)
        part[rows, :] = jnp.dot(
            g[rows, :], u[...].reshape(R, D), preferred_element_type=F32
        ).astype(BF)

    def rows_of(ref, start, n):
        return ref.at[pl.ds(pl.multiple_of(start, 16), n)]

    def value(ref, start, n):
        return ref[pl.ds(pl.multiple_of(start, 16), n), :].astype(F32)

    def a_rows(k):
        return ((x + k) % 4) * (2 * NA)

    other = FIRST_B + (1 - yh) * (4 * NB)
    mine = FIRST_B + yh * (4 * NB)
    to_left, to_right = at_x(3), at_x(1)

    second_pass(a_rows(2), 2 * NA)
    far_r = send(rows_of(part, a_rows(2), NA), fw.at[0], rs_s.at[0], rs_r.at[0], to_right)
    far_l = send(rows_of(part, a_rows(2) + NA, NA), fw.at[1], rs_s.at[1], rs_r.at[1], to_left)
    second_pass(other, 2 * NB)
    rs_b = [send(rows_of(part, other, 2 * NB), rb.at[0], rs_s.at[2], rs_r.at[2], y_peer)]
    second_pass(a_rows(1), 2 * NA)
    rs_a = [send(rows_of(part, a_rows(1) + NA, NA), ra.at[0, 1], rs_s.at[3], rs_r.at[3], to_right)]
    second_pass(a_rows(3), 2 * NA)
    rs_a.append(send(rows_of(part, a_rows(3), NA), ra.at[1, 0], rs_s.at[4], rs_r.at[4], to_left))
    second_pass(other + 2 * NB, 2 * NB)
    rs_b.append(send(rows_of(part, other + 2 * NB, 2 * NB), rb.at[1], rs_s.at[5], rs_r.at[5], y_peer))
    second_pass(a_rows(0), 2 * NA)
    second_pass(mine, 2 * NB)
    second_pass(mine + 2 * NB, 2 * NB)

    def emb_product(cc, yy):
        q = cc * 2 + yy
        lanes = pl.ds(pl.multiple_of(q * Q, Q), Q)
        ed[cc, yy] = lax.dot_general(
            g[:, lanes], unit[...], (((0,), (0,)), ((), ())), preferred_element_type=F32
        ).astype(BF)

    emb_product(1 - c, 0)
    emb_product(1 - c, 1)
    em1 = send(ed.at[1 - c], r1, em_s.at[0], em_r.at[0], core_peer)

    far_r.wait()
    both[0] = (value(part, a_rows(1), NA) + fw[0].astype(F32)).astype(BF)
    rs_a.append(send(both.at[0], ra.at[0, 0], rs_s.at[6], rs_r.at[6], to_right))
    far_l.wait()
    both[1] = (value(part, a_rows(3) + NA, NA) + fw[1].astype(F32)).astype(BF)
    rs_a.append(send(both.at[1], ra.at[1, 1], rs_s.at[7], rs_r.at[7], to_left))
    emb_product(c, 0)
    emb_product(c, 1)

    def to_x_owner(k):
        slot = jnp.where(k == 0, 1, k) - 1
        return pltpu.make_async_remote_copy(
            src_ref=sb.at[(x + k) % 4], dst_ref=rb2.at[slot],
            send_sem=rs_s.at[9 + slot], recv_sem=rs_r.at[9 + slot],
            device_id=at_x(k), device_id_type=MESH,
        )

    def half_b(half):
        rs_b[half].wait()
        sum_b = value(part, mine + half * (2 * NB), 2 * NB) + rb[half].astype(F32)
        sb[2 * half : 2 * half + 2] = sum_b.astype(BF).reshape(2, NB, D)
        for place in (2 * half, 2 * half + 1):

            @pl.when(x != place)
            def _():
                to_x_owner((place + 4 - x) % 4).start()

    half_b(0)
    em1.wait()
    f1[...] = (ed[c].astype(F32) + r1[...].astype(F32)).astype(BF).reshape(2, 4, 64, D)
    em2 = []
    for i, k in enumerate((2, 1, 15)):
        for yy in range(2):
            at = 1 + i * 2 + yy
            em2.append(send(f1.at[yy, (zl + k) % 4], r2.at[i, yy], em_s.at[at], em_r.at[at], at_z(k)))
    for cp in rs_a:
        cp.wait()
    sum_a = value(part, a_rows(0), 2 * NA)
    for side in range(2):
        sum_a = sum_a + ra[side].reshape(2 * NA, D).astype(F32)
    sa[...] = sum_a.astype(BF).reshape(2, NA, D)
    rs2 = [send(sa.at[1 - yh], ra2, rs_s.at[8], rs_r.at[8], y_peer)]
    half_b(1)
    rs2 += [to_x_owner(k) for k in (2, 1, 3)]

    serial = [12]

    def pass_on(start, n, where):
        at = serial[0]
        serial[0] += 1
        rows = rows_of(out, start, n)
        return send(rows, rows, rs_s.at[at], rs_r.at[at], where)

    def a_start(k, half):
        return a_rows(k) + half * NA

    def b_start(k, half):
        return FIRST_B + half * (4 * NB) + ((x + k) % 4) * NB

    mine_a, mine_b = a_start(0, yh), b_start(0, yh)
    inv_b, unit_b = unit_rows(value(proto, mine_b, NB))
    inv_a, unit_a = unit_rows(value(proto, mine_a, NA))
    for cp in rs2:
        cp.wait()
    dir_b = value(sb.at[x], 0, NB)
    for k in range(3):
        dir_b = dir_b + rb2[k].astype(F32)
    out[pl.ds(pl.multiple_of(mine_b, 16), NB), :] = finish_rows(dir_b, unit_b, inv_b)
    b_near = [pass_on(mine_b, NB, to_right), pass_on(mine_b, NB, to_left)]
    rest = [pass_on(mine_b, NB, y_peer)]
    dir_a = sa[yh].astype(F32) + ra2[...].astype(F32)
    out[pl.ds(pl.multiple_of(mine_a, 16), NA), :] = finish_rows(dir_a, unit_a, inv_a)
    a_cross = pass_on(mine_a, NA, y_peer)
    a_near = [pass_on(mine_a, NA, to_right), pass_on(mine_a, NA, to_left)]

    for cp in em2:
        cp.wait()
    f2[...] = (
        f1[:, zl].astype(F32) + r2[0].astype(F32) + r2[1].astype(F32) + r2[2].astype(F32)
    ).astype(BF)
    em3 = []
    for i, k in enumerate((8, 4, 12)):
        to = pl.ds(pl.multiple_of(((zh + k // 4) % 4) * 16, 16), 16)
        for yy in range(2):
            at = 7 + i * 2 + yy
            em3.append(send(f2.at[yy, to], r3.at[i, yy], em_s.at[at], em_r.at[at], at_z(k)))

    b_cut, a_cut = 64, 80
    b_near[0].wait()
    b_far = [pass_on(b_start(3, yh), b_cut, to_right)]
    rest.append(pass_on(b_start(3, yh), NB, y_peer))
    b_near[1].wait()
    b_far.append(pass_on(b_start(1, yh) + b_cut, NB - b_cut, to_left))
    rest.append(pass_on(b_start(1, yh), NB, y_peer))
    a_cross.wait()
    c_near = [pass_on(a_start(0, 1 - yh), NA, to_right), pass_on(a_start(0, 1 - yh), NA, to_left)]
    a_near[0].wait()
    rest.append(pass_on(a_start(3, yh), a_cut, to_right))
    a_near[1].wait()
    rest.append(pass_on(a_start(1, yh) + a_cut, NA - a_cut, to_left))
    b_far[0].wait()
    rest.append(pass_on(b_start(2, yh), b_cut, y_peer))
    b_far[1].wait()
    rest.append(pass_on(b_start(2, yh) + b_cut, NB - b_cut, y_peer))
    for cp in em3:
        cp.wait()
    own3 = pl.ds(pl.multiple_of(zh * 16, 16), 16)
    f3[...] = (
        f2[:, own3].astype(F32) + r3[0].astype(F32) + r3[1].astype(F32) + r3[2].astype(F32)
    ).astype(BF)
    em4 = send(f3.at[1 - y], r4, em_s.at[13], em_r.at[13], ylo_peer)
    c_near[0].wait()
    rest.append(pass_on(a_start(3, 1 - yh), a_cut, to_right))
    c_near[1].wait()
    rest.append(pass_on(a_start(1, 1 - yh) + a_cut, NA - a_cut, to_left))

    em4.wait()
    emb_dir = f3[y].astype(F32) + r4[...].astype(F32)
    emb_inv, emb_unit = unit_rows(emb_ref[...])
    emb_out[...] = finish_rows(emb_dir, emb_unit, emb_inv)

    for cp in rest:
        cp.wait()


def write_out(emb_grad, proto_grad, emb_out, proto_out, emb_sem, proto_sem):
    copies = [
        pltpu.make_async_copy(proto_grad, proto_out, proto_sem),
        pltpu.make_async_copy(emb_grad, emb_out, emb_sem),
    ]
    for cp in copies:
        cp.start()
    for cp in copies:
        cp.wait()


def on_device(embeddings, labels, row_weight, prototypes):
    vmem = pl.BlockSpec(memory_space=pltpu.VMEM)
    anywhere = pl.BlockSpec(memory_space=pl.ANY)
    dma = pltpu.SemaphoreType.DMA
    grads = pl.pallas_call(
        kernel,
        out_shape=(
            pltpu.VMEM((16, D), BF),
            pltpu.VMEM((C, D), BF),
        ),
        in_specs=[anywhere] * 4,
        out_specs=(vmem, vmem),
        scratch_shapes=[
            pltpu.VMEM((16, D), BF),
            pltpu.VMEM((8, 128), jnp.int32),
            pltpu.VMEM((8, 128), F32),
            pltpu.VMEM((C, D), BF),
            pltpu.VMEM((C, D), BF),
            pltpu.VMEM((2, 2, 4, 64, D), BF),
            pltpu.VMEM((4, C, Q), F32),
            pltpu.VMEM((C, R), BF),
            pltpu.VMEM((C, D), BF),
            pltpu.VMEM((1, R), jnp.int32),
            pltpu.VMEM((7, 1, R), F32),
            pltpu.VMEM((3, 1, R), F32),
            pltpu.VMEM((15, 1, R), F32),
            pltpu.VMEM((2, NA, D), BF),
            pltpu.VMEM((2, NA, D), BF),
            pltpu.VMEM((2, 2, NA, D), BF),
            pltpu.VMEM((2, 2 * NB, D), BF),
            pltpu.VMEM((NA, D), BF),
            pltpu.VMEM((3, NB, D), BF),
            pltpu.VMEM((2, NA, D), BF),
            pltpu.VMEM((4, NB, D), BF),
            pltpu.VMEM((2, 2, Q, D), BF),
            pltpu.VMEM((2, Q, D), BF),
            pltpu.VMEM((2, 4, 64, D), BF),
            pltpu.VMEM((3, 2, 64, D), BF),
            pltpu.VMEM((2, 64, D), BF),
            pltpu.VMEM((3, 2, 16, D), BF),
            pltpu.VMEM((2, 16, D), BF),
            pltpu.VMEM((16, D), BF),
            dma((4,)), pltpu.SemaphoreType.REGULAR,
            dma((18,)), dma((18,)),
            dma((3,)), dma((3,)),
            dma((15,)), dma((15,)),
            dma((30,)), dma((30,)),
            dma((14,)), dma((14,)),
        ],
        compiler_params=pltpu.CompilerParams(
            collective_id=0, has_side_effects=True, vmem_limit_bytes=56 * 2**20
        ),
        name="margin_softmax_backward",
    )(embeddings, labels.reshape(8, 128), row_weight.reshape(8, 128), prototypes)
    return pl.pallas_call(
        write_out,
        out_shape=(
            jax.ShapeDtypeStruct((16, D), BF),
            jax.ShapeDtypeStruct((C, D), BF),
        ),
        in_specs=[vmem, vmem],
        out_specs=(anywhere, anywhere),
        scratch_shapes=[dma, dma],
        name="write_out",
    )(*[pltpu.with_memory_space_constraint(grad, pltpu.VMEM) for grad in grads])


def solution(mesh):
    return jax.shard_map(
        on_device,
        mesh=mesh,
        in_specs=(P(("dp", "cls"), None), P("dp"), P("dp"), P("cls", None)),
        out_specs=(P(("dp", "cls"), None), P("cls", None)),
        check_vma=False,
    )
```

```python
import math

import jax
import jax.numpy as jnp
from jax import lax
from jax.experimental import pallas as pl
from jax.experimental.pallas import tpu as pltpu
from jax.sharding import PartitionSpec as P

scale_factor = 64.0
margin = 0.5
sine_floor = 0.04
norm_eps = 1e-06
log2e = 1.4426950408889634
MESH = pl.DeviceIdType.MESH
F32 = jnp.float32
BF = jnp.bfloat16

D = 512
C = 2048
R = 1024
Q = 256
NA = 144
NB = 112
FIRST_B = 8 * NA
CH = 256


def unit_rows(values):
    wide = values.astype(F32)
    inverse = lax.rsqrt(jnp.sum(wide * wide, axis=1, keepdims=True) + norm_eps)
    return (inverse, wide * inverse)


def finish_rows(direction, unit_part, inverse):
    return (
        inverse * (direction - unit_part * jnp.sum(unit_part * direction, axis=1, keepdims=True))
    ).astype(BF)


def order_rows(labels, weights, lab_ref, tot):
    pieces = [(labels >> 12), (labels >> 6) & 63, labels & 63]
    pieces = [piece.astype(F32) for piece in pieces]
    rest = weights
    for _ in range(3):
        top = rest.astype(BF).astype(F32)
        pieces.append(top)
        rest = rest - top
    stacked = jnp.concatenate(pieces, axis=0).astype(BF)
    lane = lax.broadcasted_iota(jnp.int32, (128, 512), 0)
    to = lax.broadcasted_iota(jnp.int32, (128, 512), 1)
    from_lane = ((to >> 6) & 1) * 64 + ((to >> 7) & 1) * 32 + (to >> 8) * 16 + (to & 15)
    move = jnp.where(lane == from_lane, 1.0, 0.0).astype(BF)
    moved = jnp.dot(stacked, move, preferred_element_type=F32)
    row = lax.broadcasted_iota(jnp.int32, (8, 128), 0)
    z_high = (lax.broadcasted_iota(jnp.int32, (8, 128), 1) >> 4) & 3
    for tile in range(8):
        keep = row == z_high * 2 + tile % 2
        cut = moved[:, tile // 2 * 128 : (tile // 2 + 1) * 128]
        got = [
            jnp.sum(jnp.where(keep, cut[8 * i : 8 * i + 8], 0.0), axis=0, keepdims=True)
            for i in range(6)
        ]
        lanes = slice(tile * 128, (tile + 1) * 128)
        lab_ref[:, lanes] = (got[0] * 4096.0 + got[1] * 64.0 + got[2]).astype(jnp.int32)
        tot[6, :, lanes] = got[3] + got[4] + got[5]


def kernel(
    emb_hbm, lab_hbm, wgt_hbm, proto_hbm,
    emb_out, out,
    emb_ref, lab_in, wgt_in, proto, unit, u, e, g, part,
    lab_ref, tot, tot_far, tot_near,
    fw, both, ra, rb, ra2, rb2, sa, sb,
    ed, r1, f1, r2, f2, r3, f3, r4,
    in_sems,
    ag_s, ag_r, tf_s, tf_r, tn_s, tn_r, rs_s, rs_r, em_s, em_r,
):
    dp = lax.axis_index("dp")
    cls = lax.axis_index("cls")
    yh, x = dp // 4, dp % 4
    z, y, c = cls // 4, (cls // 2) % 2, cls % 2
    zh, zl = z // 4, z % 4

    def at_z(k):
        return (dp, ((z + k) % 16) * 4 + y * 2 + c)

    def near(k, dy, dc):
        yy = (y + dy) % 2
        cc = (c + dc) % 2
        return (dp, ((z + k) % 16) * 4 + yy * 2 + cc)

    def at_x(k):
        return (yh * 4 + (x + k) % 4, cls)

    y_peer = ((1 - yh) * 4 + x, cls)
    core_peer = near(0, 0, 1)
    ylo_peer = near(0, 1, 0)
    places = [(k, dy, dc) for k in (2, 1, 15, 0) for dy, dc in ((1, 1), (1, 0), (0, 1), (0, 0))][:-1]

    def send(src, dst, ssem, rsem, where):
        cp = pltpu.make_async_remote_copy(
            src_ref=src, dst_ref=dst, send_sem=ssem, recv_sem=rsem,
            device_id=where, device_id_type=MESH,
        )
        cp.start()
        return cp

    barrier = pltpu.get_barrier_semaphore()
    friends = [at_z(k) for k in (8, 4, 12)] + [near(*place) for place in places]
    friends += [at_x(1), at_x(2), at_x(3), y_peer]
    for friend in friends:
        pl.semaphore_signal(barrier, inc=1, device_id=friend, device_id_type=MESH)
    sources = ((emb_hbm, emb_ref), (lab_hbm, lab_in), (wgt_hbm, wgt_in), (proto_hbm, proto))
    loads = [pltpu.make_async_copy(src, dst, in_sems.at[i]) for i, (src, dst) in enumerate(sources)]
    for load in loads:
        load.start()
    loads[0].wait()
    emb_inv, emb_unit = unit_rows(emb_ref[...])
    u[c, y, zl, pl.ds(pl.multiple_of(zh * 16, 16), 16), :] = emb_unit.astype(BF)
    pl.semaphore_wait(barrier, len(friends))

    sends = []
    own_block = u.at[c, y, zl, pl.ds(pl.multiple_of(zh * 16, 16), 16)]
    p1 = [send(own_block, own_block, ag_s.at[i], ag_r.at[i], at_z(k)) for i, k in enumerate((8, 4, 12))]

    for load in loads[1:]:
        load.wait()

    def normalize(i, carry):
        rows = pl.ds(pl.multiple_of(i * CH, CH), CH)
        unit[rows, :] = unit_rows(proto[rows, :])[1].astype(BF)
        return carry

    lax.fori_loop(0, C // CH // 2, normalize, 0)
    for cp in p1:
        cp.wait()
    own_set = u.at[c, y, zl]
    p2 = [send(own_set, own_set, ag_s.at[3 + i], ag_r.at[3 + i], at_z(k)) for i, k in enumerate((1, 15, 2))]
    lax.fori_loop(C // CH // 2, C // CH, normalize, 0)
    order_rows(lab_in[...], wgt_in[...], lab_ref, tot)
    toy = [send(own_set, own_set, ag_s.at[6], ag_r.at[6], ylo_peer)]
    toc = [send(own_set, own_set, ag_s.at[10], ag_r.at[10], core_peer)]
    for i, k in enumerate((1, 15, 2)):
        p2[i].wait()
        got = u.at[c, y, (zl + 16 - k) % 4]
        toy.append(send(got, got, ag_s.at[7 + i], ag_r.at[7 + i], ylo_peer))
        toc.append(send(got, got, ag_s.at[11 + i], ag_r.at[11 + i], core_peer))

    class_iota = lax.broadcasted_iota(jnp.int32, (C, Q), 0)
    first_class = cls * C

    def first_pass(cc, yy):
        q = cc * 2 + yy
        lanes = pl.ds(pl.multiple_of(q * Q, Q), Q)
        labels = lab_ref[:, lanes] - first_class
        rows_u = u[cc, yy].reshape(Q, D)

        cosine = lax.dot_general(
            unit[...], rows_u, (((1,), (1,)), ((), ())), preferred_element_type=F32
        )
        is_target = class_iota == labels
        ex = jnp.where(is_target, 0.0, jnp.exp2(cosine * (scale_factor * log2e)))
        e[q] = ex
        total = jnp.sum(ex, axis=0, keepdims=True)
        target_cos = jnp.sum(jnp.where(is_target, cosine, 0.0), axis=0, keepdims=True)
        here = (labels >= 0) & (labels < C)
        sine = jnp.sqrt(jnp.maximum(1.0 - target_cos * target_cos, sine_floor))
        target_logit = scale_factor * (target_cos * math.cos(margin) - sine * math.sin(margin))
        target_exp = jnp.exp(target_logit)
        tot[0, :, lanes] = total + jnp.where(here, target_exp, 0.0)
        bound_free = 1.0 - target_cos * target_cos > sine_floor
        slope = scale_factor * (
            math.cos(margin) + jnp.where(bound_free, math.sin(margin) * target_cos / sine, 0.0)
        )
        tot[1, :, lanes] = target_exp
        tot[2, :, lanes] = slope

    first_pass(c, y)
    for cp in toc:
        cp.wait()
    first_pass(1 - c, y)
    tod = []
    for i, k in enumerate((0, 1, 15, 2)):
        toy[i].wait()
        got = u.at[c, 1 - y, (zl + 16 - k) % 4]
        tod.append(send(got, got, ag_s.at[14 + i], ag_r.at[14 + i], core_peer))
    first_pass(c, 1 - y)
    for cp in tod:
        cp.wait()
    first_pass(1 - c, 1 - y)

    apart = []
    for i, k in enumerate((8, 4, 12)):
        apart.append(send(tot.at[0], tot_far.at[i], tf_s.at[i], tf_r.at[i], at_z(k)))
    for cp in apart:
        cp.wait()
    tot[3] = tot[0] + tot_far[0] + tot_far[1] + tot_far[2]
    around = []
    for i, place in enumerate(places):
        around.append(send(tot.at[3], tot_near.at[i], tn_s.at[i], tn_r.at[i], near(*place)))
    for cp in around:
        cp.wait()
    totals = tot[3]
    for i in range(15):
        totals = totals + tot_near[i]

    weight = tot[6]
    row_scale = scale_factor * weight / totals
    label_grad = weight * (tot[1] / totals - 1.0) * tot[2]
    tot[4] = row_scale
    tot[5] = label_grad

    def second_pass(base, n):
        base = pl.multiple_of(base, 16)
        rows = pl.ds(base, n)
        for q in range(4):
            lanes = slice(q * Q, (q + 1) * Q)
            is_target = class_iota[:n] == lab_ref[:, lanes] - (first_class + base)
            grad = jnp.where(is_target, tot[5, :, lanes], e[q, rows, :] * tot[4, :, lanes])
            g[rows, lanes] = grad.astype(BF)
        part[rows, :] = jnp.dot(
            g[rows, :], u[...].reshape(R, D), preferred_element_type=F32
        ).astype(BF)

    def rows_of(ref, start, n):
        return ref.at[pl.ds(pl.multiple_of(start, 16), n)]

    def value(ref, start, n):
        return ref[pl.ds(pl.multiple_of(start, 16), n), :].astype(F32)

    def a_rows(k):
        return ((x + k) % 4) * (2 * NA)

    other = FIRST_B + (1 - yh) * (4 * NB)
    mine = FIRST_B + yh * (4 * NB)
    to_left, to_right = at_x(3), at_x(1)

    second_pass(other, 2 * NB)
    rs_b = [send(rows_of(part, other, 2 * NB), rb.at[0], rs_s.at[2], rs_r.at[2], y_peer)]
    second_pass(a_rows(2), 2 * NA)
    far_r = send(rows_of(part, a_rows(2), NA), fw.at[0], rs_s.at[0], rs_r.at[0], to_right)
    far_l = send(rows_of(part, a_rows(2) + NA, NA), fw.at[1], rs_s.at[1], rs_r.at[1], to_left)
    second_pass(a_rows(1), 2 * NA)
    rs_a = [send(rows_of(part, a_rows(1) + NA, NA), ra.at[0, 1], rs_s.at[3], rs_r.at[3], to_right)]
    second_pass(a_rows(3), 2 * NA)
    rs_a.append(send(rows_of(part, a_rows(3), NA), ra.at[1, 0], rs_s.at[4], rs_r.at[4], to_left))
    second_pass(other + 2 * NB, 2 * NB)
    rs_b.append(send(rows_of(part, other + 2 * NB, 2 * NB), rb.at[1], rs_s.at[5], rs_r.at[5], y_peer))
    second_pass(a_rows(0), 2 * NA)
    second_pass(mine, 2 * NB)
    second_pass(mine + 2 * NB, 2 * NB)

    def emb_product(cc, yy):
        q = cc * 2 + yy
        lanes = pl.ds(pl.multiple_of(q * Q, Q), Q)
        ed[cc, yy] = lax.dot_general(
            g[:, lanes], unit[...], (((0,), (0,)), ((), ())), preferred_element_type=F32
        ).astype(BF)

    emb_product(1 - c, 0)
    emb_product(1 - c, 1)
    em1 = send(ed.at[1 - c], r1, em_s.at[0], em_r.at[0], core_peer)

    far_r.wait()
    both[0] = (value(part, a_rows(1), NA) + fw[0].astype(F32)).astype(BF)
    rs_a.append(send(both.at[0], ra.at[0, 0], rs_s.at[6], rs_r.at[6], to_right))
    far_l.wait()
    both[1] = (value(part, a_rows(3) + NA, NA) + fw[1].astype(F32)).astype(BF)
    rs_a.append(send(both.at[1], ra.at[1, 1], rs_s.at[7], rs_r.at[7], to_left))
    emb_product(c, 0)
    emb_product(c, 1)

    def to_x_owner(k):
        slot = jnp.where(k == 0, 1, k) - 1
        return pltpu.make_async_remote_copy(
            src_ref=sb.at[(x + k) % 4], dst_ref=rb2.at[slot],
            send_sem=rs_s.at[9 + slot], recv_sem=rs_r.at[9 + slot],
            device_id=at_x(k), device_id_type=MESH,
        )

    def half_b(half):
        rs_b[half].wait()
        sum_b = value(part, mine + half * (2 * NB), 2 * NB) + rb[half].astype(F32)
        sb[2 * half : 2 * half + 2] = sum_b.astype(BF).reshape(2, NB, D)
        for place in (2 * half, 2 * half + 1):

            @pl.when(x != place)
            def _():
                to_x_owner((place + 4 - x) % 4).start()

    half_b(0)
    em1.wait()
    f1[...] = (ed[c].astype(F32) + r1[...].astype(F32)).astype(BF).reshape(2, 4, 64, D)
    em2 = []
    for i, k in enumerate((2, 1, 15)):
        for yy in range(2):
            at = 1 + i * 2 + yy
            em2.append(send(f1.at[yy, (zl + k) % 4], r2.at[i, yy], em_s.at[at], em_r.at[at], at_z(k)))
    for cp in rs_a:
        cp.wait()
    sum_a = value(part, a_rows(0), 2 * NA)
    for side in range(2):
        sum_a = sum_a + ra[side].reshape(2 * NA, D).astype(F32)
    sa[...] = sum_a.astype(BF).reshape(2, NA, D)
    rs2 = [send(sa.at[1 - yh], ra2, rs_s.at[8], rs_r.at[8], y_peer)]
    half_b(1)
    rs2 += [to_x_owner(k) for k in (2, 1, 3)]

    serial = [12]

    def pass_on(start, n, where):
        at = serial[0]
        serial[0] += 1
        rows = rows_of(out, start, n)
        return send(rows, rows, rs_s.at[at], rs_r.at[at], where)

    def a_start(k, half):
        return a_rows(k) + half * NA

    def b_start(k, half):
        return FIRST_B + half * (4 * NB) + ((x + k) % 4) * NB

    mine_a, mine_b = a_start(0, yh), b_start(0, yh)
    inv_b, unit_b = unit_rows(value(proto, mine_b, NB))
    inv_a, unit_a = unit_rows(value(proto, mine_a, NA))
    rs2[0].wait()
    dir_a = sa[yh].astype(F32) + ra2[...].astype(F32)
    out[pl.ds(pl.multiple_of(mine_a, 16), NA), :] = finish_rows(dir_a, unit_a, inv_a)
    a_cross = pass_on(mine_a, NA, y_peer)
    for cp in rs2[1:]:
        cp.wait()
    dir_b = value(sb.at[x], 0, NB)
    for k in range(3):
        dir_b = dir_b + rb2[k].astype(F32)
    out[pl.ds(pl.multiple_of(mine_b, 16), NB), :] = finish_rows(dir_b, unit_b, inv_b)
    b_near = [pass_on(mine_b, NB, to_right), pass_on(mine_b, NB, to_left)]
    a_near = [pass_on(mine_a, NA, to_right), pass_on(mine_a, NA, to_left)]
    rest = [pass_on(mine_b, NB, y_peer)]

    for cp in em2:
        cp.wait()
    f2[...] = (
        f1[:, zl].astype(F32) + r2[0].astype(F32) + r2[1].astype(F32) + r2[2].astype(F32)
    ).astype(BF)
    em3 = []
    for i, k in enumerate((8, 4, 12)):
        to = pl.ds(pl.multiple_of(((zh + k // 4) % 4) * 16, 16), 16)
        for yy in range(2):
            at = 7 + i * 2 + yy
            em3.append(send(f2.at[yy, to], r3.at[i, yy], em_s.at[at], em_r.at[at], at_z(k)))

    b_cut, a_cut = 64, 80
    b_near[0].wait()
    b_far = [pass_on(b_start(3, yh), b_cut, to_right)]
    rest.append(pass_on(b_start(3, yh), NB, y_peer))
    b_near[1].wait()
    b_far.append(pass_on(b_start(1, yh) + b_cut, NB - b_cut, to_left))
    rest.append(pass_on(b_start(1, yh), NB, y_peer))
    a_cross.wait()
    c_near = [pass_on(a_start(0, 1 - yh), NA, to_right), pass_on(a_start(0, 1 - yh), NA, to_left)]
    a_near[0].wait()
    rest.append(pass_on(a_start(3, yh), a_cut, to_right))
    a_near[1].wait()
    rest.append(pass_on(a_start(1, yh) + a_cut, NA - a_cut, to_left))
    b_far[0].wait()
    rest.append(pass_on(b_start(2, yh), b_cut, y_peer))
    b_far[1].wait()
    rest.append(pass_on(b_start(2, yh) + b_cut, NB - b_cut, y_peer))
    for cp in em3:
        cp.wait()
    own3 = pl.ds(pl.multiple_of(zh * 16, 16), 16)
    f3[...] = (
        f2[:, own3].astype(F32) + r3[0].astype(F32) + r3[1].astype(F32) + r3[2].astype(F32)
    ).astype(BF)
    em4 = send(f3.at[1 - y], r4, em_s.at[13], em_r.at[13], ylo_peer)
    c_near[0].wait()
    rest.append(pass_on(a_start(3, 1 - yh), a_cut, to_right))
    c_near[1].wait()
    rest.append(pass_on(a_start(1, 1 - yh) + a_cut, NA - a_cut, to_left))

    em4.wait()
    emb_dir = f3[y].astype(F32) + r4[...].astype(F32)
    emb_inv, emb_unit = unit_rows(emb_ref[...])
    emb_out[...] = finish_rows(emb_dir, emb_unit, emb_inv)

    for cp in rest:
        cp.wait()


def write_out(emb_grad, proto_grad, emb_out, proto_out, emb_sem, proto_sem):
    copies = [
        pltpu.make_async_copy(proto_grad, proto_out, proto_sem),
        pltpu.make_async_copy(emb_grad, emb_out, emb_sem),
    ]
    for cp in copies:
        cp.start()
    for cp in copies:
        cp.wait()


def on_device(embeddings, labels, row_weight, prototypes):
    vmem = pl.BlockSpec(memory_space=pltpu.VMEM)
    anywhere = pl.BlockSpec(memory_space=pl.ANY)
    dma = pltpu.SemaphoreType.DMA
    grads = pl.pallas_call(
        kernel,
        out_shape=(
            pltpu.VMEM((16, D), BF),
            pltpu.VMEM((C, D), BF),
        ),
        in_specs=[anywhere] * 4,
        out_specs=(vmem, vmem),
        scratch_shapes=[
            pltpu.VMEM((16, D), BF),
            pltpu.VMEM((8, 128), jnp.int32),
            pltpu.VMEM((8, 128), F32),
            pltpu.VMEM((C, D), BF),
            pltpu.VMEM((C, D), BF),
            pltpu.VMEM((2, 2, 4, 64, D), BF),
            pltpu.VMEM((4, C, Q), F32),
            pltpu.VMEM((C, R), BF),
            pltpu.VMEM((C, D), BF),
            pltpu.VMEM((1, R), jnp.int32),
            pltpu.VMEM((7, 1, R), F32),
            pltpu.VMEM((3, 1, R), F32),
            pltpu.VMEM((15, 1, R), F32),
            pltpu.VMEM((2, NA, D), BF),
            pltpu.VMEM((2, NA, D), BF),
            pltpu.VMEM((2, 2, NA, D), BF),
            pltpu.VMEM((2, 2 * NB, D), BF),
            pltpu.VMEM((NA, D), BF),
            pltpu.VMEM((3, NB, D), BF),
            pltpu.VMEM((2, NA, D), BF),
            pltpu.VMEM((4, NB, D), BF),
            pltpu.VMEM((2, 2, Q, D), BF),
            pltpu.VMEM((2, Q, D), BF),
            pltpu.VMEM((2, 4, 64, D), BF),
            pltpu.VMEM((3, 2, 64, D), BF),
            pltpu.VMEM((2, 64, D), BF),
            pltpu.VMEM((3, 2, 16, D), BF),
            pltpu.VMEM((2, 16, D), BF),
            pltpu.VMEM((16, D), BF),
            dma((4,)),
            dma((18,)), dma((18,)),
            dma((3,)), dma((3,)),
            dma((15,)), dma((15,)),
            dma((30,)), dma((30,)),
            dma((14,)), dma((14,)),
        ],
        compiler_params=pltpu.CompilerParams(
            collective_id=0, has_side_effects=True, vmem_limit_bytes=56 * 2**20
        ),
        name="margin_softmax_backward",
    )(embeddings, labels.reshape(8, 128), row_weight.reshape(8, 128), prototypes)
    return pl.pallas_call(
        write_out,
        out_shape=(
            jax.ShapeDtypeStruct((16, D), BF),
            jax.ShapeDtypeStruct((C, D), BF),
        ),
        in_specs=[vmem, vmem],
        out_specs=(anywhere, anywhere),
        scratch_shapes=[dma, dma],
        name="write_out",
    )(*[pltpu.with_memory_space_constraint(grad, pltpu.VMEM) for grad in grads])


def solution(mesh):
    return jax.shard_map(
        on_device,
        mesh=mesh,
        in_specs=(P(("dp", "cls"), None), P("dp"), P("dp"), P("cls", None)),
        out_specs=(P(("dp", "cls"), None), P("cls", None)),
        check_vma=False,
    )
```

```python
import math

import jax
import jax.numpy as jnp
from jax import lax
from jax.experimental import pallas as pl
from jax.experimental.pallas import tpu as pltpu
from jax.sharding import PartitionSpec as P

scale_factor = 64.0
margin = 0.5
sine_floor = 0.04
norm_eps = 1e-06
log2e = 1.4426950408889634
MESH = pl.DeviceIdType.MESH
F32 = jnp.float32
BF = jnp.bfloat16

D = 512
C = 2048
R = 1024
Q = 256
NA = 144
NB = (64, 48)
FIRST_B = (8 * NA, 8 * (NA + NB[0]))
CH = 256


def unit_rows(values):
    wide = values.astype(F32)
    inverse = lax.rsqrt(jnp.sum(wide * wide, axis=1, keepdims=True) + norm_eps)
    return (inverse, wide * inverse)


def finish_rows(direction, unit_part, inverse):
    return (
        inverse * (direction - unit_part * jnp.sum(unit_part * direction, axis=1, keepdims=True))
    ).astype(BF)


def order_rows(labels, weights, lab_ref, tot):
    pieces = [(labels >> 12), (labels >> 6) & 63, labels & 63]
    pieces = [piece.astype(F32) for piece in pieces]
    rest = weights
    for _ in range(3):
        top = rest.astype(BF).astype(F32)
        pieces.append(top)
        rest = rest - top
    stacked = jnp.concatenate(pieces, axis=0).astype(BF)
    lane = lax.broadcasted_iota(jnp.int32, (128, 512), 0)
    to = lax.broadcasted_iota(jnp.int32, (128, 512), 1)
    from_lane = ((to >> 6) & 1) * 64 + ((to >> 7) & 1) * 32 + (to >> 8) * 16 + (to & 15)
    move = jnp.where(lane == from_lane, 1.0, 0.0).astype(BF)
    moved = jnp.dot(stacked, move, preferred_element_type=F32)
    row = lax.broadcasted_iota(jnp.int32, (8, 128), 0)
    z_high = (lax.broadcasted_iota(jnp.int32, (8, 128), 1) >> 4) & 3
    for tile in range(8):
        keep = row == z_high * 2 + tile % 2
        cut = moved[:, tile // 2 * 128 : (tile // 2 + 1) * 128]
        got = [
            jnp.sum(jnp.where(keep, cut[8 * i : 8 * i + 8], 0.0), axis=0, keepdims=True)
            for i in range(6)
        ]
        lanes = slice(tile * 128, (tile + 1) * 128)
        lab_ref[:, lanes] = (got[0] * 4096.0 + got[1] * 64.0 + got[2]).astype(jnp.int32)
        tot[6, :, lanes] = got[3] + got[4] + got[5]


def kernel(
    emb_hbm, lab_hbm, wgt_hbm, proto_hbm,
    emb_out, out,
    emb_ref, lab_in, wgt_in, proto, unit, u, e, g, part,
    lab_ref, tot, tot_far, tot_near,
    fw, both, ra, ra2, sa, rb0, rb1, sb0, sb1, rx0, rx1,
    ed, r1, f1, r2, f2, r3, f3, r4,
    in_sems,
    ag_s, ag_r, tf_s, tf_r, tn_s, tn_r, rs_s, rs_r, em_s, em_r,
):
    rb, sb, rx = (rb0, rb1), (sb0, sb1), (rx0, rx1)
    dp = lax.axis_index("dp")
    cls = lax.axis_index("cls")
    yh, x = dp // 4, dp % 4
    z, y, c = cls // 4, (cls // 2) % 2, cls % 2
    zh, zl = z // 4, z % 4

    def at_z(k):
        return (dp, ((z + k) % 16) * 4 + y * 2 + c)

    def near(k, dy, dc):
        yy = (y + dy) % 2
        cc = (c + dc) % 2
        return (dp, ((z + k) % 16) * 4 + yy * 2 + cc)

    def at_x(k):
        return (yh * 4 + (x + k) % 4, cls)

    y_peer = ((1 - yh) * 4 + x, cls)
    core_peer = near(0, 0, 1)
    ylo_peer = near(0, 1, 0)
    places = [(k, dy, dc) for k in (2, 1, 15, 0) for dy, dc in ((1, 1), (1, 0), (0, 1), (0, 0))][:-1]

    def send(src, dst, ssem, rsem, where):
        cp = pltpu.make_async_remote_copy(
            src_ref=src, dst_ref=dst, send_sem=ssem, recv_sem=rsem,
            device_id=where, device_id_type=MESH,
        )
        cp.start()
        return cp

    barrier = pltpu.get_barrier_semaphore()
    friends = [at_z(k) for k in (8, 4, 12)] + [near(*place) for place in places]
    friends += [at_x(1), at_x(2), at_x(3), y_peer]
    for friend in friends:
        pl.semaphore_signal(barrier, inc=1, device_id=friend, device_id_type=MESH)
    sources = ((emb_hbm, emb_ref), (lab_hbm, lab_in), (wgt_hbm, wgt_in), (proto_hbm, proto))
    loads = [pltpu.make_async_copy(src, dst, in_sems.at[i]) for i, (src, dst) in enumerate(sources)]
    for load in loads:
        load.start()
    loads[0].wait()
    emb_inv, emb_unit = unit_rows(emb_ref[...])
    u[c, y, zl, pl.ds(pl.multiple_of(zh * 16, 16), 16), :] = emb_unit.astype(BF)
    pl.semaphore_wait(barrier, len(friends))

    sends = []
    own_block = u.at[c, y, zl, pl.ds(pl.multiple_of(zh * 16, 16), 16)]
    p1 = [send(own_block, own_block, ag_s.at[i], ag_r.at[i], at_z(k)) for i, k in enumerate((8, 4, 12))]

    for load in loads[1:]:
        load.wait()

    def normalize(i, carry):
        rows = pl.ds(pl.multiple_of(i * CH, CH), CH)
        unit[rows, :] = unit_rows(proto[rows, :])[1].astype(BF)
        return carry

    lax.fori_loop(0, C // CH // 2, normalize, 0)
    for cp in p1:
        cp.wait()
    own_set = u.at[c, y, zl]
    p2 = [send(own_set, own_set, ag_s.at[3 + i], ag_r.at[3 + i], at_z(k)) for i, k in enumerate((1, 15, 2))]
    lax.fori_loop(C // CH // 2, C // CH, normalize, 0)
    order_rows(lab_in[...], wgt_in[...], lab_ref, tot)
    toy = [send(own_set, own_set, ag_s.at[6], ag_r.at[6], ylo_peer)]
    toc = [send(own_set, own_set, ag_s.at[10], ag_r.at[10], core_peer)]
    for i, k in enumerate((1, 15, 2)):
        p2[i].wait()
        got = u.at[c, y, (zl + 16 - k) % 4]
        toy.append(send(got, got, ag_s.at[7 + i], ag_r.at[7 + i], ylo_peer))
        toc.append(send(got, got, ag_s.at[11 + i], ag_r.at[11 + i], core_peer))

    class_iota = lax.broadcasted_iota(jnp.int32, (C, Q), 0)
    first_class = cls * C

    def first_pass(cc, yy):
        q = cc * 2 + yy
        lanes = pl.ds(pl.multiple_of(q * Q, Q), Q)
        labels = lab_ref[:, lanes] - first_class
        rows_u = u[cc, yy].reshape(Q, D)

        cosine = lax.dot_general(
            unit[...], rows_u, (((1,), (1,)), ((), ())), preferred_element_type=F32
        )
        is_target = class_iota == labels
        ex = jnp.where(is_target, 0.0, jnp.exp2(cosine * (scale_factor * log2e)))
        e[q] = ex
        total = jnp.sum(ex, axis=0, keepdims=True)
        target_cos = jnp.sum(jnp.where(is_target, cosine, 0.0), axis=0, keepdims=True)
        here = (labels >= 0) & (labels < C)
        sine = jnp.sqrt(jnp.maximum(1.0 - target_cos * target_cos, sine_floor))
        target_logit = scale_factor * (target_cos * math.cos(margin) - sine * math.sin(margin))
        target_exp = jnp.exp(target_logit)
        tot[0, :, lanes] = total + jnp.where(here, target_exp, 0.0)
        bound_free = 1.0 - target_cos * target_cos > sine_floor
        slope = scale_factor * (
            math.cos(margin) + jnp.where(bound_free, math.sin(margin) * target_cos / sine, 0.0)
        )
        tot[1, :, lanes] = target_exp
        tot[2, :, lanes] = slope

    first_pass(c, y)
    for cp in toc:
        cp.wait()
    first_pass(1 - c, y)
    tod = []
    for i, k in enumerate((0, 1, 15, 2)):
        toy[i].wait()
        got = u.at[c, 1 - y, (zl + 16 - k) % 4]
        tod.append(send(got, got, ag_s.at[14 + i], ag_r.at[14 + i], core_peer))
    first_pass(c, 1 - y)
    for cp in tod:
        cp.wait()
    first_pass(1 - c, 1 - y)

    apart = []
    for i, k in enumerate((8, 4, 12)):
        apart.append(send(tot.at[0], tot_far.at[i], tf_s.at[i], tf_r.at[i], at_z(k)))
    for cp in apart:
        cp.wait()
    tot[3] = tot[0] + tot_far[0] + tot_far[1] + tot_far[2]
    around = []
    for i, place in enumerate(places):
        around.append(send(tot.at[3], tot_near.at[i], tn_s.at[i], tn_r.at[i], near(*place)))
    for cp in around:
        cp.wait()
    totals = tot[3]
    for i in range(15):
        totals = totals + tot_near[i]

    weight = tot[6]
    row_scale = scale_factor * weight / totals
    label_grad = weight * (tot[1] / totals - 1.0) * tot[2]
    tot[4] = row_scale
    tot[5] = label_grad

    def second_pass(base, n):
        base = pl.multiple_of(base, 16)
        rows = pl.ds(base, n)
        for q in range(4):
            lanes = slice(q * Q, (q + 1) * Q)
            is_target = class_iota[:n] == lab_ref[:, lanes] - (first_class + base)
            grad = jnp.where(is_target, tot[5, :, lanes], e[q, rows, :] * tot[4, :, lanes])
            g[rows, lanes] = grad.astype(BF)
        part[rows, :] = jnp.dot(
            g[rows, :], u[...].reshape(R, D), preferred_element_type=F32
        ).astype(BF)

    def rows_of(ref, start, n):
        return ref.at[pl.ds(pl.multiple_of(start, 16), n)]

    def value(ref, start, n):
        return ref[pl.ds(pl.multiple_of(start, 16), n), :].astype(F32)

    def a_rows(k):
        return ((x + k) % 4) * (2 * NA)

    def b_rows(lot, half, k=None):
        first = FIRST_B[lot] + half * (4 * NB[lot])
        return first if k is None else first + ((x + k) % 4) * NB[lot]

    to_left, to_right = at_x(3), at_x(1)

    def send_b(lot):
        n = 4 * NB[lot]
        base = b_rows(lot, 1 - yh)
        second_pass(base, n)
        return send(rows_of(part, base, n), rb[lot], rs_s.at[2 + lot], rs_r.at[2 + lot], y_peer)

    rs_b = [send_b(0)]
    second_pass(a_rows(2), 2 * NA)
    far_r = send(rows_of(part, a_rows(2), NA), fw.at[0], rs_s.at[0], rs_r.at[0], to_right)
    far_l = send(rows_of(part, a_rows(2) + NA, NA), fw.at[1], rs_s.at[1], rs_r.at[1], to_left)
    second_pass(a_rows(1), 2 * NA)
    rs_a = [send(rows_of(part, a_rows(1) + NA, NA), ra.at[0, 1], rs_s.at[4], rs_r.at[4], to_right)]
    second_pass(a_rows(3), 2 * NA)
    rs_a.append(send(rows_of(part, a_rows(3), NA), ra.at[1, 0], rs_s.at[5], rs_r.at[5], to_left))
    rs_b.append(send_b(1))
    second_pass(a_rows(0), 2 * NA)
    for lot in range(2):
        second_pass(b_rows(lot, yh), 4 * NB[lot])

    def emb_product(cc, yy):
        q = cc * 2 + yy
        lanes = pl.ds(pl.multiple_of(q * Q, Q), Q)
        ed[cc, yy] = lax.dot_general(
            g[:, lanes], unit[...], (((0,), (0,)), ((), ())), preferred_element_type=F32
        ).astype(BF)

    emb_product(1 - c, 0)
    emb_product(1 - c, 1)
    em1 = send(ed.at[1 - c], r1, em_s.at[0], em_r.at[0], core_peer)

    far_r.wait()
    both[0] = (value(part, a_rows(1), NA) + fw[0].astype(F32)).astype(BF)
    rs_a.append(send(both.at[0], ra.at[0, 0], rs_s.at[6], rs_r.at[6], to_right))
    far_l.wait()
    both[1] = (value(part, a_rows(3) + NA, NA) + fw[1].astype(F32)).astype(BF)
    rs_a.append(send(both.at[1], ra.at[1, 1], rs_s.at[7], rs_r.at[7], to_left))
    emb_product(c, 0)
    emb_product(c, 1)

    def own_b(lot):
        n = NB[lot]
        rs_b[lot].wait()
        sum_b = value(part, b_rows(lot, yh), 4 * n) + rb[lot][...].astype(F32)
        sb[lot][...] = sum_b.astype(BF).reshape(4, n, D)
        sent = []
        for k in (2, 1, 3):
            at = 8 + 3 * lot + k
            sent.append(send(sb[lot].at[(x + k) % 4], rx[lot].at[k - 1], rs_s.at[at], rs_r.at[at], at_x(k)))
        return sent

    rs2_b = [own_b(0)]
    em1.wait()
    f1[...] = (ed[c].astype(F32) + r1[...].astype(F32)).astype(BF).reshape(2, 4, 64, D)
    em2 = []
    for i, k in enumerate((2, 1, 15)):
        for yy in range(2):
            at = 1 + i * 2 + yy
            em2.append(send(f1.at[yy, (zl + k) % 4], r2.at[i, yy], em_s.at[at], em_r.at[at], at_z(k)))
    for cp in rs_a:
        cp.wait()
    sum_a = value(part, a_rows(0), 2 * NA)
    for side in range(2):
        sum_a = sum_a + ra[side].reshape(2 * NA, D).astype(F32)
    sa[...] = sum_a.astype(BF).reshape(2, NA, D)
    rs2_a = send(sa.at[1 - yh], ra2, rs_s.at[8], rs_r.at[8], y_peer)
    rs2_b.append(own_b(1))

    serial = [15]
    rest = []

    def pass_on(start, n, where):
        at = serial[0]
        serial[0] += 1
        rows = rows_of(out, start, n)
        return send(rows, rows, rs_s.at[at], rs_r.at[at], where)

    def a_start(k, half):
        return a_rows(k) + half * NA

    def store(start, n, direction):
        inverse, unit_part = unit_rows(value(proto, start, n))
        out[pl.ds(pl.multiple_of(start, 16), n), :] = finish_rows(direction, unit_part, inverse)

    def finish_b(lot):
        for cp in rs2_b[lot]:
            cp.wait()
        direction = value(sb[lot].at[x], 0, NB[lot])
        for k in range(3):
            direction = direction + rx[lot][k].astype(F32)
        start = b_rows(lot, yh, 0)
        store(start, NB[lot], direction)
        near_b = [pass_on(start, NB[lot], to_right), pass_on(start, NB[lot], to_left)]
        rest.append(pass_on(start, NB[lot], y_peer))
        return near_b

    b_near = [finish_b(0)]
    rs2_a.wait()
    mine_a = a_start(0, yh)
    store(mine_a, NA, sa[yh].astype(F32) + ra2[...].astype(F32))
    a_cross = pass_on(mine_a, NA, y_peer)
    b_near.append(finish_b(1))
    a_near = [pass_on(mine_a, NA, to_right), pass_on(mine_a, NA, to_left)]

    for cp in em2:
        cp.wait()
    f2[...] = (
        f1[:, zl].astype(F32) + r2[0].astype(F32) + r2[1].astype(F32) + r2[2].astype(F32)
    ).astype(BF)
    em3 = []
    for i, k in enumerate((8, 4, 12)):
        to = pl.ds(pl.multiple_of(((zh + k // 4) % 4) * 16, 16), 16)
        for yy in range(2):
            at = 7 + i * 2 + yy
            em3.append(send(f2.at[yy, to], r3.at[i, yy], em_s.at[at], em_r.at[at], at_z(k)))

    b_cut, a_cut = 32, 80

    def hand_on_b(lot):
        n = NB[lot]
        b_near[lot][0].wait()
        left = b_rows(lot, yh, 3)
        far = [pass_on(left, b_cut, to_right)]
        rest.append(pass_on(left, n, y_peer))
        b_near[lot][1].wait()
        right = b_rows(lot, yh, 1)
        far.append(pass_on(right + b_cut, n - b_cut, to_left))
        rest.append(pass_on(right, n, y_peer))
        return far

    b_far = [hand_on_b(0), hand_on_b(1)]
    a_cross.wait()
    crossed = a_start(0, 1 - yh)
    c_near = [pass_on(crossed, a_cut, to_right), pass_on(crossed + a_cut, NA - a_cut, to_left)]
    rest.append(pass_on(crossed + a_cut, NA - a_cut, to_right))
    rest.append(pass_on(crossed, a_cut, to_left))
    a_near[0].wait()
    rest.append(pass_on(a_start(3, yh), a_cut, to_right))
    a_near[1].wait()
    rest.append(pass_on(a_start(1, yh) + a_cut, NA - a_cut, to_left))
    for lot in range(2):
        start = b_rows(lot, yh, 2)
        b_far[lot][0].wait()
        rest.append(pass_on(start, b_cut, y_peer))
        b_far[lot][1].wait()
        rest.append(pass_on(start + b_cut, NB[lot] - b_cut, y_peer))
    c_near[0].wait()
    rest.append(pass_on(a_start(3, 1 - yh), a_cut, to_right))
    c_near[1].wait()
    rest.append(pass_on(a_start(1, 1 - yh) + a_cut, NA - a_cut, to_left))

    for cp in em3:
        cp.wait()
    own3 = pl.ds(pl.multiple_of(zh * 16, 16), 16)
    f3[...] = (
        f2[:, own3].astype(F32) + r3[0].astype(F32) + r3[1].astype(F32) + r3[2].astype(F32)
    ).astype(BF)
    em4 = send(f3.at[1 - y], r4, em_s.at[13], em_r.at[13], ylo_peer)
    em4.wait()
    emb_dir = f3[y].astype(F32) + r4[...].astype(F32)
    emb_inv, emb_unit = unit_rows(emb_ref[...])
    emb_out[...] = finish_rows(emb_dir, emb_unit, emb_inv)

    for cp in rest:
        cp.wait()


def write_out(emb_grad, proto_grad, emb_out, proto_out, emb_sem, proto_sem):
    copies = [
        pltpu.make_async_copy(proto_grad, proto_out, proto_sem),
        pltpu.make_async_copy(emb_grad, emb_out, emb_sem),
    ]
    for cp in copies:
        cp.start()
    for cp in copies:
        cp.wait()


def on_device(embeddings, labels, row_weight, prototypes):
    vmem = pl.BlockSpec(memory_space=pltpu.VMEM)
    anywhere = pl.BlockSpec(memory_space=pl.ANY)
    dma = pltpu.SemaphoreType.DMA
    grads = pl.pallas_call(
        kernel,
        out_shape=(
            pltpu.VMEM((16, D), BF),
            pltpu.VMEM((C, D), BF),
        ),
        in_specs=[anywhere] * 4,
        out_specs=(vmem, vmem),
        scratch_shapes=[
            pltpu.VMEM((16, D), BF),
            pltpu.VMEM((8, 128), jnp.int32),
            pltpu.VMEM((8, 128), F32),
            pltpu.VMEM((C, D), BF),
            pltpu.VMEM((C, D), BF),
            pltpu.VMEM((2, 2, 4, 64, D), BF),
            pltpu.VMEM((4, C, Q), F32),
            pltpu.VMEM((C, R), BF),
            pltpu.VMEM((C, D), BF),
            pltpu.VMEM((1, R), jnp.int32),
            pltpu.VMEM((7, 1, R), F32),
            pltpu.VMEM((3, 1, R), F32),
            pltpu.VMEM((15, 1, R), F32),
            pltpu.VMEM((2, NA, D), BF),
            pltpu.VMEM((2, NA, D), BF),
            pltpu.VMEM((2, 2, NA, D), BF),
            pltpu.VMEM((NA, D), BF),
            pltpu.VMEM((2, NA, D), BF),
            *[pltpu.VMEM((4 * n, D), BF) for n in NB],
            *[pltpu.VMEM((4, n, D), BF) for n in NB],
            *[pltpu.VMEM((3, n, D), BF) for n in NB],
            pltpu.VMEM((2, 2, Q, D), BF),
            pltpu.VMEM((2, Q, D), BF),
            pltpu.VMEM((2, 4, 64, D), BF),
            pltpu.VMEM((3, 2, 64, D), BF),
            pltpu.VMEM((2, 64, D), BF),
            pltpu.VMEM((3, 2, 16, D), BF),
            pltpu.VMEM((2, 16, D), BF),
            pltpu.VMEM((16, D), BF),
            dma((4,)),
            dma((18,)), dma((18,)),
            dma((3,)), dma((3,)),
            dma((15,)), dma((15,)),
            dma((48,)), dma((48,)),
            dma((14,)), dma((14,)),
        ],
        compiler_params=pltpu.CompilerParams(
            collective_id=0, has_side_effects=True, vmem_limit_bytes=56 * 2**20
        ),
        name="margin_softmax_backward",
    )(embeddings, labels.reshape(8, 128), row_weight.reshape(8, 128), prototypes)
    return pl.pallas_call(
        write_out,
        out_shape=(
            jax.ShapeDtypeStruct((16, D), BF),
            jax.ShapeDtypeStruct((C, D), BF),
        ),
        in_specs=[vmem, vmem],
        out_specs=(anywhere, anywhere),
        scratch_shapes=[dma, dma],
        name="write_out",
    )(*[pltpu.with_memory_space_constraint(grad, pltpu.VMEM) for grad in grads])


def solution(mesh):
    return jax.shard_map(
        on_device,
        mesh=mesh,
        in_specs=(P(("dp", "cls"), None), P("dp"), P("dp"), P("cls", None)),
        out_specs=(P(("dp", "cls"), None), P("cls", None)),
        check_vma=False,
    )
```

```python
import math

import jax
import jax.numpy as jnp
from jax import lax
from jax.experimental import pallas as pl
from jax.experimental.pallas import tpu as pltpu
from jax.sharding import PartitionSpec as P

scale_factor = 64.0
margin = 0.5
sine_floor = 0.04
norm_eps = 1e-06
log2e = 1.4426950408889634
MESH = pl.DeviceIdType.MESH
F32 = jnp.float32
BF = jnp.bfloat16

D = 512
C = 2048
R = 1024
Q = 256
NA = 144
NB = (64, 48)
FIRST_B = (8 * NA, 8 * (NA + NB[0]))
CH = 256


def unit_rows(values):
    wide = values.astype(F32)
    inverse = lax.rsqrt(jnp.sum(wide * wide, axis=1, keepdims=True) + norm_eps)
    return (inverse, wide * inverse)


def finish_rows(direction, unit_part, inverse):
    return (
        inverse * (direction - unit_part * jnp.sum(unit_part * direction, axis=1, keepdims=True))
    ).astype(BF)


def order_rows(labels, weights, lab_ref, tot):
    pieces = [(labels >> 12), (labels >> 6) & 63, labels & 63]
    pieces = [piece.astype(F32) for piece in pieces]
    rest = weights
    for _ in range(3):
        top = rest.astype(BF).astype(F32)
        pieces.append(top)
        rest = rest - top
    stacked = jnp.concatenate(pieces, axis=0).astype(BF)
    lane = lax.broadcasted_iota(jnp.int32, (128, 512), 0)
    to = lax.broadcasted_iota(jnp.int32, (128, 512), 1)
    from_lane = ((to >> 6) & 1) * 64 + ((to >> 7) & 1) * 32 + (to >> 8) * 16 + (to & 15)
    move = jnp.where(lane == from_lane, 1.0, 0.0).astype(BF)
    moved = jnp.dot(stacked, move, preferred_element_type=F32)
    row = lax.broadcasted_iota(jnp.int32, (8, 128), 0)
    z_high = (lax.broadcasted_iota(jnp.int32, (8, 128), 1) >> 4) & 3
    for tile in range(8):
        keep = row == z_high * 2 + tile % 2
        cut = moved[:, tile // 2 * 128 : (tile // 2 + 1) * 128]
        got = [
            jnp.sum(jnp.where(keep, cut[8 * i : 8 * i + 8], 0.0), axis=0, keepdims=True)
            for i in range(6)
        ]
        lanes = slice(tile * 128, (tile + 1) * 128)
        lab_ref[:, lanes] = (got[0] * 4096.0 + got[1] * 64.0 + got[2]).astype(jnp.int32)
        tot[6, :, lanes] = got[3] + got[4] + got[5]


def kernel(
    emb_hbm, lab_hbm, wgt_hbm, proto_hbm,
    emb_out, out,
    emb_ref, lab_in, wgt_in, proto, unit, u, e, g, part,
    lab_ref, tot, tot_far, tot_near,
    fw, both, ra, ra2, sa, rb0, rb1, sb0, sb1, rx0, rx1,
    ed, r1, f1, r2, f2, r3, f3, r4,
    in_sems,
    ag_s, ag_r, tf_s, tf_r, tn_s, tn_r, rs_s, rs_r, em_s, em_r,
):
    rb, sb, rx = (rb0, rb1), (sb0, sb1), (rx0, rx1)
    dp = lax.axis_index("dp")
    cls = lax.axis_index("cls")
    yh, x = dp // 4, dp % 4
    z, y, c = cls // 4, (cls // 2) % 2, cls % 2
    zh, zl = z // 4, z % 4

    def at_z(k):
        return (dp, ((z + k) % 16) * 4 + y * 2 + c)

    def near(k, dy, dc):
        yy = (y + dy) % 2
        cc = (c + dc) % 2
        return (dp, ((z + k) % 16) * 4 + yy * 2 + cc)

    def at_x(k):
        return (yh * 4 + (x + k) % 4, cls)

    y_peer = ((1 - yh) * 4 + x, cls)
    core_peer = near(0, 0, 1)
    ylo_peer = near(0, 1, 0)
    places = [(k, dy, dc) for k in (2, 1, 15, 0) for dy, dc in ((1, 1), (1, 0), (0, 1), (0, 0))][:-1]

    def send(src, dst, ssem, rsem, where):
        cp = pltpu.make_async_remote_copy(
            src_ref=src, dst_ref=dst, send_sem=ssem, recv_sem=rsem,
            device_id=where, device_id_type=MESH,
        )
        cp.start()
        return cp

    barrier = pltpu.get_barrier_semaphore()
    friends = [at_z(k) for k in (8, 4, 12)] + [near(*place) for place in places]
    friends += [at_x(1), at_x(2), at_x(3), y_peer]
    for friend in friends:
        pl.semaphore_signal(barrier, inc=1, device_id=friend, device_id_type=MESH)
    sources = ((emb_hbm, emb_ref), (lab_hbm, lab_in), (wgt_hbm, wgt_in), (proto_hbm, proto))
    loads = [pltpu.make_async_copy(src, dst, in_sems.at[i]) for i, (src, dst) in enumerate(sources)]
    for load in loads:
        load.start()
    loads[0].wait()
    emb_inv, emb_unit = unit_rows(emb_ref[...])
    u[c, y, zl, pl.ds(pl.multiple_of(zh * 16, 16), 16), :] = emb_unit.astype(BF)
    pl.semaphore_wait(barrier, len(friends))

    sends = []
    own_block = u.at[c, y, zl, pl.ds(pl.multiple_of(zh * 16, 16), 16)]
    p1 = [send(own_block, own_block, ag_s.at[i], ag_r.at[i], at_z(k)) for i, k in enumerate((8, 4, 12))]

    for load in loads[1:]:
        load.wait()

    def normalize(i, carry):
        rows = pl.ds(pl.multiple_of(i * CH, CH), CH)
        unit[rows, :] = unit_rows(proto[rows, :])[1].astype(BF)
        return carry

    lax.fori_loop(0, C // CH // 2, normalize, 0)
    for cp in p1:
        cp.wait()
    own_set = u.at[c, y, zl]
    p2 = [send(own_set, own_set, ag_s.at[3 + i], ag_r.at[3 + i], at_z(k)) for i, k in enumerate((1, 15, 2))]
    toy = [send(own_set, own_set, ag_s.at[6], ag_r.at[6], ylo_peer)]
    toc = [send(own_set, own_set, ag_s.at[10], ag_r.at[10], core_peer)]
    lax.fori_loop(C // CH // 2, C // CH, normalize, 0)
    order_rows(lab_in[...], wgt_in[...], lab_ref, tot)
    toy[0].wait()
    beside = u.at[c, 1 - y, zl]
    over = send(beside, beside, ag_s.at[9], ag_r.at[9], at_z(2))
    tod = [send(beside, beside, ag_s.at[14], ag_r.at[14], core_peer)]
    for i, k in enumerate((1, 15, 2)):
        p2[i].wait()
        got = u.at[c, y, (zl + 16 - k) % 4]
        if k != 2:
            toy.append(send(got, got, ag_s.at[7 + i], ag_r.at[7 + i], ylo_peer))
        toc.append(send(got, got, ag_s.at[11 + i], ag_r.at[11 + i], core_peer))

    class_iota = lax.broadcasted_iota(jnp.int32, (C, Q), 0)
    first_class = cls * C

    def first_pass(cc, yy):
        q = cc * 2 + yy
        lanes = pl.ds(pl.multiple_of(q * Q, Q), Q)
        labels = lab_ref[:, lanes] - first_class
        rows_u = u[cc, yy].reshape(Q, D)

        cosine = lax.dot_general(
            unit[...], rows_u, (((1,), (1,)), ((), ())), preferred_element_type=F32
        )
        is_target = class_iota == labels
        ex = jnp.where(is_target, 0.0, jnp.exp2(cosine * (scale_factor * log2e)))
        e[q] = ex
        total = jnp.sum(ex, axis=0, keepdims=True)
        target_cos = jnp.sum(jnp.where(is_target, cosine, 0.0), axis=0, keepdims=True)
        here = (labels >= 0) & (labels < C)
        sine = jnp.sqrt(jnp.maximum(1.0 - target_cos * target_cos, sine_floor))
        target_logit = scale_factor * (target_cos * math.cos(margin) - sine * math.sin(margin))
        target_exp = jnp.exp(target_logit)
        tot[0, :, lanes] = total + jnp.where(here, target_exp, 0.0)
        bound_free = 1.0 - target_cos * target_cos > sine_floor
        slope = scale_factor * (
            math.cos(margin) + jnp.where(bound_free, math.sin(margin) * target_cos / sine, 0.0)
        )
        tot[1, :, lanes] = target_exp
        tot[2, :, lanes] = slope

    first_pass(c, y)
    for cp in toc:
        cp.wait()
    first_pass(1 - c, y)
    for i, (k, arrival) in enumerate(((1, toy[1]), (15, toy[2]), (2, over))):
        arrival.wait()
        got = u.at[c, 1 - y, (zl + 16 - k) % 4]
        tod.append(send(got, got, ag_s.at[15 + i], ag_r.at[15 + i], core_peer))
    first_pass(c, 1 - y)
    for cp in tod:
        cp.wait()
    first_pass(1 - c, 1 - y)

    apart = []
    for i, k in enumerate((8, 4, 12)):
        apart.append(send(tot.at[0], tot_far.at[i], tf_s.at[i], tf_r.at[i], at_z(k)))
    for cp in apart:
        cp.wait()
    tot[3] = tot[0] + tot_far[0] + tot_far[1] + tot_far[2]
    around = []
    for i, place in enumerate(places):
        around.append(send(tot.at[3], tot_near.at[i], tn_s.at[i], tn_r.at[i], near(*place)))
    for cp in around:
        cp.wait()
    totals = tot[3]
    for i in range(15):
        totals = totals + tot_near[i]

    weight = tot[6]
    row_scale = scale_factor * weight / totals
    label_grad = weight * (tot[1] / totals - 1.0) * tot[2]
    tot[4] = row_scale
    tot[5] = label_grad

    def second_pass(base, n):
        base = pl.multiple_of(base, 16)
        rows = pl.ds(base, n)
        for q in range(4):
            lanes = slice(q * Q, (q + 1) * Q)
            is_target = class_iota[:n] == lab_ref[:, lanes] - (first_class + base)
            grad = jnp.where(is_target, tot[5, :, lanes], e[q, rows, :] * tot[4, :, lanes])
            g[rows, lanes] = grad.astype(BF)
        part[rows, :] = jnp.dot(
            g[rows, :], u[...].reshape(R, D), preferred_element_type=F32
        ).astype(BF)

    def rows_of(ref, start, n):
        return ref.at[pl.ds(pl.multiple_of(start, 16), n)]

    def value(ref, start, n):
        return ref[pl.ds(pl.multiple_of(start, 16), n), :].astype(F32)

    def a_rows(k):
        return ((x + k) % 4) * (2 * NA)

    def b_rows(lot, half, k=None):
        first = FIRST_B[lot] + half * (4 * NB[lot])
        return first if k is None else first + ((x + k) % 4) * NB[lot]

    to_left, to_right = at_x(3), at_x(1)

    def send_b(lot):
        n = 4 * NB[lot]
        base = b_rows(lot, 1 - yh)
        second_pass(base, n)
        return send(rows_of(part, base, n), rb[lot], rs_s.at[2 + lot], rs_r.at[2 + lot], y_peer)

    second_pass(a_rows(2), 2 * NA)
    far_r = send(rows_of(part, a_rows(2), NA), fw.at[0], rs_s.at[0], rs_r.at[0], to_right)
    far_l = send(rows_of(part, a_rows(2) + NA, NA), fw.at[1], rs_s.at[1], rs_r.at[1], to_left)
    rs_b = [send_b(0)]
    second_pass(a_rows(1), 2 * NA)
    rs_a = [send(rows_of(part, a_rows(1) + NA, NA), ra.at[0, 1], rs_s.at[4], rs_r.at[4], to_right)]
    second_pass(a_rows(3), 2 * NA)
    rs_a.append(send(rows_of(part, a_rows(3), NA), ra.at[1, 0], rs_s.at[5], rs_r.at[5], to_left))
    rs_b.append(send_b(1))
    second_pass(a_rows(0), 2 * NA)
    for lot in range(2):
        second_pass(b_rows(lot, yh), 4 * NB[lot])

    def emb_product(cc, yy):
        q = cc * 2 + yy
        lanes = pl.ds(pl.multiple_of(q * Q, Q), Q)
        ed[cc, yy] = lax.dot_general(
            g[:, lanes], unit[...], (((0,), (0,)), ((), ())), preferred_element_type=F32
        ).astype(BF)

    emb_product(1 - c, 0)
    emb_product(1 - c, 1)
    em1 = send(ed.at[1 - c], r1, em_s.at[0], em_r.at[0], core_peer)

    far_r.wait()
    both[0] = (value(part, a_rows(1), NA) + fw[0].astype(F32)).astype(BF)
    rs_a.append(send(both.at[0], ra.at[0, 0], rs_s.at[6], rs_r.at[6], to_right))
    far_l.wait()
    both[1] = (value(part, a_rows(3) + NA, NA) + fw[1].astype(F32)).astype(BF)
    rs_a.append(send(both.at[1], ra.at[1, 1], rs_s.at[7], rs_r.at[7], to_left))
    emb_product(c, 0)
    emb_product(c, 1)

    def own_b(lot):
        n = NB[lot]
        rs_b[lot].wait()
        sum_b = value(part, b_rows(lot, yh), 4 * n) + rb[lot][...].astype(F32)
        sb[lot][...] = sum_b.astype(BF).reshape(4, n, D)
        sent = []
        for k in (2, 1, 3):
            at = 8 + 3 * lot + k
            sent.append(send(sb[lot].at[(x + k) % 4], rx[lot].at[k - 1], rs_s.at[at], rs_r.at[at], at_x(k)))
        return sent

    rs2_b = [own_b(0)]
    em1.wait()
    f1[...] = (ed[c].astype(F32) + r1[...].astype(F32)).astype(BF).reshape(2, 4, 64, D)
    em2 = []
    for i, k in enumerate((2, 1, 15)):
        for yy in range(2):
            at = 1 + i * 2 + yy
            em2.append(send(f1.at[yy, (zl + k) % 4], r2.at[i, yy], em_s.at[at], em_r.at[at], at_z(k)))
    for cp in rs_a:
        cp.wait()
    sum_a = value(part, a_rows(0), 2 * NA)
    for side in range(2):
        sum_a = sum_a + ra[side].reshape(2 * NA, D).astype(F32)
    sa[...] = sum_a.astype(BF).reshape(2, NA, D)
    rs2_a = send(sa.at[1 - yh], ra2, rs_s.at[8], rs_r.at[8], y_peer)
    rs2_b.append(own_b(1))

    serial = [15]
    rest = []

    def pass_on(start, n, where):
        at = serial[0]
        serial[0] += 1
        rows = rows_of(out, start, n)
        return send(rows, rows, rs_s.at[at], rs_r.at[at], where)

    def a_start(k, half):
        return a_rows(k) + half * NA

    def store(start, n, direction):
        inverse, unit_part = unit_rows(value(proto, start, n))
        out[pl.ds(pl.multiple_of(start, 16), n), :] = finish_rows(direction, unit_part, inverse)

    def finish_b(lot):
        for cp in rs2_b[lot]:
            cp.wait()
        direction = value(sb[lot].at[x], 0, NB[lot])
        for k in range(3):
            direction = direction + rx[lot][k].astype(F32)
        start = b_rows(lot, yh, 0)
        store(start, NB[lot], direction)
        near_b = [pass_on(start, NB[lot], to_right), pass_on(start, NB[lot], to_left)]
        rest.append(pass_on(start, NB[lot], y_peer))
        return near_b

    b_near = [finish_b(0)]
    rs2_a.wait()
    mine_a = a_start(0, yh)
    store(mine_a, NA, sa[yh].astype(F32) + ra2[...].astype(F32))
    a_cross = pass_on(mine_a, NA, y_peer)
    b_near.append(finish_b(1))
    a_near = [pass_on(mine_a, NA, to_right), pass_on(mine_a, NA, to_left)]

    for cp in em2:
        cp.wait()
    f2[...] = (
        f1[:, zl].astype(F32) + r2[0].astype(F32) + r2[1].astype(F32) + r2[2].astype(F32)
    ).astype(BF)
    em3 = []
    for i, k in enumerate((8, 4, 12)):
        to = pl.ds(pl.multiple_of(((zh + k // 4) % 4) * 16, 16), 16)
        for yy in range(2):
            at = 7 + i * 2 + yy
            em3.append(send(f2.at[yy, to], r3.at[i, yy], em_s.at[at], em_r.at[at], at_z(k)))

    b_cut, a_cut = 32, 80

    def hand_on_b(lot):
        n = NB[lot]
        b_near[lot][0].wait()
        left = b_rows(lot, yh, 3)
        far = [pass_on(left, b_cut, to_right)]
        rest.append(pass_on(left, n, y_peer))
        b_near[lot][1].wait()
        right = b_rows(lot, yh, 1)
        far.append(pass_on(right + b_cut, n - b_cut, to_left))
        rest.append(pass_on(right, n, y_peer))
        return far

    b_far = [hand_on_b(0), hand_on_b(1)]
    a_cross.wait()
    crossed = a_start(0, 1 - yh)
    c_near = [pass_on(crossed, a_cut, to_right), pass_on(crossed + a_cut, NA - a_cut, to_left)]
    rest.append(pass_on(crossed + a_cut, NA - a_cut, to_right))
    rest.append(pass_on(crossed, a_cut, to_left))
    a_near[0].wait()
    rest.append(pass_on(a_start(3, yh), a_cut, to_right))
    a_near[1].wait()
    rest.append(pass_on(a_start(1, yh) + a_cut, NA - a_cut, to_left))
    for lot in range(2):
        start = b_rows(lot, yh, 2)
        b_far[lot][0].wait()
        rest.append(pass_on(start, b_cut, y_peer))
        b_far[lot][1].wait()
        rest.append(pass_on(start + b_cut, NB[lot] - b_cut, y_peer))
    c_near[0].wait()
    rest.append(pass_on(a_start(3, 1 - yh), a_cut, to_right))
    c_near[1].wait()
    rest.append(pass_on(a_start(1, 1 - yh) + a_cut, NA - a_cut, to_left))

    for cp in em3:
        cp.wait()
    own3 = pl.ds(pl.multiple_of(zh * 16, 16), 16)
    f3[...] = (
        f2[:, own3].astype(F32) + r3[0].astype(F32) + r3[1].astype(F32) + r3[2].astype(F32)
    ).astype(BF)
    em4 = send(f3.at[1 - y], r4, em_s.at[13], em_r.at[13], ylo_peer)
    em4.wait()
    emb_dir = f3[y].astype(F32) + r4[...].astype(F32)
    emb_inv, emb_unit = unit_rows(emb_ref[...])
    emb_out[...] = finish_rows(emb_dir, emb_unit, emb_inv)

    for cp in rest:
        cp.wait()


def write_out(emb_grad, proto_grad, emb_out, proto_out, sems):
    copies = [pltpu.make_async_copy(emb_grad, emb_out, sems.at[8])]
    for i in range(8):
        rows = pl.ds(i * (C // 8), C // 8)
        copies.append(pltpu.make_async_copy(proto_grad.at[rows], proto_out.at[rows], sems.at[i]))
    for cp in copies:
        cp.start()
    for cp in copies:
        cp.wait()


def on_device(embeddings, labels, row_weight, prototypes):
    vmem = pl.BlockSpec(memory_space=pltpu.VMEM)
    anywhere = pl.BlockSpec(memory_space=pl.ANY)
    dma = pltpu.SemaphoreType.DMA
    grads = pl.pallas_call(
        kernel,
        out_shape=(
            pltpu.VMEM((16, D), BF),
            pltpu.VMEM((C, D), BF),
        ),
        in_specs=[anywhere] * 4,
        out_specs=(vmem, vmem),
        scratch_shapes=[
            pltpu.VMEM((16, D), BF),
            pltpu.VMEM((8, 128), jnp.int32),
            pltpu.VMEM((8, 128), F32),
            pltpu.VMEM((C, D), BF),
            pltpu.VMEM((C, D), BF),
            pltpu.VMEM((2, 2, 4, 64, D), BF),
            pltpu.VMEM((4, C, Q), F32),
            pltpu.VMEM((C, R), BF),
            pltpu.VMEM((C, D), BF),
            pltpu.VMEM((1, R), jnp.int32),
            pltpu.VMEM((7, 1, R), F32),
            pltpu.VMEM((3, 1, R), F32),
            pltpu.VMEM((15, 1, R), F32),
            pltpu.VMEM((2, NA, D), BF),
            pltpu.VMEM((2, NA, D), BF),
            pltpu.VMEM((2, 2, NA, D), BF),
            pltpu.VMEM((NA, D), BF),
            pltpu.VMEM((2, NA, D), BF),
            *[pltpu.VMEM((4 * n, D), BF) for n in NB],
            *[pltpu.VMEM((4, n, D), BF) for n in NB],
            *[pltpu.VMEM((3, n, D), BF) for n in NB],
            pltpu.VMEM((2, 2, Q, D), BF),
            pltpu.VMEM((2, Q, D), BF),
            pltpu.VMEM((2, 4, 64, D), BF),
            pltpu.VMEM((3, 2, 64, D), BF),
            pltpu.VMEM((2, 64, D), BF),
            pltpu.VMEM((3, 2, 16, D), BF),
            pltpu.VMEM((2, 16, D), BF),
            pltpu.VMEM((16, D), BF),
            dma((4,)),
            dma((18,)), dma((18,)),
            dma((3,)), dma((3,)),
            dma((15,)), dma((15,)),
            dma((48,)), dma((48,)),
            dma((14,)), dma((14,)),
        ],
        compiler_params=pltpu.CompilerParams(
            collective_id=0, has_side_effects=True, vmem_limit_bytes=56 * 2**20
        ),
        name="margin_softmax_backward",
    )(embeddings, labels.reshape(8, 128), row_weight.reshape(8, 128), prototypes)
    return pl.pallas_call(
        write_out,
        out_shape=(
            jax.ShapeDtypeStruct((16, D), BF),
            jax.ShapeDtypeStruct((C, D), BF),
        ),
        in_specs=[vmem, vmem],
        out_specs=(anywhere, anywhere),
        scratch_shapes=[dma((9,))],
        name="write_out",
    )(*[pltpu.with_memory_space_constraint(grad, pltpu.VMEM) for grad in grads])


def solution(mesh):
    return jax.shard_map(
        on_device,
        mesh=mesh,
        in_specs=(P(("dp", "cls"), None), P("dp"), P("dp"), P("cls", None)),
        out_specs=(P(("dp", "cls"), None), P("cls", None)),
        check_vma=False,
    )
```

```python
import math

import jax
import jax.numpy as jnp
from jax import lax
from jax.experimental import pallas as pl
from jax.experimental.pallas import tpu as pltpu
from jax.sharding import PartitionSpec as P

scale_factor = 64.0
margin = 0.5
sine_floor = 0.04
norm_eps = 1e-06
log2e = 1.4426950408889634
MESH = pl.DeviceIdType.MESH
F32 = jnp.float32
BF = jnp.bfloat16

D = 512
C = 2048
R = 1024
Q = 256
NA = (80, 64)
NB = (64, 48)
FIRST_A = (0, 8 * NA[0])
FIRST_B = (8 * sum(NA), 8 * (sum(NA) + NB[0]))
CH = 256


def unit_rows(values):
    wide = values.astype(F32)
    inverse = lax.rsqrt(jnp.sum(wide * wide, axis=1, keepdims=True) + norm_eps)
    return (inverse, wide * inverse)


def finish_rows(direction, unit_part, inverse):
    return (
        inverse * (direction - unit_part * jnp.sum(unit_part * direction, axis=1, keepdims=True))
    ).astype(BF)


def order_rows(labels, weights, lab_ref, tot):
    pieces = [(labels >> 12), (labels >> 6) & 63, labels & 63]
    pieces = [piece.astype(F32) for piece in pieces]
    rest = weights
    for _ in range(3):
        top = rest.astype(BF).astype(F32)
        pieces.append(top)
        rest = rest - top
    stacked = jnp.concatenate(pieces, axis=0).astype(BF)
    lane = lax.broadcasted_iota(jnp.int32, (128, 512), 0)
    to = lax.broadcasted_iota(jnp.int32, (128, 512), 1)
    from_lane = ((to >> 6) & 1) * 64 + ((to >> 7) & 1) * 32 + (to >> 8) * 16 + (to & 15)
    move = jnp.where(lane == from_lane, 1.0, 0.0).astype(BF)
    moved = jnp.dot(stacked, move, preferred_element_type=F32)
    row = lax.broadcasted_iota(jnp.int32, (8, 128), 0)
    z_high = (lax.broadcasted_iota(jnp.int32, (8, 128), 1) >> 4) & 3
    for tile in range(8):
        keep = row == z_high * 2 + tile % 2
        cut = moved[:, tile // 2 * 128 : (tile // 2 + 1) * 128]
        got = [
            jnp.sum(jnp.where(keep, cut[8 * i : 8 * i + 8], 0.0), axis=0, keepdims=True)
            for i in range(6)
        ]
        lanes = slice(tile * 128, (tile + 1) * 128)
        lab_ref[:, lanes] = (got[0] * 4096.0 + got[1] * 64.0 + got[2]).astype(jnp.int32)
        tot[6, :, lanes] = got[3] + got[4] + got[5]


def kernel(
    emb_hbm, lab_hbm, wgt_hbm, proto_hbm,
    emb_out, out,
    emb_ref, lab_in, wgt_in, proto, unit, u, e, g, part,
    lab_ref, tot, tot_far, tot_near,
    fw0, fw1, both0, both1, ra0, ra1, rc0, rc1, sa0, sa1, rb0, rb1, sb0, sb1, rx0, rx1,
    ed, r1, f1, r2, f2, r3, f3, r4,
    in_sems,
    ag_s, ag_r, tf_s, tf_r, tn_s, tn_r, rs_s, rs_r, em_s, em_r,
):
    fw, both, ra, ra2, sa = (fw0, fw1), (both0, both1), (ra0, ra1), (rc0, rc1), (sa0, sa1)
    rb, sb, rx = (rb0, rb1), (sb0, sb1), (rx0, rx1)
    dp = lax.axis_index("dp")
    cls = lax.axis_index("cls")
    yh, x = dp // 4, dp % 4
    z, y, c = cls // 4, (cls // 2) % 2, cls % 2
    zh, zl = z // 4, z % 4

    def at_z(k):
        return (dp, ((z + k) % 16) * 4 + y * 2 + c)

    def near(k, dy, dc):
        yy = (y + dy) % 2
        cc = (c + dc) % 2
        return (dp, ((z + k) % 16) * 4 + yy * 2 + cc)

    def at_x(k):
        return (yh * 4 + (x + k) % 4, cls)

    y_peer = ((1 - yh) * 4 + x, cls)
    core_peer = near(0, 0, 1)
    ylo_peer = near(0, 1, 0)
    places = [(k, dy, dc) for k in (2, 1, 15, 0) for dy, dc in ((1, 1), (1, 0), (0, 1), (0, 0))][:-1]

    def send(src, dst, ssem, rsem, where):
        cp = pltpu.make_async_remote_copy(
            src_ref=src, dst_ref=dst, send_sem=ssem, recv_sem=rsem,
            device_id=where, device_id_type=MESH,
        )
        cp.start()
        return cp

    barrier = pltpu.get_barrier_semaphore()
    friends = [at_z(k) for k in (8, 4, 12)] + [near(*place) for place in places]
    friends += [at_x(1), at_x(2), at_x(3), y_peer]
    for friend in friends:
        pl.semaphore_signal(barrier, inc=1, device_id=friend, device_id_type=MESH)
    sources = ((emb_hbm, emb_ref), (lab_hbm, lab_in), (wgt_hbm, wgt_in), (proto_hbm, proto))
    loads = [pltpu.make_async_copy(src, dst, in_sems.at[i]) for i, (src, dst) in enumerate(sources)]
    for load in loads:
        load.start()
    loads[0].wait()
    emb_inv, emb_unit = unit_rows(emb_ref[...])
    u[c, y, zl, pl.ds(pl.multiple_of(zh * 16, 16), 16), :] = emb_unit.astype(BF)
    pl.semaphore_wait(barrier, len(friends))

    sends = []
    own_block = u.at[c, y, zl, pl.ds(pl.multiple_of(zh * 16, 16), 16)]
    p1 = [send(own_block, own_block, ag_s.at[i], ag_r.at[i], at_z(k)) for i, k in enumerate((8, 4, 12))]

    for load in loads[1:]:
        load.wait()

    def normalize(i, carry):
        rows = pl.ds(pl.multiple_of(i * CH, CH), CH)
        unit[rows, :] = unit_rows(proto[rows, :])[1].astype(BF)
        return carry

    lax.fori_loop(0, C // CH // 2, normalize, 0)
    for cp in p1:
        cp.wait()
    own_set = u.at[c, y, zl]
    p2 = [send(own_set, own_set, ag_s.at[3 + i], ag_r.at[3 + i], at_z(k)) for i, k in enumerate((1, 15, 2))]
    lax.fori_loop(C // CH // 2, C // CH, normalize, 0)
    order_rows(lab_in[...], wgt_in[...], lab_ref, tot)
    toy = [send(own_set, own_set, ag_s.at[6], ag_r.at[6], ylo_peer)]
    toc = [send(own_set, own_set, ag_s.at[10], ag_r.at[10], core_peer)]
    for i, k in enumerate((1, 15, 2)):
        p2[i].wait()
        got = u.at[c, y, (zl + 16 - k) % 4]
        toy.append(send(got, got, ag_s.at[7 + i], ag_r.at[7 + i], ylo_peer))
        toc.append(send(got, got, ag_s.at[11 + i], ag_r.at[11 + i], core_peer))

    class_iota = lax.broadcasted_iota(jnp.int32, (C, Q), 0)
    first_class = cls * C

    def first_pass(cc, yy):
        q = cc * 2 + yy
        lanes = pl.ds(pl.multiple_of(q * Q, Q), Q)
        labels = lab_ref[:, lanes] - first_class
        rows_u = u[cc, yy].reshape(Q, D)

        cosine = lax.dot_general(
            unit[...], rows_u, (((1,), (1,)), ((), ())), preferred_element_type=F32
        )
        is_target = class_iota == labels
        ex = jnp.where(is_target, 0.0, jnp.exp2(cosine * (scale_factor * log2e)))
        e[q] = ex
        total = jnp.sum(ex, axis=0, keepdims=True)
        target_cos = jnp.sum(jnp.where(is_target, cosine, 0.0), axis=0, keepdims=True)
        here = (labels >= 0) & (labels < C)
        sine = jnp.sqrt(jnp.maximum(1.0 - target_cos * target_cos, sine_floor))
        target_logit = scale_factor * (target_cos * math.cos(margin) - sine * math.sin(margin))
        target_exp = jnp.exp(target_logit)
        tot[0, :, lanes] = total + jnp.where(here, target_exp, 0.0)
        bound_free = 1.0 - target_cos * target_cos > sine_floor
        slope = scale_factor * (
            math.cos(margin) + jnp.where(bound_free, math.sin(margin) * target_cos / sine, 0.0)
        )
        tot[1, :, lanes] = target_exp
        tot[2, :, lanes] = slope

    first_pass(c, y)
    for cp in toc:
        cp.wait()
    first_pass(1 - c, y)
    tod = []
    for i, k in enumerate((0, 1, 15, 2)):
        toy[i].wait()
        got = u.at[c, 1 - y, (zl + 16 - k) % 4]
        tod.append(send(got, got, ag_s.at[14 + i], ag_r.at[14 + i], core_peer))
    first_pass(c, 1 - y)
    for cp in tod:
        cp.wait()
    first_pass(1 - c, 1 - y)

    apart = []
    for i, k in enumerate((8, 4, 12)):
        apart.append(send(tot.at[0], tot_far.at[i], tf_s.at[i], tf_r.at[i], at_z(k)))
    for cp in apart:
        cp.wait()
    tot[3] = tot[0] + tot_far[0] + tot_far[1] + tot_far[2]
    around = []
    for i, place in enumerate(places):
        around.append(send(tot.at[3], tot_near.at[i], tn_s.at[i], tn_r.at[i], near(*place)))
    for cp in around:
        cp.wait()
    totals = tot[3]
    for i in range(15):
        totals = totals + tot_near[i]

    weight = tot[6]
    row_scale = scale_factor * weight / totals
    label_grad = weight * (tot[1] / totals - 1.0) * tot[2]
    tot[4] = row_scale
    tot[5] = label_grad

    def second_pass(base, n):
        base = pl.multiple_of(base, 16)
        rows = pl.ds(base, n)
        for q in range(4):
            lanes = slice(q * Q, (q + 1) * Q)
            is_target = class_iota[:n] == lab_ref[:, lanes] - (first_class + base)
            grad = jnp.where(is_target, tot[5, :, lanes], e[q, rows, :] * tot[4, :, lanes])
            g[rows, lanes] = grad.astype(BF)
        part[rows, :] = jnp.dot(
            g[rows, :], u[...].reshape(R, D), preferred_element_type=F32
        ).astype(BF)

    def rows_of(ref, start, n):
        return ref.at[pl.ds(pl.multiple_of(start, 16), n)]

    def value(ref, start, n):
        return ref[pl.ds(pl.multiple_of(start, 16), n), :].astype(F32)

    def a_rows(lot, k):
        return FIRST_A[lot] + ((x + k) % 4) * (2 * NA[lot])

    def b_rows(lot, half, k=None):
        first = FIRST_B[lot] + half * (4 * NB[lot])
        return first if k is None else first + ((x + k) % 4) * NB[lot]

    to_left, to_right = at_x(3), at_x(1)

    serial = [0]

    def ship(src, dst, where):
        at = serial[0]
        serial[0] += 1
        return send(src, dst, rs_s.at[at], rs_r.at[at], where)

    far, rs_a, rs_b = [], ([], []), []

    def send_far(lot):
        n, base = NA[lot], a_rows(lot, 2)
        second_pass(base, 2 * n)
        to_r = ship(rows_of(part, base, n), fw[lot].at[0], to_right)
        far.append((to_r, ship(rows_of(part, base + n, n), fw[lot].at[1], to_left)))

    def send_plain(lot):
        n, base = NA[lot], a_rows(lot, 1)
        second_pass(base, 2 * n)
        rs_a[lot].append(ship(rows_of(part, base + n, n), ra[lot].at[0, 1], to_right))
        base = a_rows(lot, 3)
        second_pass(base, 2 * n)
        rs_a[lot].append(ship(rows_of(part, base, n), ra[lot].at[1, 0], to_left))

    def send_joined(lot):
        n = NA[lot]
        for side, start, to in ((0, a_rows(lot, 1), to_right), (1, a_rows(lot, 3) + n, to_left)):
            far[lot][side].wait()
            both[lot][side] = (value(part, start, n) + fw[lot][side].astype(F32)).astype(BF)
            rs_a[lot].append(ship(both[lot].at[side], ra[lot].at[side, side], to))

    def send_b(lot):
        n, base = 4 * NB[lot], b_rows(lot, 1 - yh)
        second_pass(base, n)
        rs_b.append(ship(rows_of(part, base, n), rb[lot], y_peer))

    send_far(0)
    send_far(1)
    send_b(0)
    send_plain(0)
    send_plain(1)
    send_b(1)
    for lot in range(2):
        second_pass(a_rows(lot, 0), 2 * NA[lot])
        second_pass(b_rows(lot, yh), 4 * NB[lot])

    def emb_product(cc, yy):
        q = cc * 2 + yy
        lanes = pl.ds(pl.multiple_of(q * Q, Q), Q)
        ed[cc, yy] = lax.dot_general(
            g[:, lanes], unit[...], (((0,), (0,)), ((), ())), preferred_element_type=F32
        ).astype(BF)

    emb_product(1 - c, 0)
    emb_product(1 - c, 1)
    em1 = send(ed.at[1 - c], r1, em_s.at[0], em_r.at[0], core_peer)

    send_joined(0)
    send_joined(1)
    emb_product(c, 0)
    emb_product(c, 1)

    def own_b(lot):
        n = NB[lot]
        rs_b[lot].wait()
        sum_b = value(part, b_rows(lot, yh), 4 * n) + rb[lot][...].astype(F32)
        sb[lot][...] = sum_b.astype(BF).reshape(4, n, D)
        sent = []
        for k in (2, 1, 3):
            sent.append(ship(sb[lot].at[(x + k) % 4], rx[lot].at[k - 1], at_x(k)))
        return sent

    def own_a(lot):
        n = NA[lot]
        for cp in rs_a[lot]:
            cp.wait()
        sum_a = value(part, a_rows(lot, 0), 2 * n)
        for side in range(2):
            sum_a = sum_a + ra[lot][side].reshape(2 * n, D).astype(F32)
        sa[lot][...] = sum_a.astype(BF).reshape(2, n, D)
        return ship(sa[lot].at[1 - yh], ra2[lot], y_peer)

    rs2_b = [own_b(0)]
    em1.wait()
    f1[...] = (ed[c].astype(F32) + r1[...].astype(F32)).astype(BF).reshape(2, 4, 64, D)
    em2 = []
    for i, k in enumerate((2, 1, 15)):
        for yy in range(2):
            at = 1 + i * 2 + yy
            em2.append(send(f1.at[yy, (zl + k) % 4], r2.at[i, yy], em_s.at[at], em_r.at[at], at_z(k)))
    rs2_a = [own_a(0), own_a(1)]
    rs2_b.append(own_b(1))

    rest = []

    def pass_on(start, n, where):
        rows = rows_of(out, start, n)
        return ship(rows, rows, where)

    def a_start(lot, k, half):
        return a_rows(lot, k) + half * NA[lot]

    def store(start, n, direction):
        inverse, unit_part = unit_rows(value(proto, start, n))
        out[pl.ds(pl.multiple_of(start, 16), n), :] = finish_rows(direction, unit_part, inverse)

    def finish_b(lot):
        for cp in rs2_b[lot]:
            cp.wait()
        direction = value(sb[lot].at[x], 0, NB[lot])
        for k in range(3):
            direction = direction + rx[lot][k].astype(F32)
        start = b_rows(lot, yh, 0)
        store(start, NB[lot], direction)
        near_b = [pass_on(start, NB[lot], to_right), pass_on(start, NB[lot], to_left)]
        rest.append(pass_on(start, NB[lot], y_peer))
        return near_b

    def finish_a(lot):
        n, start = NA[lot], a_start(lot, 0, yh)
        rs2_a[lot].wait()
        store(start, n, sa[lot][yh].astype(F32) + ra2[lot][...].astype(F32))
        cross = pass_on(start, n, y_peer)
        return cross, pass_on(start, n, to_right), pass_on(start, n, to_left)

    b_near = [finish_b(0)]
    a_near = [finish_a(0), finish_a(1)]
    b_near.append(finish_b(1))

    for cp in em2:
        cp.wait()
    f2[...] = (
        f1[:, zl].astype(F32) + r2[0].astype(F32) + r2[1].astype(F32) + r2[2].astype(F32)
    ).astype(BF)
    em3 = []
    for i, k in enumerate((8, 4, 12)):
        to = pl.ds(pl.multiple_of(((zh + k // 4) % 4) * 16, 16), 16)
        for yy in range(2):
            at = 7 + i * 2 + yy
            em3.append(send(f2.at[yy, to], r3.at[i, yy], em_s.at[at], em_r.at[at], at_z(k)))

    a_cut, b_cut = (48, 32), (32, 16)

    def hand_on_b(lot):
        n, cut = NB[lot], b_cut[lot]
        b_near[lot][0].wait()
        left = b_rows(lot, yh, 3)
        far_r = pass_on(left, cut, to_right)
        rest.append(pass_on(left, n, y_peer))
        b_near[lot][1].wait()
        right = b_rows(lot, yh, 1)
        far_l = pass_on(right + cut, n - cut, to_left)
        rest.append(pass_on(right, n, y_peer))
        return far_r, far_l

    def cross_b(lot):
        n, cut, start = NB[lot], b_cut[lot], b_rows(lot, yh, 2)
        b_far[lot][0].wait()
        rest.append(pass_on(start, cut, y_peer))
        b_far[lot][1].wait()
        rest.append(pass_on(start + cut, n - cut, y_peer))

    def spread_a(lot):
        n, cut, start = NA[lot], a_cut[lot], a_start(lot, 0, 1 - yh)
        a_near[lot][0].wait()
        pair = (pass_on(start, cut, to_right), pass_on(start + cut, n - cut, to_left))
        rest.append(pass_on(start + cut, n - cut, to_right))
        rest.append(pass_on(start, cut, to_left))
        return pair

    def hand_on_a(lot, half, pair):
        n, cut = NA[lot], a_cut[lot]
        pair[0].wait()
        rest.append(pass_on(a_start(lot, 3, half), cut, to_right))
        pair[1].wait()
        rest.append(pass_on(a_start(lot, 1, half) + cut, n - cut, to_left))

    b_far = [hand_on_b(0)]
    c_near = [spread_a(0)]
    hand_on_a(0, yh, a_near[0][1:])
    c_near.append(spread_a(1))
    b_far.append(hand_on_b(1))
    hand_on_a(1, yh, a_near[1][1:])
    cross_b(0)
    hand_on_a(0, 1 - yh, c_near[0])
    cross_b(1)
    hand_on_a(1, 1 - yh, c_near[1])

    for cp in em3:
        cp.wait()
    own3 = pl.ds(pl.multiple_of(zh * 16, 16), 16)
    f3[...] = (
        f2[:, own3].astype(F32) + r3[0].astype(F32) + r3[1].astype(F32) + r3[2].astype(F32)
    ).astype(BF)
    em4 = send(f3.at[1 - y], r4, em_s.at[13], em_r.at[13], ylo_peer)
    em4.wait()
    emb_dir = f3[y].astype(F32) + r4[...].astype(F32)
    emb_inv, emb_unit = unit_rows(emb_ref[...])
    emb_out[...] = finish_rows(emb_dir, emb_unit, emb_inv)

    for cp in rest:
        cp.wait()


def write_out(emb_grad, proto_grad, emb_out, proto_out, sems):
    copies = [pltpu.make_async_copy(emb_grad, emb_out, sems.at[8])]
    for i in range(8):
        rows = pl.ds(i * (C // 8), C // 8)
        copies.append(pltpu.make_async_copy(proto_grad.at[rows], proto_out.at[rows], sems.at[i]))
    for cp in copies:
        cp.start()
    for cp in copies:
        cp.wait()


def on_device(embeddings, labels, row_weight, prototypes):
    vmem = pl.BlockSpec(memory_space=pltpu.VMEM)
    anywhere = pl.BlockSpec(memory_space=pl.ANY)
    dma = pltpu.SemaphoreType.DMA
    grads = pl.pallas_call(
        kernel,
        out_shape=(
            pltpu.VMEM((16, D), BF),
            pltpu.VMEM((C, D), BF),
        ),
        in_specs=[anywhere] * 4,
        out_specs=(vmem, vmem),
        scratch_shapes=[
            pltpu.VMEM((16, D), BF),
            pltpu.VMEM((8, 128), jnp.int32),
            pltpu.VMEM((8, 128), F32),
            pltpu.VMEM((C, D), BF),
            pltpu.VMEM((C, D), BF),
            pltpu.VMEM((2, 2, 4, 64, D), BF),
            pltpu.VMEM((4, C, Q), F32),
            pltpu.VMEM((C, R), BF),
            pltpu.VMEM((C, D), BF),
            pltpu.VMEM((1, R), jnp.int32),
            pltpu.VMEM((7, 1, R), F32),
            pltpu.VMEM((3, 1, R), F32),
            pltpu.VMEM((15, 1, R), F32),
            *[pltpu.VMEM((2, n, D), BF) for n in NA],
            *[pltpu.VMEM((2, n, D), BF) for n in NA],
            *[pltpu.VMEM((2, 2, n, D), BF) for n in NA],
            *[pltpu.VMEM((n, D), BF) for n in NA],
            *[pltpu.VMEM((2, n, D), BF) for n in NA],
            *[pltpu.VMEM((4 * n, D), BF) for n in NB],
            *[pltpu.VMEM((4, n, D), BF) for n in NB],
            *[pltpu.VMEM((3, n, D), BF) for n in NB],
            pltpu.VMEM((2, 2, Q, D), BF),
            pltpu.VMEM((2, Q, D), BF),
            pltpu.VMEM((2, 4, 64, D), BF),
            pltpu.VMEM((3, 2, 64, D), BF),
            pltpu.VMEM((2, 64, D), BF),
            pltpu.VMEM((3, 2, 16, D), BF),
            pltpu.VMEM((2, 16, D), BF),
            pltpu.VMEM((16, D), BF),
            dma((4,)),
            dma((18,)), dma((18,)),
            dma((3,)), dma((3,)),
            dma((15,)), dma((15,)),
            dma((64,)), dma((64,)),
            dma((14,)), dma((14,)),
        ],
        compiler_params=pltpu.CompilerParams(
            collective_id=0, has_side_effects=True, vmem_limit_bytes=56 * 2**20
        ),
        name="margin_softmax_backward",
    )(embeddings, labels.reshape(8, 128), row_weight.reshape(8, 128), prototypes)
    return pl.pallas_call(
        write_out,
        out_shape=(
            jax.ShapeDtypeStruct((16, D), BF),
            jax.ShapeDtypeStruct((C, D), BF),
        ),
        in_specs=[vmem, vmem],
        out_specs=(anywhere, anywhere),
        scratch_shapes=[dma((9,))],
        name="write_out",
    )(*[pltpu.with_memory_space_constraint(grad, pltpu.VMEM) for grad in grads])


def solution(mesh):
    return jax.shard_map(
        on_device,
        mesh=mesh,
        in_specs=(P(("dp", "cls"), None), P("dp"), P("dp"), P("cls", None)),
        out_specs=(P(("dp", "cls"), None), P("cls", None)),
        check_vma=False,
    )
```

```python
import math

import jax
import jax.numpy as jnp
from jax import lax
from jax.experimental import pallas as pl
from jax.experimental.pallas import tpu as pltpu
from jax.sharding import PartitionSpec as P

scale_factor = 64.0
margin = 0.5
sine_floor = 0.04
norm_eps = 1e-06
log2e = 1.4426950408889634
MESH = pl.DeviceIdType.MESH
F32 = jnp.float32
BF = jnp.bfloat16

D = 512
C = 2048
R = 1024
Q = 256
NA = (80, 64)
NB = (64, 48)
FIRST_A = (0, 8 * NA[0])
FIRST_B = (8 * sum(NA), 8 * (sum(NA) + NB[0]))
CH = 256


def unit_rows(values):
    wide = values.astype(F32)
    inverse = lax.rsqrt(jnp.sum(wide * wide, axis=1, keepdims=True) + norm_eps)
    return (inverse, wide * inverse)


def finish_rows(direction, unit_part, inverse):
    return (
        inverse * (direction - unit_part * jnp.sum(unit_part * direction, axis=1, keepdims=True))
    ).astype(BF)


def order_rows(labels, weights, lab_ref, tot):
    pieces = [(labels >> 12), (labels >> 6) & 63, labels & 63]
    pieces = [piece.astype(F32) for piece in pieces]
    rest = weights
    for _ in range(3):
        top = rest.astype(BF).astype(F32)
        pieces.append(top)
        rest = rest - top
    stacked = jnp.concatenate(pieces, axis=0).astype(BF)
    lane = lax.broadcasted_iota(jnp.int32, (128, 512), 0)
    to = lax.broadcasted_iota(jnp.int32, (128, 512), 1)
    from_lane = ((to >> 6) & 1) * 64 + ((to >> 7) & 1) * 32 + (to >> 8) * 16 + (to & 15)
    move = jnp.where(lane == from_lane, 1.0, 0.0).astype(BF)
    moved = jnp.dot(stacked, move, preferred_element_type=F32)
    row = lax.broadcasted_iota(jnp.int32, (8, 128), 0)
    z_high = (lax.broadcasted_iota(jnp.int32, (8, 128), 1) >> 4) & 3
    for tile in range(8):
        keep = row == z_high * 2 + tile % 2
        cut = moved[:, tile // 2 * 128 : (tile // 2 + 1) * 128]
        got = [
            jnp.sum(jnp.where(keep, cut[8 * i : 8 * i + 8], 0.0), axis=0, keepdims=True)
            for i in range(6)
        ]
        lanes = slice(tile * 128, (tile + 1) * 128)
        lab_ref[:, lanes] = (got[0] * 4096.0 + got[1] * 64.0 + got[2]).astype(jnp.int32)
        tot[6, :, lanes] = got[3] + got[4] + got[5]


def kernel(
    emb_hbm, lab_hbm, wgt_hbm, proto_hbm,
    emb_out, out,
    emb_ref, lab_in, wgt_in, proto, unit, u, e, g, part,
    lab_ref, tot, tot_far, tot_near,
    fw0, fw1, both0, both1, ra0, ra1, rc0, rc1, sa0, sa1, rb0, rb1, sb0, sb1, rx0, rx1,
    ed, r1, f1, r2, f2, r3, f3, r4,
    in_sems,
    ag_s, ag_r, tf_s, tf_r, tn_s, tn_r, rs_s, rs_r, em_s, em_r,
):
    fw, both, ra, ra2, sa = (fw0, fw1), (both0, both1), (ra0, ra1), (rc0, rc1), (sa0, sa1)
    rb, sb, rx = (rb0, rb1), (sb0, sb1), (rx0, rx1)
    dp = lax.axis_index("dp")
    cls = lax.axis_index("cls")
    yh, x = dp // 4, dp % 4
    z, y, c = cls // 4, (cls // 2) % 2, cls % 2
    zh, zl = z // 4, z % 4

    def at_z(k):
        return (dp, ((z + k) % 16) * 4 + y * 2 + c)

    def near(k, dy, dc):
        yy = (y + dy) % 2
        cc = (c + dc) % 2
        return (dp, ((z + k) % 16) * 4 + yy * 2 + cc)

    def at_x(k):
        return (yh * 4 + (x + k) % 4, cls)

    y_peer = ((1 - yh) * 4 + x, cls)
    core_peer = near(0, 0, 1)
    ylo_peer = near(0, 1, 0)
    places = [(k, dy, dc) for k in (2, 1, 15, 0) for dy, dc in ((1, 1), (1, 0), (0, 1), (0, 0))][:-1]

    def send(src, dst, ssem, rsem, where):
        cp = pltpu.make_async_remote_copy(
            src_ref=src, dst_ref=dst, send_sem=ssem, recv_sem=rsem,
            device_id=where, device_id_type=MESH,
        )
        cp.start()
        return cp

    barrier = pltpu.get_barrier_semaphore()
    friends = [at_z(k) for k in (8, 4, 12)] + [near(*place) for place in places]
    friends += [at_x(1), at_x(2), at_x(3), y_peer]
    for friend in friends:
        pl.semaphore_signal(barrier, inc=1, device_id=friend, device_id_type=MESH)
    sources = ((emb_hbm, emb_ref), (lab_hbm, lab_in), (wgt_hbm, wgt_in), (proto_hbm, proto))
    loads = [pltpu.make_async_copy(src, dst, in_sems.at[i]) for i, (src, dst) in enumerate(sources)]
    for load in loads:
        load.start()
    loads[0].wait()
    emb_inv, emb_unit = unit_rows(emb_ref[...])
    u[c, y, zl, pl.ds(pl.multiple_of(zh * 16, 16), 16), :] = emb_unit.astype(BF)
    pl.semaphore_wait(barrier, len(friends))

    sends = []
    own_block = u.at[c, y, zl, pl.ds(pl.multiple_of(zh * 16, 16), 16)]
    p1 = [send(own_block, own_block, ag_s.at[i], ag_r.at[i], at_z(k)) for i, k in enumerate((8, 4, 12))]

    for load in loads[1:]:
        load.wait()

    def normalize(i, carry):
        rows = pl.ds(pl.multiple_of(i * CH, CH), CH)
        unit[rows, :] = unit_rows(proto[rows, :])[1].astype(BF)
        return carry

    lax.fori_loop(0, C // CH // 2, normalize, 0)
    for cp in p1:
        cp.wait()
    own_set = u.at[c, y, zl]
    p2 = [send(own_set, own_set, ag_s.at[3 + i], ag_r.at[3 + i], at_z(k)) for i, k in enumerate((1, 15, 2))]
    lax.fori_loop(C // CH // 2, C // CH, normalize, 0)
    order_rows(lab_in[...], wgt_in[...], lab_ref, tot)
    toy = [send(own_set, own_set, ag_s.at[6], ag_r.at[6], ylo_peer)]
    toc = [send(own_set, own_set, ag_s.at[10], ag_r.at[10], core_peer)]
    for i, k in enumerate((1, 15, 2)):
        p2[i].wait()
        got = u.at[c, y, (zl + 16 - k) % 4]
        toy.append(send(got, got, ag_s.at[7 + i], ag_r.at[7 + i], ylo_peer))
        toc.append(send(got, got, ag_s.at[11 + i], ag_r.at[11 + i], core_peer))

    class_iota = lax.broadcasted_iota(jnp.int32, (C, Q), 0)
    first_class = cls * C

    def first_pass(cc, yy):
        q = cc * 2 + yy
        lanes = pl.ds(pl.multiple_of(q * Q, Q), Q)
        labels = lab_ref[:, lanes] - first_class
        rows_u = u[cc, yy].reshape(Q, D)

        cosine = lax.dot_general(
            unit[...], rows_u, (((1,), (1,)), ((), ())), preferred_element_type=F32
        )
        is_target = class_iota == labels
        ex = jnp.where(is_target, 0.0, jnp.exp2(cosine * (scale_factor * log2e)))
        e[q] = ex
        total = jnp.sum(ex, axis=0, keepdims=True)
        target_cos = jnp.sum(jnp.where(is_target, cosine, 0.0), axis=0, keepdims=True)
        here = (labels >= 0) & (labels < C)
        sine = jnp.sqrt(jnp.maximum(1.0 - target_cos * target_cos, sine_floor))
        target_logit = scale_factor * (target_cos * math.cos(margin) - sine * math.sin(margin))
        target_exp = jnp.exp(target_logit)
        tot[0, :, lanes] = total + jnp.where(here, target_exp, 0.0)
        bound_free = 1.0 - target_cos * target_cos > sine_floor
        slope = scale_factor * (
            math.cos(margin) + jnp.where(bound_free, math.sin(margin) * target_cos / sine, 0.0)
        )
        tot[1, :, lanes] = target_exp
        tot[2, :, lanes] = slope

    first_pass(c, y)
    for cp in toc:
        cp.wait()
    first_pass(1 - c, y)
    tod = []
    for i, k in enumerate((0, 1, 15, 2)):
        toy[i].wait()
        got = u.at[c, 1 - y, (zl + 16 - k) % 4]
        tod.append(send(got, got, ag_s.at[14 + i], ag_r.at[14 + i], core_peer))
    first_pass(c, 1 - y)
    for cp in tod:
        cp.wait()
    first_pass(1 - c, 1 - y)

    apart = []
    for i, k in enumerate((8, 4, 12)):
        apart.append(send(tot.at[0], tot_far.at[i], tf_s.at[i], tf_r.at[i], at_z(k)))
    for cp in apart:
        cp.wait()
    tot[3] = tot[0] + tot_far[0] + tot_far[1] + tot_far[2]
    around = []
    for i, place in enumerate(places):
        around.append(send(tot.at[3], tot_near.at[i], tn_s.at[i], tn_r.at[i], near(*place)))
    for cp in around:
        cp.wait()
    totals = tot[3]
    for i in range(15):
        totals = totals + tot_near[i]

    weight = tot[6]
    row_scale = scale_factor * weight / totals
    label_grad = weight * (tot[1] / totals - 1.0) * tot[2]
    tot[4] = row_scale
    tot[5] = label_grad

    def second_pass(base, n):
        base = pl.multiple_of(base, 16)
        rows = pl.ds(base, n)
        for q in range(4):
            lanes = slice(q * Q, (q + 1) * Q)
            is_target = class_iota[:n] == lab_ref[:, lanes] - (first_class + base)
            grad = jnp.where(is_target, tot[5, :, lanes], e[q, rows, :] * tot[4, :, lanes])
            g[rows, lanes] = grad.astype(BF)
        part[rows, :] = jnp.dot(
            g[rows, :], u[...].reshape(R, D), preferred_element_type=F32
        ).astype(BF)

    def rows_of(ref, start, n):
        return ref.at[pl.ds(pl.multiple_of(start, 16), n)]

    def value(ref, start, n):
        return ref[pl.ds(pl.multiple_of(start, 16), n), :].astype(F32)

    def a_rows(lot, k):
        return FIRST_A[lot] + ((x + k) % 4) * (2 * NA[lot])

    def b_rows(lot, half, k=None):
        first = FIRST_B[lot] + half * (4 * NB[lot])
        return first if k is None else first + ((x + k) % 4) * NB[lot]

    to_left, to_right = at_x(3), at_x(1)

    serial = [0]

    def ship(src, dst, where):
        at = serial[0]
        serial[0] += 1
        return send(src, dst, rs_s.at[at], rs_r.at[at], where)

    far, rs_a, rs_b = [], ([], []), []

    def send_far(lot):
        n, base = NA[lot], a_rows(lot, 2)
        second_pass(base, 2 * n)
        to_r = ship(rows_of(part, base, n), fw[lot].at[0], to_right)
        far.append((to_r, ship(rows_of(part, base + n, n), fw[lot].at[1], to_left)))

    def send_plain(lot):
        n, base = NA[lot], a_rows(lot, 1)
        second_pass(base, 2 * n)
        rs_a[lot].append(ship(rows_of(part, base + n, n), ra[lot].at[0, 1], to_right))
        base = a_rows(lot, 3)
        second_pass(base, 2 * n)
        rs_a[lot].append(ship(rows_of(part, base, n), ra[lot].at[1, 0], to_left))

    def send_joined(lot):
        n = NA[lot]
        for side, start, to in ((0, a_rows(lot, 1), to_right), (1, a_rows(lot, 3) + n, to_left)):
            far[lot][side].wait()
            both[lot][side] = (value(part, start, n) + fw[lot][side].astype(F32)).astype(BF)
            rs_a[lot].append(ship(both[lot].at[side], ra[lot].at[side, side], to))

    def send_b(lot):
        n, base = 4 * NB[lot], b_rows(lot, 1 - yh)
        second_pass(base, n)
        rs_b.append(ship(rows_of(part, base, n), rb[lot], y_peer))

    send_far(0)
    send_far(1)
    send_b(0)
    send_plain(0)
    send_plain(1)
    send_b(1)
    for lot in range(2):
        second_pass(a_rows(lot, 0), 2 * NA[lot])
        second_pass(b_rows(lot, yh), 4 * NB[lot])

    def emb_product(cc, yy):
        q = cc * 2 + yy
        lanes = pl.ds(pl.multiple_of(q * Q, Q), Q)
        ed[cc, yy] = lax.dot_general(
            g[:, lanes], unit[...], (((0,), (0,)), ((), ())), preferred_element_type=F32
        ).astype(BF)

    emb_product(1 - c, 0)
    emb_product(1 - c, 1)
    em1 = send(ed.at[1 - c], r1, em_s.at[0], em_r.at[0], core_peer)

    send_joined(0)
    send_joined(1)
    emb_product(c, 0)
    emb_product(c, 1)

    def own_b(lot):
        n = NB[lot]
        rs_b[lot].wait()
        sum_b = value(part, b_rows(lot, yh), 4 * n) + rb[lot][...].astype(F32)
        sb[lot][...] = sum_b.astype(BF).reshape(4, n, D)
        sent = []
        for k in (2, 1, 3):
            sent.append(ship(sb[lot].at[(x + k) % 4], rx[lot].at[k - 1], at_x(k)))
        return sent

    def own_a(lot):
        n = NA[lot]
        for cp in rs_a[lot]:
            cp.wait()
        sum_a = value(part, a_rows(lot, 0), 2 * n)
        for side in range(2):
            sum_a = sum_a + ra[lot][side].reshape(2 * n, D).astype(F32)
        sa[lot][...] = sum_a.astype(BF).reshape(2, n, D)
        return ship(sa[lot].at[1 - yh], ra2[lot], y_peer)

    rs2_b = [own_b(0)]
    em1.wait()
    f1[...] = (ed[c].astype(F32) + r1[...].astype(F32)).astype(BF).reshape(2, 4, 64, D)
    em2 = []
    for i, k in enumerate((2, 1, 15)):
        for yy in range(2):
            at = 1 + i * 2 + yy
            em2.append(send(f1.at[yy, (zl + k) % 4], r2.at[i, yy], em_s.at[at], em_r.at[at], at_z(k)))
    rs2_a = [own_a(0), own_a(1)]
    rs2_b.append(own_b(1))

    rest = []
    direct_a, direct_b = (1,), (1,)

    def pass_on(start, n, where):
        rows = rows_of(out, start, n)
        return ship(rows, rows, where)

    def a_start(lot, k, half):
        return a_rows(lot, k) + half * NA[lot]

    def store(start, n, direction):
        inverse, unit_part = unit_rows(value(proto, start, n))
        out[pl.ds(pl.multiple_of(start, 16), n), :] = finish_rows(direction, unit_part, inverse)

    def finish_b(lot):
        for cp in rs2_b[lot]:
            cp.wait()
        direction = value(sb[lot].at[x], 0, NB[lot])
        for k in range(3):
            direction = direction + rx[lot][k].astype(F32)
        start = b_rows(lot, yh, 0)
        store(start, NB[lot], direction)
        near_b = [pass_on(start, NB[lot], to_right), pass_on(start, NB[lot], to_left)]
        if lot in direct_b:
            near_b.append(pass_on(start, NB[lot], at_x(2)))
        rest.append(pass_on(start, NB[lot], y_peer))
        return near_b

    def finish_a(lot):
        n, start = NA[lot], a_start(lot, 0, yh)
        rs2_a[lot].wait()
        store(start, n, sa[lot][yh].astype(F32) + ra2[lot][...].astype(F32))
        cross = pass_on(start, n, y_peer)
        return cross, pass_on(start, n, to_right), pass_on(start, n, to_left)

    b_near = [finish_b(0)]
    a_near = [finish_a(0), finish_a(1)]
    b_near.append(finish_b(1))

    for cp in em2:
        cp.wait()
    f2[...] = (
        f1[:, zl].astype(F32) + r2[0].astype(F32) + r2[1].astype(F32) + r2[2].astype(F32)
    ).astype(BF)
    em3 = []
    for i, k in enumerate((8, 4, 12)):
        to = pl.ds(pl.multiple_of(((zh + k // 4) % 4) * 16, 16), 16)
        for yy in range(2):
            at = 7 + i * 2 + yy
            em3.append(send(f2.at[yy, to], r3.at[i, yy], em_s.at[at], em_r.at[at], at_z(k)))

    a_cut, b_cut = (48, 32), (32, 16)

    def hand_on_b(lot):
        n, cut = NB[lot], b_cut[lot]
        b_near[lot][0].wait()
        left = b_rows(lot, yh, 3)
        far_r = far_l = None
        if lot not in direct_b:
            far_r = pass_on(left, cut, to_right)
        rest.append(pass_on(left, n, y_peer))
        b_near[lot][1].wait()
        right = b_rows(lot, yh, 1)
        if lot not in direct_b:
            far_l = pass_on(right + cut, n - cut, to_left)
        rest.append(pass_on(right, n, y_peer))
        return far_r, far_l

    def cross_b(lot):
        n, cut, start = NB[lot], b_cut[lot], b_rows(lot, yh, 2)
        if lot in direct_b:
            b_near[lot][2].wait()
            rest.append(pass_on(start, n, y_peer))
            return
        b_far[lot][0].wait()
        rest.append(pass_on(start, cut, y_peer))
        b_far[lot][1].wait()
        rest.append(pass_on(start + cut, n - cut, y_peer))

    def spread_a(lot):
        n, cut, start = NA[lot], a_cut[lot], a_start(lot, 0, 1 - yh)
        a_near[lot][0].wait()
        if lot in direct_a:
            for k in (2, 1, 3):
                rest.append(pass_on(start, n, at_x(k)))
            return None
        pair = (pass_on(start, cut, to_right), pass_on(start + cut, n - cut, to_left))
        rest.append(pass_on(start + cut, n - cut, to_right))
        rest.append(pass_on(start, cut, to_left))
        return pair

    def hand_on_a(lot, half, pair):
        if pair is None:
            return
        n, cut = NA[lot], a_cut[lot]
        pair[0].wait()
        rest.append(pass_on(a_start(lot, 3, half), cut, to_right))
        pair[1].wait()
        rest.append(pass_on(a_start(lot, 1, half) + cut, n - cut, to_left))

    b_far = [hand_on_b(0)]
    c_near = [spread_a(0)]
    hand_on_a(0, yh, a_near[0][1:])
    c_near.append(spread_a(1))
    b_far.append(hand_on_b(1))
    hand_on_a(1, yh, a_near[1][1:])
    cross_b(0)
    hand_on_a(0, 1 - yh, c_near[0])
    cross_b(1)
    hand_on_a(1, 1 - yh, c_near[1])

    for cp in em3:
        cp.wait()
    own3 = pl.ds(pl.multiple_of(zh * 16, 16), 16)
    f3[...] = (
        f2[:, own3].astype(F32) + r3[0].astype(F32) + r3[1].astype(F32) + r3[2].astype(F32)
    ).astype(BF)
    em4 = send(f3.at[1 - y], r4, em_s.at[13], em_r.at[13], ylo_peer)
    em4.wait()
    emb_dir = f3[y].astype(F32) + r4[...].astype(F32)
    emb_inv, emb_unit = unit_rows(emb_ref[...])
    emb_out[...] = finish_rows(emb_dir, emb_unit, emb_inv)

    for cp in rest:
        cp.wait()


def write_out(emb_grad, proto_grad, emb_out, proto_out, sems):
    copies = [pltpu.make_async_copy(emb_grad, emb_out, sems.at[8])]
    for i in range(8):
        rows = pl.ds(i * (C // 8), C // 8)
        copies.append(pltpu.make_async_copy(proto_grad.at[rows], proto_out.at[rows], sems.at[i]))
    for cp in copies:
        cp.start()
    for cp in copies:
        cp.wait()


def on_device(embeddings, labels, row_weight, prototypes):
    vmem = pl.BlockSpec(memory_space=pltpu.VMEM)
    anywhere = pl.BlockSpec(memory_space=pl.ANY)
    dma = pltpu.SemaphoreType.DMA
    grads = pl.pallas_call(
        kernel,
        out_shape=(
            pltpu.VMEM((16, D), BF),
            pltpu.VMEM((C, D), BF),
        ),
        in_specs=[anywhere] * 4,
        out_specs=(vmem, vmem),
        scratch_shapes=[
            pltpu.VMEM((16, D), BF),
            pltpu.VMEM((8, 128), jnp.int32),
            pltpu.VMEM((8, 128), F32),
            pltpu.VMEM((C, D), BF),
            pltpu.VMEM((C, D), BF),
            pltpu.VMEM((2, 2, 4, 64, D), BF),
            pltpu.VMEM((4, C, Q), F32),
            pltpu.VMEM((C, R), BF),
            pltpu.VMEM((C, D), BF),
            pltpu.VMEM((1, R), jnp.int32),
            pltpu.VMEM((7, 1, R), F32),
            pltpu.VMEM((3, 1, R), F32),
            pltpu.VMEM((15, 1, R), F32),
            *[pltpu.VMEM((2, n, D), BF) for n in NA],
            *[pltpu.VMEM((2, n, D), BF) for n in NA],
            *[pltpu.VMEM((2, 2, n, D), BF) for n in NA],
            *[pltpu.VMEM((n, D), BF) for n in NA],
            *[pltpu.VMEM((2, n, D), BF) for n in NA],
            *[pltpu.VMEM((4 * n, D), BF) for n in NB],
            *[pltpu.VMEM((4, n, D), BF) for n in NB],
            *[pltpu.VMEM((3, n, D), BF) for n in NB],
            pltpu.VMEM((2, 2, Q, D), BF),
            pltpu.VMEM((2, Q, D), BF),
            pltpu.VMEM((2, 4, 64, D), BF),
            pltpu.VMEM((3, 2, 64, D), BF),
            pltpu.VMEM((2, 64, D), BF),
            pltpu.VMEM((3, 2, 16, D), BF),
            pltpu.VMEM((2, 16, D), BF),
            pltpu.VMEM((16, D), BF),
            dma((4,)),
            dma((18,)), dma((18,)),
            dma((3,)), dma((3,)),
            dma((15,)), dma((15,)),
            dma((64,)), dma((64,)),
            dma((14,)), dma((14,)),
        ],
        compiler_params=pltpu.CompilerParams(
            collective_id=0, has_side_effects=True, vmem_limit_bytes=56 * 2**20
        ),
        name="margin_softmax_backward",
    )(embeddings, labels.reshape(8, 128), row_weight.reshape(8, 128), prototypes)
    return pl.pallas_call(
        write_out,
        out_shape=(
            jax.ShapeDtypeStruct((16, D), BF),
            jax.ShapeDtypeStruct((C, D), BF),
        ),
        in_specs=[vmem, vmem],
        out_specs=(anywhere, anywhere),
        scratch_shapes=[dma((9,))],
        name="write_out",
    )(*[pltpu.with_memory_space_constraint(grad, pltpu.VMEM) for grad in grads])


def solution(mesh):
    return jax.shard_map(
        on_device,
        mesh=mesh,
        in_specs=(P(("dp", "cls"), None), P("dp"), P("dp"), P("cls", None)),
        out_specs=(P(("dp", "cls"), None), P("cls", None)),
        check_vma=False,
    )
```

```python
import math

import jax
import jax.numpy as jnp
from jax import lax
from jax.experimental import pallas as pl
from jax.experimental.pallas import tpu as pltpu
from jax.sharding import PartitionSpec as P

scale_factor = 64.0
margin = 0.5
sine_floor = 0.04
norm_eps = 1e-06
log2e = 1.4426950408889634
MESH = pl.DeviceIdType.MESH
F32 = jnp.float32
BF = jnp.bfloat16

D = 512
C = 2048
R = 1024
Q = 256
NA = (96, 48)
NB = (64, 48)
FIRST_A = (0, 8 * NA[0])
FIRST_B = (8 * sum(NA), 8 * (sum(NA) + NB[0]))
CH = 256


def unit_rows(values):
    wide = values.astype(F32)
    inverse = lax.rsqrt(jnp.sum(wide * wide, axis=1, keepdims=True) + norm_eps)
    return (inverse, wide * inverse)


def finish_rows(direction, unit_part, inverse):
    return (
        inverse * (direction - unit_part * jnp.sum(unit_part * direction, axis=1, keepdims=True))
    ).astype(BF)


def order_rows(labels, weights, lab_ref, tot):
    pieces = [(labels >> 12), (labels >> 6) & 63, labels & 63]
    pieces = [piece.astype(F32) for piece in pieces]
    rest = weights
    for _ in range(3):
        top = rest.astype(BF).astype(F32)
        pieces.append(top)
        rest = rest - top
    stacked = jnp.concatenate(pieces, axis=0).astype(BF)
    lane = lax.broadcasted_iota(jnp.int32, (128, 512), 0)
    to = lax.broadcasted_iota(jnp.int32, (128, 512), 1)
    from_lane = ((to >> 6) & 1) * 64 + ((to >> 7) & 1) * 32 + (to >> 8) * 16 + (to & 15)
    move = jnp.where(lane == from_lane, 1.0, 0.0).astype(BF)
    moved = jnp.dot(stacked, move, preferred_element_type=F32)
    row = lax.broadcasted_iota(jnp.int32, (8, 128), 0)
    z_high = (lax.broadcasted_iota(jnp.int32, (8, 128), 1) >> 4) & 3
    for tile in range(8):
        keep = row == z_high * 2 + tile % 2
        cut = moved[:, tile // 2 * 128 : (tile // 2 + 1) * 128]
        got = [
            jnp.sum(jnp.where(keep, cut[8 * i : 8 * i + 8], 0.0), axis=0, keepdims=True)
            for i in range(6)
        ]
        lanes = slice(tile * 128, (tile + 1) * 128)
        lab_ref[:, lanes] = (got[0] * 4096.0 + got[1] * 64.0 + got[2]).astype(jnp.int32)
        tot[6, :, lanes] = got[3] + got[4] + got[5]


def kernel(
    emb_hbm, lab_hbm, wgt_hbm, proto_hbm,
    emb_out, out,
    emb_ref, lab_in, wgt_in, proto, unit, u, e, g, part,
    lab_ref, tot, tot_far, tot_near,
    fw0, fw1, both0, both1, ra0, ra1, rc0, rc1, sa0, sa1, rb0, rb1, sb0, sb1, rx0, rx1,
    ed, r1, f1, r2, f2, r3, f3, r4,
    in_sems,
    ag_s, ag_r, tf_s, tf_r, tn_s, tn_r, rs_s, rs_r, em_s, em_r,
):
    fw, both, ra, ra2, sa = (fw0, fw1), (both0, both1), (ra0, ra1), (rc0, rc1), (sa0, sa1)
    rb, sb, rx = (rb0, rb1), (sb0, sb1), (rx0, rx1)
    dp = lax.axis_index("dp")
    cls = lax.axis_index("cls")
    yh, x = dp // 4, dp % 4
    z, y, c = cls // 4, (cls // 2) % 2, cls % 2
    zh, zl = z // 4, z % 4

    def at_z(k):
        return (dp, ((z + k) % 16) * 4 + y * 2 + c)

    def near(k, dy, dc):
        yy = (y + dy) % 2
        cc = (c + dc) % 2
        return (dp, ((z + k) % 16) * 4 + yy * 2 + cc)

    def at_x(k):
        return (yh * 4 + (x + k) % 4, cls)

    y_peer = ((1 - yh) * 4 + x, cls)
    core_peer = near(0, 0, 1)
    ylo_peer = near(0, 1, 0)
    places = [(k, dy, dc) for k in (2, 1, 15, 0) for dy, dc in ((1, 1), (1, 0), (0, 1), (0, 0))][:-1]

    def send(src, dst, ssem, rsem, where):
        cp = pltpu.make_async_remote_copy(
            src_ref=src, dst_ref=dst, send_sem=ssem, recv_sem=rsem,
            device_id=where, device_id_type=MESH,
        )
        cp.start()
        return cp

    barrier = pltpu.get_barrier_semaphore()
    friends = [at_z(k) for k in (8, 4, 12)] + [near(*place) for place in places]
    friends += [at_x(1), at_x(2), at_x(3), y_peer]
    for friend in friends:
        pl.semaphore_signal(barrier, inc=1, device_id=friend, device_id_type=MESH)
    sources = ((emb_hbm, emb_ref), (lab_hbm, lab_in), (wgt_hbm, wgt_in), (proto_hbm, proto))
    loads = [pltpu.make_async_copy(src, dst, in_sems.at[i]) for i, (src, dst) in enumerate(sources)]
    for load in loads:
        load.start()
    loads[0].wait()
    emb_inv, emb_unit = unit_rows(emb_ref[...])
    u[c, y, zl, pl.ds(pl.multiple_of(zh * 16, 16), 16), :] = emb_unit.astype(BF)
    pl.semaphore_wait(barrier, len(friends))

    sends = []
    own_block = u.at[c, y, zl, pl.ds(pl.multiple_of(zh * 16, 16), 16)]
    p1 = [send(own_block, own_block, ag_s.at[i], ag_r.at[i], at_z(k)) for i, k in enumerate((8, 4, 12))]

    for load in loads[1:]:
        load.wait()

    def normalize(i, carry):
        rows = pl.ds(pl.multiple_of(i * CH, CH), CH)
        unit[rows, :] = unit_rows(proto[rows, :])[1].astype(BF)
        return carry

    lax.fori_loop(0, C // CH // 2, normalize, 0)
    for cp in p1:
        cp.wait()
    own_set = u.at[c, y, zl]
    p2 = [send(own_set, own_set, ag_s.at[3 + i], ag_r.at[3 + i], at_z(k)) for i, k in enumerate((1, 15, 2))]
    lax.fori_loop(C // CH // 2, C // CH, normalize, 0)
    order_rows(lab_in[...], wgt_in[...], lab_ref, tot)
    toy = [send(own_set, own_set, ag_s.at[6], ag_r.at[6], ylo_peer)]
    toc = [send(own_set, own_set, ag_s.at[10], ag_r.at[10], core_peer)]
    for i, k in enumerate((1, 15, 2)):
        p2[i].wait()
        got = u.at[c, y, (zl + 16 - k) % 4]
        toy.append(send(got, got, ag_s.at[7 + i], ag_r.at[7 + i], ylo_peer))
        toc.append(send(got, got, ag_s.at[11 + i], ag_r.at[11 + i], core_peer))

    class_iota = lax.broadcasted_iota(jnp.int32, (C, Q), 0)
    first_class = cls * C

    def first_pass(cc, yy):
        q = cc * 2 + yy
        lanes = pl.ds(pl.multiple_of(q * Q, Q), Q)
        labels = lab_ref[:, lanes] - first_class
        rows_u = u[cc, yy].reshape(Q, D)

        cosine = lax.dot_general(
            unit[...], rows_u, (((1,), (1,)), ((), ())), preferred_element_type=F32
        )
        is_target = class_iota == labels
        ex = jnp.where(is_target, 0.0, jnp.exp2(cosine * (scale_factor * log2e)))
        e[q] = ex
        total = jnp.sum(ex, axis=0, keepdims=True)
        target_cos = jnp.sum(jnp.where(is_target, cosine, 0.0), axis=0, keepdims=True)
        here = (labels >= 0) & (labels < C)
        sine = jnp.sqrt(jnp.maximum(1.0 - target_cos * target_cos, sine_floor))
        target_logit = scale_factor * (target_cos * math.cos(margin) - sine * math.sin(margin))
        target_exp = jnp.exp(target_logit)
        tot[0, :, lanes] = total + jnp.where(here, target_exp, 0.0)
        bound_free = 1.0 - target_cos * target_cos > sine_floor
        slope = scale_factor * (
            math.cos(margin) + jnp.where(bound_free, math.sin(margin) * target_cos / sine, 0.0)
        )
        tot[1, :, lanes] = target_exp
        tot[2, :, lanes] = slope

    first_pass(c, y)
    for cp in toc:
        cp.wait()
    first_pass(1 - c, y)
    tod = []
    for i, k in enumerate((0, 1, 15, 2)):
        toy[i].wait()
        got = u.at[c, 1 - y, (zl + 16 - k) % 4]
        tod.append(send(got, got, ag_s.at[14 + i], ag_r.at[14 + i], core_peer))
    first_pass(c, 1 - y)
    for cp in tod:
        cp.wait()
    first_pass(1 - c, 1 - y)

    apart = []
    for i, k in enumerate((8, 4, 12)):
        apart.append(send(tot.at[0], tot_far.at[i], tf_s.at[i], tf_r.at[i], at_z(k)))
    for cp in apart:
        cp.wait()
    tot[3] = tot[0] + tot_far[0] + tot_far[1] + tot_far[2]
    around = []
    for i, place in enumerate(places):
        around.append(send(tot.at[3], tot_near.at[i], tn_s.at[i], tn_r.at[i], near(*place)))
    for cp in around:
        cp.wait()
    totals = tot[3]
    for i in range(15):
        totals = totals + tot_near[i]

    weight = tot[6]
    row_scale = scale_factor * weight / totals
    label_grad = weight * (tot[1] / totals - 1.0) * tot[2]
    tot[4] = row_scale
    tot[5] = label_grad

    def second_pass(base, n):
        base = pl.multiple_of(base, 16)
        rows = pl.ds(base, n)
        for q in range(4):
            lanes = slice(q * Q, (q + 1) * Q)
            is_target = class_iota[:n] == lab_ref[:, lanes] - (first_class + base)
            grad = jnp.where(is_target, tot[5, :, lanes], e[q, rows, :] * tot[4, :, lanes])
            g[rows, lanes] = grad.astype(BF)
        part[rows, :] = jnp.dot(
            g[rows, :], u[...].reshape(R, D), preferred_element_type=F32
        ).astype(BF)

    def rows_of(ref, start, n):
        return ref.at[pl.ds(pl.multiple_of(start, 16), n)]

    def value(ref, start, n):
        return ref[pl.ds(pl.multiple_of(start, 16), n), :].astype(F32)

    def a_rows(lot, k):
        return FIRST_A[lot] + ((x + k) % 4) * (2 * NA[lot])

    def b_rows(lot, half, k=None):
        first = FIRST_B[lot] + half * (4 * NB[lot])
        return first if k is None else first + ((x + k) % 4) * NB[lot]

    to_left, to_right = at_x(3), at_x(1)

    serial = [0]

    def ship(src, dst, where):
        at = serial[0]
        serial[0] += 1
        return send(src, dst, rs_s.at[at], rs_r.at[at], where)

    far, rs_a, rs_b = [], ([], []), []

    def send_far(lot):
        n, base = NA[lot], a_rows(lot, 2)
        second_pass(base, 2 * n)
        to_r = ship(rows_of(part, base, n), fw[lot].at[0], to_right)
        far.append((to_r, ship(rows_of(part, base + n, n), fw[lot].at[1], to_left)))

    def send_plain(lot):
        n, base = NA[lot], a_rows(lot, 1)
        second_pass(base, 2 * n)
        rs_a[lot].append(ship(rows_of(part, base + n, n), ra[lot].at[0, 1], to_right))
        base = a_rows(lot, 3)
        second_pass(base, 2 * n)
        rs_a[lot].append(ship(rows_of(part, base, n), ra[lot].at[1, 0], to_left))

    def send_joined(lot):
        n = NA[lot]
        for side, start, to in ((0, a_rows(lot, 1), to_right), (1, a_rows(lot, 3) + n, to_left)):
            far[lot][side].wait()
            both[lot][side] = (value(part, start, n) + fw[lot][side].astype(F32)).astype(BF)
            rs_a[lot].append(ship(both[lot].at[side], ra[lot].at[side, side], to))

    def send_b(lot):
        n, base = 4 * NB[lot], b_rows(lot, 1 - yh)
        second_pass(base, n)
        rs_b.append(ship(rows_of(part, base, n), rb[lot], y_peer))

    send_far(0)
    send_far(1)
    send_b(0)
    send_plain(0)
    send_plain(1)
    send_b(1)
    for lot in range(2):
        second_pass(a_rows(lot, 0), 2 * NA[lot])
        second_pass(b_rows(lot, yh), 4 * NB[lot])

    def emb_product(cc, yy):
        q = cc * 2 + yy
        lanes = pl.ds(pl.multiple_of(q * Q, Q), Q)
        ed[cc, yy] = lax.dot_general(
            g[:, lanes], unit[...], (((0,), (0,)), ((), ())), preferred_element_type=F32
        ).astype(BF)

    emb_product(1 - c, 0)
    emb_product(1 - c, 1)
    em1 = send(ed.at[1 - c], r1, em_s.at[0], em_r.at[0], core_peer)

    send_joined(0)
    send_joined(1)
    emb_product(c, 0)
    emb_product(c, 1)

    def own_b(lot):
        n = NB[lot]
        rs_b[lot].wait()
        sum_b = value(part, b_rows(lot, yh), 4 * n) + rb[lot][...].astype(F32)
        sb[lot][...] = sum_b.astype(BF).reshape(4, n, D)
        sent = []
        for k in (2, 1, 3):
            sent.append(ship(sb[lot].at[(x + k) % 4], rx[lot].at[k - 1], at_x(k)))
        return sent

    def own_a(lot):
        n = NA[lot]
        for cp in rs_a[lot]:
            cp.wait()
        sum_a = value(part, a_rows(lot, 0), 2 * n)
        for side in range(2):
            sum_a = sum_a + ra[lot][side].reshape(2 * n, D).astype(F32)
        sa[lot][...] = sum_a.astype(BF).reshape(2, n, D)
        return ship(sa[lot].at[1 - yh], ra2[lot], y_peer)

    rs2_b = [own_b(0)]
    em1.wait()
    f1[...] = (ed[c].astype(F32) + r1[...].astype(F32)).astype(BF).reshape(2, 4, 64, D)
    em2 = []
    for i, k in enumerate((2, 1, 15)):
        for yy in range(2):
            at = 1 + i * 2 + yy
            em2.append(send(f1.at[yy, (zl + k) % 4], r2.at[i, yy], em_s.at[at], em_r.at[at], at_z(k)))
    rs2_a = [own_a(0), own_a(1)]
    rs2_b.append(own_b(1))

    rest = []
    direct_a, direct_b = (1,), (1,)

    def pass_on(start, n, where):
        rows = rows_of(out, start, n)
        return ship(rows, rows, where)

    def a_start(lot, k, half):
        return a_rows(lot, k) + half * NA[lot]

    def store(start, n, direction):
        inverse, unit_part = unit_rows(value(proto, start, n))
        out[pl.ds(pl.multiple_of(start, 16), n), :] = finish_rows(direction, unit_part, inverse)

    def finish_b(lot):
        for cp in rs2_b[lot]:
            cp.wait()
        direction = value(sb[lot].at[x], 0, NB[lot])
        for k in range(3):
            direction = direction + rx[lot][k].astype(F32)
        start = b_rows(lot, yh, 0)
        store(start, NB[lot], direction)
        near_b = [pass_on(start, NB[lot], to_right), pass_on(start, NB[lot], to_left)]
        if lot in direct_b:
            near_b.append(pass_on(start, NB[lot], at_x(2)))
        rest.append(pass_on(start, NB[lot], y_peer))
        return near_b

    def finish_a(lot):
        n, start = NA[lot], a_start(lot, 0, yh)
        rs2_a[lot].wait()
        store(start, n, sa[lot][yh].astype(F32) + ra2[lot][...].astype(F32))
        cross = pass_on(start, n, y_peer)
        return cross, pass_on(start, n, to_right), pass_on(start, n, to_left)

    b_near = [finish_b(0)]
    a_near = [finish_a(0), finish_a(1)]
    b_near.append(finish_b(1))

    for cp in em2:
        cp.wait()
    f2[...] = (
        f1[:, zl].astype(F32) + r2[0].astype(F32) + r2[1].astype(F32) + r2[2].astype(F32)
    ).astype(BF)
    em3 = []
    for i, k in enumerate((8, 4, 12)):
        to = pl.ds(pl.multiple_of(((zh + k // 4) % 4) * 16, 16), 16)
        for yy in range(2):
            at = 7 + i * 2 + yy
            em3.append(send(f2.at[yy, to], r3.at[i, yy], em_s.at[at], em_r.at[at], at_z(k)))

    a_cut, b_cut = (48, 16), (32, 16)

    def hand_on_b(lot):
        n, cut = NB[lot], b_cut[lot]
        b_near[lot][0].wait()
        left = b_rows(lot, yh, 3)
        far_r = far_l = None
        if lot not in direct_b:
            far_r = pass_on(left, cut, to_right)
        rest.append(pass_on(left, n, y_peer))
        b_near[lot][1].wait()
        right = b_rows(lot, yh, 1)
        if lot not in direct_b:
            far_l = pass_on(right + cut, n - cut, to_left)
        rest.append(pass_on(right, n, y_peer))
        return far_r, far_l

    def cross_b(lot):
        n, cut, start = NB[lot], b_cut[lot], b_rows(lot, yh, 2)
        if lot in direct_b:
            b_near[lot][2].wait()
            rest.append(pass_on(start, n, y_peer))
            return
        b_far[lot][0].wait()
        rest.append(pass_on(start, cut, y_peer))
        b_far[lot][1].wait()
        rest.append(pass_on(start + cut, n - cut, y_peer))

    def spread_a(lot):
        n, cut, start = NA[lot], a_cut[lot], a_start(lot, 0, 1 - yh)
        a_near[lot][0].wait()
        if lot in direct_a:
            for k in (2, 1, 3):
                rest.append(pass_on(start, n, at_x(k)))
            return None
        pair = (pass_on(start, cut, to_right), pass_on(start + cut, n - cut, to_left))
        rest.append(pass_on(start + cut, n - cut, to_right))
        rest.append(pass_on(start, cut, to_left))
        return pair

    def hand_on_a(lot, half, pair):
        if pair is None:
            return
        n, cut = NA[lot], a_cut[lot]
        pair[0].wait()
        rest.append(pass_on(a_start(lot, 3, half), cut, to_right))
        pair[1].wait()
        rest.append(pass_on(a_start(lot, 1, half) + cut, n - cut, to_left))

    b_far = [hand_on_b(0)]
    c_near = [spread_a(0)]
    hand_on_a(0, yh, a_near[0][1:])
    c_near.append(spread_a(1))
    b_far.append(hand_on_b(1))
    hand_on_a(1, yh, a_near[1][1:])
    cross_b(0)
    hand_on_a(0, 1 - yh, c_near[0])
    cross_b(1)
    hand_on_a(1, 1 - yh, c_near[1])

    for cp in em3:
        cp.wait()
    own3 = pl.ds(pl.multiple_of(zh * 16, 16), 16)
    f3[...] = (
        f2[:, own3].astype(F32) + r3[0].astype(F32) + r3[1].astype(F32) + r3[2].astype(F32)
    ).astype(BF)
    em4 = send(f3.at[1 - y], r4, em_s.at[13], em_r.at[13], ylo_peer)
    em4.wait()
    emb_dir = f3[y].astype(F32) + r4[...].astype(F32)
    emb_inv, emb_unit = unit_rows(emb_ref[...])
    emb_out[...] = finish_rows(emb_dir, emb_unit, emb_inv)

    for cp in rest:
        cp.wait()


def write_out(emb_grad, proto_grad, emb_out, proto_out, sems):
    copies = [pltpu.make_async_copy(emb_grad, emb_out, sems.at[8])]
    for i in range(8):
        rows = pl.ds(i * (C // 8), C // 8)
        copies.append(pltpu.make_async_copy(proto_grad.at[rows], proto_out.at[rows], sems.at[i]))
    for cp in copies:
        cp.start()
    for cp in copies:
        cp.wait()


def on_device(embeddings, labels, row_weight, prototypes):
    vmem = pl.BlockSpec(memory_space=pltpu.VMEM)
    anywhere = pl.BlockSpec(memory_space=pl.ANY)
    dma = pltpu.SemaphoreType.DMA
    grads = pl.pallas_call(
        kernel,
        out_shape=(
            pltpu.VMEM((16, D), BF),
            pltpu.VMEM((C, D), BF),
        ),
        in_specs=[anywhere] * 4,
        out_specs=(vmem, vmem),
        scratch_shapes=[
            pltpu.VMEM((16, D), BF),
            pltpu.VMEM((8, 128), jnp.int32),
            pltpu.VMEM((8, 128), F32),
            pltpu.VMEM((C, D), BF),
            pltpu.VMEM((C, D), BF),
            pltpu.VMEM((2, 2, 4, 64, D), BF),
            pltpu.VMEM((4, C, Q), F32),
            pltpu.VMEM((C, R), BF),
            pltpu.VMEM((C, D), BF),
            pltpu.VMEM((1, R), jnp.int32),
            pltpu.VMEM((7, 1, R), F32),
            pltpu.VMEM((3, 1, R), F32),
            pltpu.VMEM((15, 1, R), F32),
            *[pltpu.VMEM((2, n, D), BF) for n in NA],
            *[pltpu.VMEM((2, n, D), BF) for n in NA],
            *[pltpu.VMEM((2, 2, n, D), BF) for n in NA],
            *[pltpu.VMEM((n, D), BF) for n in NA],
            *[pltpu.VMEM((2, n, D), BF) for n in NA],
            *[pltpu.VMEM((4 * n, D), BF) for n in NB],
            *[pltpu.VMEM((4, n, D), BF) for n in NB],
            *[pltpu.VMEM((3, n, D), BF) for n in NB],
            pltpu.VMEM((2, 2, Q, D), BF),
            pltpu.VMEM((2, Q, D), BF),
            pltpu.VMEM((2, 4, 64, D), BF),
            pltpu.VMEM((3, 2, 64, D), BF),
            pltpu.VMEM((2, 64, D), BF),
            pltpu.VMEM((3, 2, 16, D), BF),
            pltpu.VMEM((2, 16, D), BF),
            pltpu.VMEM((16, D), BF),
            dma((4,)),
            dma((18,)), dma((18,)),
            dma((3,)), dma((3,)),
            dma((15,)), dma((15,)),
            dma((64,)), dma((64,)),
            dma((14,)), dma((14,)),
        ],
        compiler_params=pltpu.CompilerParams(
            collective_id=0, has_side_effects=True, vmem_limit_bytes=56 * 2**20
        ),
        name="margin_softmax_backward",
    )(embeddings, labels.reshape(8, 128), row_weight.reshape(8, 128), prototypes)
    return pl.pallas_call(
        write_out,
        out_shape=(
            jax.ShapeDtypeStruct((16, D), BF),
            jax.ShapeDtypeStruct((C, D), BF),
        ),
        in_specs=[vmem, vmem],
        out_specs=(anywhere, anywhere),
        scratch_shapes=[dma((9,))],
        name="write_out",
    )(*[pltpu.with_memory_space_constraint(grad, pltpu.VMEM) for grad in grads])


def solution(mesh):
    return jax.shard_map(
        on_device,
        mesh=mesh,
        in_specs=(P(("dp", "cls"), None), P("dp"), P("dp"), P("cls", None)),
        out_specs=(P(("dp", "cls"), None), P("cls", None)),
        check_vma=False,
    )
```
